32 devices in a mesh: seg: 16 (over z, y, core), item: 2 (over x).
Axes of the slice: x: 2, y: 2, z: 4, core: 2. Of those that a mesh axis runs over, the one named last changes fastest.
Arguments:
- hidden: bfloat16 [4, 2, 16, 522, 256], P(None, 'item', 'seg'), may hold values from -6 to 6
- write_cotangent: bfloat16 [4, 2, 16, 10, 256], P(None, 'item', 'seg'), may hold values from -6 to 6
- targets: bfloat16 [4, 2, 16, 80, 256], P(None, 'item', 'seg'), may hold values from -6 to 6
- positions: int32 [4, 2, 16, 80], P(None, 'item', 'seg'), may hold values from 0 to 501, as said below
- counts: int32 [4, 2, 16], P(None, 'item', 'seg'), may hold values from 40 to 80, as said below
- w_query: bfloat16 [2, 256, 256], replicated, may hold values from -0.375 to 0.375
- b_query: float32 [2, 256], replicated, may hold values from -3 to 3
- w_key: bfloat16 [2, 256, 256], replicated, may hold values from -0.375 to 0.375
- w_value: bfloat16 [2, 256, 256], replicated, may hold values from -0.375 to 0.375
- b_value: float32 [2, 256], replicated, may hold values from -3 to 3
- w_out: bfloat16 [2, 256, 256], replicated, may hold values from -6 to 6
- b_out: float32 [2, 256], replicated, may hold values from -3 to 3
- gain_attn: float32 [2, 256], replicated, may hold values from 0.5 to 1.5
- shift_attn: float32 [2, 256], replicated, may hold values from -2 to 2
- w_up: bfloat16 [2, 256, 1024], replicated, may hold values from -0.375 to 0.375
- b_up: float32 [2, 1024], replicated, may hold values from -3 to 3
- w_down: bfloat16 [2, 1024, 256], replicated, may hold values from -0.1875 to 0.1875
- b_down: float32 [2, 256], replicated, may hold values from -3 to 3
- gain_ffn: float32 [2, 256], replicated, may hold values from 0.5 to 1.5
- shift_ffn: float32 [2, 256], replicated, may hold values from -2 to 2
Outputs:
- output: bfloat16 [4, 2, 16, 522, 256], P(None, 'item', 'seg')
- hidden_grad: bfloat16 [4, 2, 16, 522, 256], P(None, 'item', 'seg')
- grad_w_query: float32 [2, 256, 256], replicated
- grad_b_query: float32 [2, 256], replicated
- grad_w_key: float32 [2, 256, 256], replicated
- grad_w_value: float32 [2, 256, 256], replicated
- grad_b_value: float32 [2, 256], replicated
- grad_w_out: float32 [2, 256, 256], replicated
- grad_b_out: float32 [2, 256], replicated
- grad_gain_attn: float32 [2, 256], replicated
- grad_shift_attn: float32 [2, 256], replicated
- grad_w_up: float32 [2, 256, 1024], replicated
- grad_b_up: float32 [2, 1024], replicated
- grad_w_down: float32 [2, 1024, 256], replicated
- grad_b_down: float32 [2, 256], replicated
- grad_gain_ffn: float32 [2, 256], replicated
- grad_shift_ffn: float32 [2, 256], replicated
The draws below stay inside these ranges and needn't reach their ends.
Inputs may be any that keep to these rules, and one draw needn't show every extreme that they name: Within one segment the 80 positions are distinct; slots at or after the segment's count are unused. `counts`: some segment uses all 80 slots.
All inputs are finite; a program needn't handle non-finite values.
Results may differ from the reference program's by a relative error of at most 0.018.
The reference program's roundings to bfloat16 on the way count: a program that leaves them out, or rounds other values in their place, can miss the bound.
Values may be sent and summed in bfloat16 or wider, within the bound.
No kernel may reach another device: no remote copies, remote signals or barrier semaphores. Data moves between devices by JAX's collectives and lax.ppermute only.
A program may use at most 128 MiB of HBM per device.

```python
import jax
import jax.numpy as jnp
from jax import lax

D = 256
HEADS = 4
FF = 1024
LAYERS = 2
MEM = 10
SEG = 502
ROWS = 522
MASKS = 80
MICRO = 4
ITEMS = 2
SEGS = 16


def draw_positions(key, part):
    key = jax.random.fold_in(key, 11)
    grid_shape = (MICRO, ITEMS, SEGS, SEG)
    scores = jax.random.randint(key, grid_shape, 0, 1 << 20) * SEG + jnp.arange(SEG, dtype=jnp.int32)
    ranking = jnp.argsort(scores, axis=-1, stable=True)
    return ranking[..., :MASKS].astype(jnp.int32)


def draw_counts(key, part):
    key = jax.random.fold_in(key, 12)
    first_key, second_key = jax.random.split(key)
    sampled = jax.random.randint(first_key, (MICRO, ITEMS, SEGS), MASKS // 2, MASKS + 1)
    chosen = jax.random.randint(second_key, (), 0, MICRO * ITEMS * SEGS)
    slot_index = jnp.arange(MICRO * ITEMS * SEGS).reshape(MICRO, ITEMS, SEGS)
    return jnp.where(slot_index == chosen, MASKS, sampled).astype(jnp.int32)


def shard_levels(key, dims, cuts, least, largest):
    loudness, own = 1.0, jax.random.fold_in(key, 6)
    for axis_at, parts in cuts:
        heights = jnp.exp(jax.random.uniform(jax.random.fold_in(own, axis_at), (parts,), jnp.float32, least / len(cuts), largest / len(cuts)))
        loudness = loudness * jnp.repeat(heights, dims[axis_at] // parts).reshape([-1 if axis == axis_at else 1 for axis in range(len(dims))])
    return loudness


def normal_values(key, dims, deviation, reach, shards=(), kind=jnp.bfloat16):
    gain = shard_levels(key, dims, shards, -0.22, 0.18) if shards else 1.0
    drawn = jax.random.normal(key, dims, jnp.float32) * deviation * gain
    return jnp.minimum(jnp.maximum(drawn, -reach), reach).astype(kind)


def setup_inputs(seed: int = 0) -> dict:
    streams_of = jax.random.split(jax.random.key(seed), 21)
    hidden = normal_values(streams_of[0], (MICRO, ITEMS, SEGS, ROWS, D), 1.0, 6.0, ((1, 2), (2, 16)))
    write_cotangent = normal_values(streams_of[1], (MICRO, ITEMS, SEGS, MEM, D), 1.0, 6.0, ((1, 2), (2, 16)))
    targets = normal_values(streams_of[2], (MICRO, ITEMS, SEGS, MASKS, D), 1.0, 6.0, ((1, 2), (2, 16)))
    positions = draw_positions(jax.random.fold_in(streams_of[20], 71), 0)
    counts = draw_counts(jax.random.fold_in(streams_of[20], 71), 0)
    w_query = normal_values(streams_of[5], (LAYERS, D, D), D ** -0.5, 0.375)
    b_query = normal_values(streams_of[6], (LAYERS, D), 0.5, 3.0, (), jnp.float32)
    w_key = normal_values(streams_of[7], (LAYERS, D, D), D ** -0.5, 0.375)
    w_value = normal_values(streams_of[8], (LAYERS, D, D), D ** -0.5, 0.375)
    b_value = normal_values(streams_of[9], (LAYERS, D), 0.5, 3.0, (), jnp.float32)
    w_out = normal_values(streams_of[10], (LAYERS, D, D), (max(1, 3 * D // ROWS)) ** -0.5, 6.0)
    b_out = normal_values(streams_of[11], (LAYERS, D), 0.5, 3.0, (), jnp.float32)
    gain_attn = jnp.clip(1.0 + 0.1 * jax.random.normal(streams_of[12], (LAYERS, D), jnp.float32), 0.5, 1.5)
    shift_attn = normal_values(streams_of[13], (LAYERS, D), 0.3, 2.0, (), jnp.float32)
    w_up = normal_values(streams_of[14], (LAYERS, D, FF), D ** -0.5, 0.375)
    b_up = normal_values(streams_of[15], (LAYERS, FF), 0.5, 3.0, (), jnp.float32)
    w_down = normal_values(streams_of[16], (LAYERS, FF, D), FF ** -0.5, 0.1875)
    b_down = normal_values(streams_of[17], (LAYERS, D), 0.5, 3.0, (), jnp.float32)
    gain_ffn = jnp.clip(1.0 + 0.1 * jax.random.normal(streams_of[18], (LAYERS, D), jnp.float32), 0.5, 1.5)
    shift_ffn = normal_values(streams_of[19], (LAYERS, D), 0.3, 2.0, (), jnp.float32)
    return dict(hidden=hidden, write_cotangent=write_cotangent, targets=targets, positions=positions, counts=counts, w_query=w_query, b_query=b_query, w_key=w_key, w_value=w_value, b_value=b_value, w_out=w_out, b_out=b_out, gain_attn=gain_attn, shift_attn=shift_attn, w_up=w_up, b_up=b_up, w_down=w_down, b_down=b_down, gain_ffn=gain_ffn, shift_ffn=shift_ffn)


@jax.custom_vjp
def low(v):
    return lax.optimization_barrier(v.astype(jnp.bfloat16)).astype(jnp.float32)

@jax.custom_vjp
def low_back(v):
    return v

def low_keep(v):
    return (low(v), None)

def low_pass(kept, grad):
    return (grad,)

def back_keep(v):
    return (v, None)

def back_low(kept, grad):
    return (low(grad),)
low.defvjp(low_keep, low_pass)
low_back.defvjp(back_keep, back_low)

def matmul_high(former, latter):
    return jnp.matmul(former, latter, precision=lax.Precision.HIGHEST)

def normalize(tensor):
    centred = tensor - lax.optimization_barrier(jnp.mean(tensor, axis=-1, keepdims=True))
    spread = lax.optimization_barrier(jnp.mean(centred * centred, axis=-1, keepdims=True))
    return centred * lax.rsqrt(spread + 1e-12)

def split_heads(tensor):
    return tensor.reshape(tensor.shape[0], tensor.shape[1], HEADS, tensor.shape[2] // HEADS)

def encoder_layer(inputs, params):
    w_query, b_query, w_key, w_value, b_value, w_out, b_out, gain_attn, shift_attn, w_up, b_up, w_down, b_down, gain_ffn, shift_ffn = params
    queries = low_back(low((matmul_high(inputs, w_query) + b_query) * 0.125))
    key_rows = low_back(low(matmul_high(inputs, w_key)))
    values = low_back(low(matmul_high(inputs, w_value) + b_value))
    scores = low_back(jnp.einsum('sqhd,skhd->shqk', split_heads(queries), split_heads(key_rows), precision=lax.Precision.HIGHEST))
    attention = low(jax.nn.softmax(scores, axis=-1))
    context = jnp.einsum('shqk,skhd->sqhd', attention, split_heads(values), precision=lax.Precision.HIGHEST).reshape(inputs.shape)
    context = low_back(low(context))
    attended = low_back(matmul_high(context, w_out) + b_out)
    middle = normalize(inputs + attended) * gain_attn + shift_attn
    upward = low_back(matmul_high(low(middle), w_up) + b_up)
    active = low(jax.nn.gelu(upward, approximate=False))
    branch = low_back(matmul_high(active, w_down) + b_down)
    return normalize(middle + branch) * gain_ffn + shift_ffn

def item_loss(lower_in, weights, cotangent, target, places, masked_count):
    lower = tuple((weight[0] for weight in weights))
    upper = tuple((weight[1] for weight in weights))
    lower_out = encoder_layer(lower_in, lower)
    moved = low_back(lower_out[:-1, ROWS - MEM:])
    read_rows = jnp.concatenate([lower_out[:1, :MEM], moved], axis=0)
    upper_in = low(jnp.concatenate([read_rows, lower_out[:, MEM:]], axis=1))
    upper_out = encoder_layer(upper_in, upper)
    token_rows = upper_out[:, MEM:MEM + SEG]
    picked = jnp.take_along_axis(token_rows, places[:, :, None], axis=1)
    alive_slots = (jnp.arange(MASKS)[None, :] < masked_count[:, None]).astype(jnp.float32)
    alive_slots = alive_slots / masked_count[:, None].astype(jnp.float32)
    mismatch = picked - target
    loss = 0.5 * jnp.sum(alive_slots[:, :, None] * mismatch * mismatch)
    loss = loss + jnp.sum(upper_out[:, ROWS - MEM:] * cotangent)
    return (loss, upper_out)

def reference(hidden, write_cotangent, targets, positions, counts, w_query, b_query, w_key, w_value, b_value, w_out, b_out, gain_attn, shift_attn, w_up, b_up, w_down, b_down, gain_ffn, shift_ffn):
    weights = tuple((weight.astype(jnp.float32) for weight in (w_query, b_query, w_key, w_value, b_value, w_out, b_out, gain_attn, shift_attn, w_up, b_up, w_down, b_down, gain_ffn, shift_ffn)))
    item_total = MICRO * ITEMS

    def flatten(tensor):
        return tensor.reshape((item_total,) + tensor.shape[2:])

    def item_step(totals, sliced):
        lower_in, cotangent, target, places, masked_count = sliced

        def loss_of(first_arg, second_arg):
            return item_loss(first_arg, second_arg, cotangent, target, places, masked_count)
        loss, pullback, upper_out = jax.vjp(loss_of, lower_in, weights, has_aux=True)
        grad_in, grad_weights = pullback(jnp.ones((), jnp.float32))
        totals = tuple((former + latter for former, latter in zip(totals, grad_weights)))
        return (totals, (upper_out.astype(jnp.bfloat16), grad_in.astype(jnp.bfloat16)))
    zero_set = tuple((jnp.zeros(weight.shape, jnp.float32) for weight in weights))
    totals, (outputs, input_grads) = lax.scan(item_step, zero_set, (flatten(hidden.astype(jnp.float32)), flatten(write_cotangent.astype(jnp.float32)), flatten(targets.astype(jnp.float32)), flatten(positions), flatten(counts)))
    output = outputs.reshape(hidden.shape)
    hidden_grad = input_grads.reshape(hidden.shape)
    return (output, hidden_grad, totals[0], totals[1], totals[2], totals[3], totals[4], totals[5], totals[6], totals[7], totals[8], totals[9], totals[10], totals[11], totals[12], totals[13], totals[14])
```

```python
import functools

import jax
import jax.numpy as jnp
from jax import lax
from jax.experimental import pallas as pl
from jax.experimental.pallas import tpu as pltpu
from jax.sharding import PartitionSpec as P

EPSILON = 1e-12
DENSITY = 0.3989422804014327
HEADS = 4
TILE = 16
LOW = -1e30
F32, BF16 = jnp.float32, jnp.bfloat16
WEIGHTS = (
    "w_query", "b_query", "w_key", "w_value", "b_value", "w_out", "b_out", "gain_attn",
    "shift_attn", "w_up", "b_up", "w_down", "b_down", "gain_ffn", "shift_ffn",
)
VECTORS = ("b_query", "b_value", "b_out", "gain_attn", "shift_attn", "b_down", "gain_ffn", "shift_ffn")
STASH = ("query", "key", "value", "prob", "prob_rest", "context_t", "context", "inverse", "normed_attn",
         "middle", "active", "slope", "normed_ffn")


def dot(a, b):
    return jnp.dot(a, b, preferred_element_type=F32)


def dot_nt(a, b):
    return lax.dot_general(a, b, (((1,), (1,)), ((), ())), preferred_element_type=F32)


def dot_tn(a, b):
    return lax.dot_general(a, b, (((0,), (0,)), ((), ())), preferred_element_type=F32)


def mean(v):
    return jnp.mean(v, axis=-1, keepdims=True)


def column_sum(v):
    return jnp.sum(v.astype(F32), axis=0, keepdims=True)


def normalize(v):
    centred = v - mean(v)
    inverse = lax.rsqrt(mean(centred * centred) + EPSILON)
    return centred * inverse, inverse


def norm_back(grad, normed, inverse):
    return inverse * (grad - mean(grad) - normed * mean(grad * normed))


def gelu_and_slope(u):
    bell = jnp.exp(u * u * -0.5)
    t = 1.0 / (1.0 + 0.23164188826 * jnp.abs(u))
    tail = t * (0.127414796 + t * (-0.142248368 + t * (0.7107068705 + t * (-0.7265760135 + t * 0.5307027145))))
    tail = tail * bell
    phi = jnp.where(u < 0.0, tail, 1.0 - tail)
    return u * phi, phi + u * bell * DENSITY


def spread_heads(rest, width):
    tiled = jnp.concatenate([rest] * HEADS, axis=0)
    return jnp.where(head_block(tiled.shape, width), tiled, jnp.zeros_like(tiled))


def head_block(shape, width):
    rows = lax.broadcasted_iota(jnp.int32, shape, 0) // TILE
    lanes = lax.broadcasted_iota(jnp.int32, shape, 1) // width
    return rows == lanes


def fold_heads(spread, width):
    own = jnp.where(head_block(spread.shape, width), spread, 0.0)
    return own[:TILE] + own[TILE : 2 * TILE] + own[2 * TILE : 3 * TILE] + own[3 * TILE :]


def own_half(pair, h, width):
    lanes = lax.broadcasted_iota(jnp.int32, pair.shape, 1) // width
    return jnp.where(lanes == h % 2, pair, jnp.zeros_like(pair))


def layer_forward(x, layer, w, st, rows):
    full, features = x.shape
    main = full - TILE
    width = features // HEADS
    row = lambda name: w[name][layer : layer + 1, :]
    q = ((dot(x, w["w_query"][0]) + row("b_query")) * 0.125).astype(BF16)
    k = dot(x, w["w_key"][0]).astype(BF16)
    v = (dot(x, w["w_value"][0]) + row("b_value")).astype(BF16)
    st["query"][...] = q
    st["key"][...] = k
    st["value"][...] = v
    q_t = q[:main].T
    v_t = v[:main].T
    live_rest = lax.broadcasted_iota(jnp.int32, (TILE, 1), 0) < rows - main
    s = dot_nt(k, spread_heads(q[main:], width))
    top, bottom = s[:main], jnp.where(live_rest, s[main:], LOW)
    peak = jnp.maximum(jnp.max(top, axis=0, keepdims=True), jnp.max(bottom, axis=0, keepdims=True))
    top, bottom = jnp.exp(top - peak), jnp.exp(bottom - peak)
    scale = 1.0 / (jnp.sum(top, axis=0, keepdims=True) + jnp.sum(bottom, axis=0, keepdims=True))
    p_rest = jnp.concatenate([(top * scale).astype(BF16), (bottom * scale).astype(BF16)], axis=0)
    st["prob_rest"][...] = p_rest
    context_rest = fold_heads(dot_tn(p_rest, v), width).astype(BF16)
    parts, bottoms = [], []
    for h in range(HEADS):
        pair = slice(2 * width * (h // 2), 2 * width * (h // 2 + 1))
        s = dot(own_half(k[:, pair], h, width), q_t[pair, :])
        top, bottom = s[:main], jnp.where(live_rest, s[main:], LOW)
        peak = jnp.maximum(jnp.max(top, axis=0, keepdims=True), jnp.max(bottom, axis=0, keepdims=True))
        top, bottom = jnp.exp(top - peak), jnp.exp(bottom - peak)
        scale = 1.0 / (jnp.sum(top, axis=0, keepdims=True) + jnp.sum(bottom, axis=0, keepdims=True))
        top, bottom = (top * scale).astype(BF16), (bottom * scale).astype(BF16)
        st["prob"][h, :main, :] = top
        st["prob"][h, main:, :] = bottom
        bottoms.append(bottom)
        parts.append(dot(v_t[h * width : (h + 1) * width, :], top))
    context_t = jnp.concatenate(parts, axis=0)
    context_t = context_t + dot_tn(spread_heads(v[main:], width), jnp.concatenate(bottoms, axis=0))
    context_t = context_t.astype(BF16)
    st["context_t"][...] = context_t
    context = jnp.concatenate([context_t.T, context_rest], axis=0)
    st["context"][...] = context
    normed_attn, inverse_attn = normalize(x.astype(F32) + dot(context, w["w_out"][0]) + row("b_out"))
    st["normed_attn"][...] = normed_attn
    middle = normed_attn * row("gain_attn") + row("shift_attn")
    middle_low = middle.astype(BF16)
    st["middle"][...] = middle_low
    total = middle + row("b_down")
    hidden_units = w["w_up"].shape[2]
    for c in range(hidden_units // features):
        part = slice(c * features, (c + 1) * features)
        u = dot(middle_low, w["w_up"][0, :, part]) + w["b_up"][layer : layer + 1, part]
        active, slope = gelu_and_slope(u)
        active = active.astype(BF16)
        st["active"][:, part] = active
        st["slope"][:, part] = slope.astype(BF16)
        total = total + dot(active, w["w_down"][0, part, :])
    normed_ffn, inverse_ffn = normalize(total)
    st["normed_ffn"][...] = normed_ffn
    st["inverse"][:, 0:1] = inverse_attn
    st["inverse"][:, 1:2] = inverse_ffn
    return normed_ffn * row("gain_ffn") + row("shift_ffn")


def layer_backward(x, grad_out, layer, w, st, g, rest, step, steps):
    full, features = x.shape
    main = full - TILE
    width = features // HEADS
    row = lambda name: w[name][layer : layer + 1, :]
    place = pl.ds(pl.multiple_of(step * TILE, TILE), TILE)

    def add(name, value):
        g[name][...] += value

    normed_ffn = st["normed_ffn"][...]
    add("gain_ffn", column_sum(grad_out * normed_ffn))
    add("shift_ffn", column_sum(grad_out))
    grad_sum = norm_back(grad_out * row("gain_ffn"), normed_ffn, st["inverse"][:, 1:2])
    grad_branch = grad_sum.astype(BF16)
    rest["branch"][place, :] = grad_branch[main:]
    add("b_down", column_sum(grad_branch))
    grad_middle = grad_sum
    middle = st["middle"][...]
    rest["middle"][place, :] = middle[main:]
    hidden_units = w["w_up"].shape[2]
    for c in range(hidden_units // features):
        part = slice(c * features, (c + 1) * features)
        grad_up = dot_nt(grad_branch, w["w_down"][0, part, :]) * st["slope"][:, part].astype(F32)
        grad_up = grad_up.astype(BF16)
        active = st["active"][:, part]
        rest["up"][place, part] = grad_up[main:]
        rest["active"][place, part] = active[main:]
        g["b_up"][:, part] += column_sum(grad_up)
        g["w_down"][part, :] += dot_tn(active[:main], grad_branch[:main])
        g["w_up"][:, part] += dot_tn(middle[:main], grad_up[:main])
        grad_middle = grad_middle + dot_nt(grad_up, w["w_up"][0, :, part])
    normed_attn = st["normed_attn"][...]
    add("gain_attn", column_sum(grad_middle * normed_attn))
    add("shift_attn", column_sum(grad_middle))
    grad_resid = norm_back(grad_middle * row("gain_attn"), normed_attn, st["inverse"][:, 0:1])
    grad_attn = grad_resid.astype(BF16)
    rest["attn"][place, :] = grad_attn[main:]
    rest["context"][place, :] = st["context"][main:, :]
    add("b_out", column_sum(grad_attn))
    context_t = st["context_t"][...]
    add("w_out", dot(context_t, grad_attn[:main]))
    grad_context = dot_nt(grad_attn, w["w_out"][0]).astype(BF16)
    grad_context_t = grad_context[:main].T
    product = grad_context_t.astype(F32) * context_t.astype(F32)
    q, k, v = st["query"][...], st["key"][...], st["value"][...]
    k_t = k[:main].T
    grad_spread = spread_heads(grad_context[main:], width)
    p_rest = st["prob_rest"][...]
    p_rest_wide = p_rest.astype(F32)
    grad_p = dot_nt(v, grad_spread)
    grad_s = p_rest_wide * (grad_p - jnp.sum(p_rest_wide * grad_p, axis=0, keepdims=True))
    grad_s = grad_s.astype(BF16)
    grad_v = dot(p_rest, grad_spread)
    grad_k = dot(grad_s, spread_heads(q[main:], width))
    grad_q_rest = fold_heads(dot_tn(grad_s, k), width).astype(BF16)
    q_parts, k_parts, v_parts, bottoms = [], [], [], []
    for h in range(HEADS):
        pair = slice(2 * width * (h // 2), 2 * width * (h // 2 + 1))
        own = slice(h * width, (h + 1) * width)
        p = st["prob"][h]
        grad_p = dot(own_half(v[:, pair], h, width), grad_context_t[pair, :])
        grad_s = p.astype(F32) * (grad_p - jnp.sum(product[own, :], axis=0, keepdims=True))
        grad_s = grad_s.astype(BF16)
        v_parts.append(dot(p, grad_context[:main, pair]))
        k_parts.append(dot(grad_s, q[:main, pair]))
        q_parts.append(dot(k_t[own, :], grad_s[:main]))
        bottoms.append(grad_s[main:])
    left = lax.broadcasted_iota(jnp.int32, (full, 2 * width), 1) < width

    def join(parts):
        return jnp.concatenate(
            [jnp.where(left, parts[i], parts[i + 1]) for i in range(0, HEADS, 2)], axis=1
        )

    grad_v = (grad_v + join(v_parts)).astype(BF16)
    grad_k = (grad_k + join(k_parts)).astype(BF16)
    grad_q_t = jnp.concatenate(q_parts, axis=0)
    grad_q_t = grad_q_t + dot_tn(spread_heads(k[main:], width), jnp.concatenate(bottoms, axis=0))
    grad_q = jnp.concatenate([grad_q_t.astype(BF16).T, grad_q_rest], axis=0) * BF16(0.125)
    rest["input"][place, :] = x[main:]
    rest["query"][place, :] = grad_q[main:]
    rest["key"][place, :] = grad_k[main:]
    rest["value"][place, :] = grad_v[main:]
    add("b_query", column_sum(grad_q))
    add("b_value", column_sum(grad_v))
    x_main = x[:main]
    add("w_query", dot_tn(x_main, grad_q[:main]))
    add("w_key", dot_tn(x_main, grad_k[:main]))
    add("w_value", dot_tn(x_main, grad_v[:main]))

    @pl.when(step == steps - 1)
    def _():
        add("w_query", dot_tn(rest["input"][...], rest["query"][...]))
        add("w_key", dot_tn(rest["input"][...], rest["key"][...]))
        add("w_value", dot_tn(rest["input"][...], rest["value"][...]))
        add("w_out", dot_tn(rest["context"][...], rest["attn"][...]))
        add("w_up", dot_tn(rest["middle"][...], rest["up"][...]))
        add("w_down", dot_tn(rest["active"][...], rest["branch"][...]))

    return (
        grad_resid
        + dot_nt(grad_q, w["w_query"][0])
        + dot_nt(grad_k, w["w_key"][0])
        + dot_nt(grad_v, w["w_value"][0])
    )


def packed_rows(features, hidden_units):
    used = 4 * features + 2 * hidden_units + len(VECTORS) + hidden_units // features
    return -(-used // 64) * 64


def emit(g, packed, features, hidden_units):
    at = 0
    for name in ("w_query", "w_key", "w_value", "w_out"):
        packed[at : at + features, :] = g[name][...].astype(BF16)
        at += features
    for c in range(hidden_units // features):
        packed[at : at + features, :] = g["w_up"][:, c * features : (c + 1) * features].astype(BF16)
        at += features
    packed[at : at + hidden_units, :] = g["w_down"][...].astype(BF16)
    at += hidden_units
    lines = [g[name][...] for name in VECTORS]
    lines += [g["b_up"][:, c * features : (c + 1) * features] for c in range(hidden_units // features)]
    lines.append(jnp.zeros((packed.shape[0] - at - len(lines), features), F32))
    packed[at:, :] = jnp.concatenate(lines, axis=0).astype(BF16)


def unpack(packed, features, hidden_units):
    out, at = {}, 0
    wide = packed.astype(F32)
    for name in ("w_query", "w_key", "w_value", "w_out"):
        out[name] = wide[:, at : at + features]
        at += features
    chunks = hidden_units // features
    out["w_up"] = jnp.concatenate(
        [wide[:, at + c * features : at + (c + 1) * features] for c in range(chunks)], axis=-1
    )
    at += hidden_units
    out["w_down"] = wide[:, at : at + hidden_units]
    at += hidden_units
    for name in VECTORS:
        out[name] = wide[:, at]
        at += 1
    out["b_up"] = wide[:, at : at + chunks].reshape(wide.shape[0], hidden_units)
    return out


def stash_shapes(full, features, hidden_units):
    main = full - TILE
    square = ((full, features), BF16)
    return {
        "query": square,
        "key": square,
        "value": square,
        "prob": ((HEADS, full, main), BF16),
        "prob_rest": ((full, HEADS * TILE), BF16),
        "context_t": ((features, main), BF16),
        "context": square,
        "inverse": ((full, 2), F32),
        "normed_attn": ((full, features), F32),
        "middle": square,
        "active": ((full, hidden_units), BF16),
        "slope": ((full, hidden_units), BF16),
        "normed_ffn": ((full, features), F32),
    }


def grad_shapes(features, hidden_units):
    sizes = {name: (features, features) for name in ("w_query", "w_key", "w_value", "w_out")}
    sizes.update({name: (1, features) for name in VECTORS})
    sizes.update(w_up=(features, hidden_units), w_down=(hidden_units, features), b_up=(1, hidden_units))
    return sizes


def rest_shapes(steps, features, hidden_units):
    sizes = {name: features for name in ("input", "query", "key", "value", "context", "attn", "middle", "branch")}
    sizes.update(up=hidden_units, active=hidden_units)
    return {name: (steps * TILE, size) for name, size in sizes.items()}


def weight_specs(weights, layer):
    specs = []
    for name in WEIGHTS:
        shape = weights[name].shape
        if len(shape) == 3:
            specs.append(pl.BlockSpec((1,) + shape[1:], lambda m: (layer, 0, 0)))
        else:
            specs.append(pl.BlockSpec(shape, lambda m: (0, 0)))
    return specs


def by_micro(shape):
    rank = len(shape)
    return pl.BlockSpec((1,) + tuple(shape[1:]), lambda m: (m,) + (0,) * (rank - 1))


def fixed(shape):
    rank = len(shape)
    return pl.BlockSpec(tuple(shape), lambda m: (0,) * rank)


PARAMS = pltpu.CompilerParams(vmem_limit_bytes=60 * 2**20, dimension_semantics=("arbitrary",))


def lower_forward_kernel(rows, x_ref, *refs):
    w = dict(zip(WEIGHTS, refs[: len(WEIGHTS)]))
    out_ref, *stash = refs[len(WEIGHTS) :]
    st = {name: ref.at[0] for name, ref in zip(STASH, stash)}
    out_ref[0] = layer_forward(x_ref[0], 0, w, st, rows).astype(BF16)


def lower_forward(x, weights, rows):
    micro, full, features = x.shape
    shapes = stash_shapes(full, features, weights["w_up"].shape[2])
    outs = [jax.ShapeDtypeStruct(x.shape, BF16)]
    outs += [jax.ShapeDtypeStruct((micro,) + shapes[name][0], shapes[name][1]) for name in STASH]
    return pl.pallas_call(
        functools.partial(lower_forward_kernel, rows),
        grid=(micro,),
        in_specs=[by_micro(x.shape)] + weight_specs(weights, 0),
        out_specs=[by_micro(o.shape) for o in outs],
        out_shape=outs,
        compiler_params=PARAMS,
        name="lower_forward",
    )(x, *[weights[name] for name in WEIGHTS])


def zero_all(g):
    for ref in g.values():
        ref[...] = jnp.zeros_like(ref)


def upper_kernel(rows, memory, lead_ref, count_ref, x_ref, arrived_ref, cot_ref, target_ref, place_ref, *refs):
    step, steps = pl.program_id(0), pl.num_programs(0)
    w = dict(zip(WEIGHTS, refs[: len(WEIGHTS)]))
    refs = refs[len(WEIGHTS) :]
    out_ref, grad_ref, back_ref, packed_ref = refs[:4]
    refs = refs[4:]
    st = dict(zip(STASH, refs[: len(STASH)]))
    refs = refs[len(STASH) :]
    full, features = x_ref.shape[1:]
    hidden_units = w["w_up"].shape[2]
    main = full - TILE
    names = list(grad_shapes(features, hidden_units))
    g = dict(zip(names, refs[: len(names)]))
    rest = dict(zip(rest_shapes(1, 1, 1), refs[len(names) :]))

    @pl.when(step == 0)
    def _():
        zero_all(g)

    lead = lead_ref[0] != 0
    x = x_ref[0]
    is_read = lax.broadcasted_iota(jnp.int32, (TILE, features), 0) < memory
    head_rows = jnp.where(jnp.logical_and(is_read, jnp.logical_not(lead)), arrived_ref[0], x[:TILE])
    x = jnp.concatenate([head_rows, x[TILE:]], axis=0)
    y = layer_forward(x, 1, w, st, rows)
    out_ref[0] = y.astype(BF16)
    count = count_ref[step]
    slots = place_ref.shape[2]
    slot_row = lax.broadcasted_iota(jnp.int32, (main, slots), 0) - memory
    slot_at = lax.broadcasted_iota(jnp.int32, (main, slots), 1)
    hit = jnp.logical_and(slot_row == place_ref[0], slot_at < count)
    hit = jnp.where(hit, 1.0, 0.0).astype(BF16)
    used = dot(hit, jnp.ones((slots, features), BF16))
    wanted = dot(hit, target_ref[0])
    grad_main = (y[:main] * used - wanted) / count.astype(F32)
    grad_out = jnp.concatenate([grad_main, cot_ref[0].astype(F32)], axis=0)
    grad_in = layer_backward(x, grad_out, 1, w, st, g, rest, step, steps)
    back_ref[0] = grad_in[:TILE].astype(BF16)
    drop = jnp.logical_and(is_read, jnp.logical_not(lead))
    grad_ref[0, :TILE, :] = jnp.where(drop, 0.0, grad_in[:TILE])
    grad_ref[0, TILE:, :] = grad_in[TILE:]

    @pl.when(step == steps - 1)
    def _():
        emit(g, packed_ref, features, hidden_units)


def smem():
    return pl.BlockSpec(memory_space=pltpu.SMEM)


def scratches(micro, features, hidden_units):
    out = [pltpu.VMEM(size, F32) for size in grad_shapes(features, hidden_units).values()]
    return out + [pltpu.VMEM(size, BF16) for size in rest_shapes(micro, features, hidden_units).values()]


def upper_both(lead, counts, x, arrived, cotangent, targets, places, weights, rows, memory):
    micro, full, features = x.shape
    hidden_units = weights["w_up"].shape[2]
    shapes = stash_shapes(full, features, hidden_units)
    outs = [
        jax.ShapeDtypeStruct(x.shape, BF16),
        jax.ShapeDtypeStruct(x.shape, F32),
        jax.ShapeDtypeStruct((micro, TILE, features), BF16),
        jax.ShapeDtypeStruct((packed_rows(features, hidden_units), features), BF16),
    ]
    ins = (x, arrived, cotangent, targets, places)
    return pl.pallas_call(
        functools.partial(upper_kernel, rows, memory),
        grid=(micro,),
        in_specs=[smem(), smem()] + [by_micro(a.shape) for a in ins] + weight_specs(weights, 1),
        out_specs=[by_micro(o.shape) for o in outs[:3]] + [fixed(outs[3].shape)],
        out_shape=outs,
        scratch_shapes=[pltpu.VMEM(*shapes[name]) for name in STASH] + scratches(micro, features, hidden_units),
        compiler_params=PARAMS,
        name="upper_both",
    )(lead, counts, *ins, *[weights[name] for name in WEIGHTS])


def lower_backward_kernel(memory, x_ref, grad_ref, back_ref, *refs):
    step, steps = pl.program_id(0), pl.num_programs(0)
    w = dict(zip(WEIGHTS, refs[: len(WEIGHTS)]))
    refs = refs[len(WEIGHTS) :]
    st = {name: ref.at[0] for name, ref in zip(STASH, refs)}
    refs = refs[len(STASH) :]
    out_ref, packed_ref = refs[:2]
    refs = refs[2:]
    full, features = x_ref.shape[1:]
    hidden_units = w["w_up"].shape[2]
    main = full - TILE
    names = list(grad_shapes(features, hidden_units))
    g = dict(zip(names, refs[: len(names)]))
    rest = dict(zip(rest_shapes(1, 1, 1), refs[len(names) :]))

    @pl.when(step == 0)
    def _():
        zero_all(g)

    is_write = lax.broadcasted_iota(jnp.int32, (TILE, features), 0) < memory
    returned = jnp.where(is_write, back_ref[0].astype(F32), 0.0)
    grad_out = jnp.concatenate([grad_ref[0, :main, :], grad_ref[0, main:, :] + returned], axis=0)
    grad_in = layer_backward(x_ref[0], grad_out, 0, w, st, g, rest, step, steps)
    out_ref[0] = grad_in.astype(BF16)

    @pl.when(step == steps - 1)
    def _():
        emit(g, packed_ref, features, hidden_units)


def lower_backward(x, grad, back, weights, stash, memory):
    micro, full, features = x.shape
    hidden_units = weights["w_up"].shape[2]
    outs = [
        jax.ShapeDtypeStruct(x.shape, BF16),
        jax.ShapeDtypeStruct((packed_rows(features, hidden_units), features), BF16),
    ]
    ins = (x, grad, back)
    return pl.pallas_call(
        functools.partial(lower_backward_kernel, memory),
        grid=(micro,),
        in_specs=[by_micro(a.shape) for a in ins]
        + weight_specs(weights, 0)
        + [by_micro(a.shape) for a in stash],
        out_specs=[by_micro(outs[0].shape), fixed(outs[1].shape)],
        out_shape=outs,
        scratch_shapes=scratches(micro, features, hidden_units),
        compiler_params=PARAMS,
        name="lower_backward",
    )(*ins, *[weights[name] for name in WEIGHTS], *stash)


def from_behind(value, axis, steps):
    count = lax.axis_size(axis)
    initial, last = (max(0, -steps), min(count, count - steps))
    return lax.ppermute(value, axis, [(source, source + steps) for source in range(initial, last)])


def sum_all(value, axes):
    order = []
    for axis in axes:
        step = 1
        while step < lax.axis_size(axis):
            order.append((axis, step))
            step *= 2
    kept, halved = value, []
    for axis, step in order:
        swap = [(i, i ^ step) for i in range(lax.axis_size(axis))]
        half = kept.shape[0] // 2
        if half % (TILE // 2):
            kept = (kept.astype(F32) + lax.ppermute(kept, axis, swap).astype(F32)).astype(BF16)
            continue
        halved.append((axis, step))
        upper = (lax.axis_index(axis) // step) % 2
        low, high = kept[:half], kept[half:]
        got = lax.ppermute(jnp.where(upper == 0, high, low), axis, swap)
        own = jnp.where(upper == 0, low, high)
        kept = (own.astype(F32) + got.astype(F32)).astype(BF16)
    for axis, step in reversed(halved):
        upper = (lax.axis_index(axis) // step) % 2
        swap = [(i, i ^ step) for i in range(lax.axis_size(axis))]
        got = lax.ppermute(kept, axis, swap)
        kept = jnp.where(upper == 0, jnp.concatenate([kept, got]), jnp.concatenate([got, kept]))
    return kept


def local(hidden, write_cotangent, targets, positions, counts, *weights):
    weights = dict(zip(WEIGHTS, weights))
    micro, _, _, rows, features = hidden.shape
    memory = write_cotangent.shape[3]
    hidden_units = weights["w_up"].shape[2]
    full = -(-rows // TILE) * TILE
    lead = (lax.axis_index("seg") == 0).astype(jnp.int32).reshape(1)
    x = jnp.pad(hidden.reshape(micro, rows, features), ((0, 0), (0, full - rows), (0, 0)))
    cotangent = write_cotangent.reshape(micro, memory, features)
    cotangent = jnp.pad(cotangent, ((0, 0), (0, TILE - memory), (0, 0)))
    target = targets.reshape(micro, targets.shape[3], features)
    places = positions.reshape(micro, 1, positions.shape[3])

    lower_out, *stash = lower_forward(x, weights, rows)
    arrived = from_behind(lower_out[:, full - TILE :], "seg", 1)
    out, grad, back, upper_packed = upper_both(
        lead, counts.reshape(micro), lower_out, arrived, cotangent, target, places, weights, rows, memory
    )
    returned = from_behind(back, "seg", -1)
    grad_in, lower_packed = lower_backward(x, grad, returned, weights, stash, memory)
    packed = jnp.concatenate([lower_packed, upper_packed], axis=0)
    packed = sum_all(packed, ("seg", "item"))
    grads = unpack(packed.reshape(2, -1, features), features, hidden_units)
    output = out[:, :rows].reshape(hidden.shape)
    hidden_grad = grad_in[:, :rows].reshape(hidden.shape)
    return (output, hidden_grad) + tuple(grads[name] for name in WEIGHTS)


def solution(mesh):
    split = P(None, "item", "seg", None, None)
    placed = (split, split, split, P(None, "item", "seg", None), P(None, "item", "seg"))
    return jax.shard_map(
        local,
        mesh=mesh,
        in_specs=placed + (P(),) * len(WEIGHTS),
        out_specs=(split, split) + (P(),) * len(WEIGHTS),
        check_vma=False,
    )
```

```python
import functools
from typing import Any, NamedTuple

import jax
import jax.numpy as jnp
from jax import lax
from jax.experimental import pallas as pl
from jax.experimental.pallas import tpu as pltpu
from jax.sharding import PartitionSpec as P

EPSILON = 1e-12
DENSITY = 0.3989422804014327
ROOT_HALF = 0.7071067811865476
HEADS = 4
TILE = 16
PIECES = 8
LOW = -1e30
F32, BF16 = jnp.float32, jnp.bfloat16


class Weights(NamedTuple):
    w_query: Any
    b_query: Any
    w_key: Any
    w_value: Any
    b_value: Any
    w_out: Any
    b_out: Any
    gain_attn: Any
    shift_attn: Any
    w_up: Any
    b_up: Any
    w_down: Any
    b_down: Any
    gain_ffn: Any
    shift_ffn: Any


class Stash(NamedTuple):
    x: Any
    query: Any
    key: Any
    value: Any
    prob: Any
    prob_rest: Any
    context_t: Any
    context: Any
    inverse: Any
    normed_attn: Any
    middle: Any
    active: Any
    slope: Any
    normed_ffn: Any


class Rest(NamedTuple):
    x: Any
    query: Any
    key: Any
    value: Any
    context: Any
    attn: Any
    middle: Any
    branch: Any
    up: Any
    active: Any


def dot(a, b):
    return jnp.dot(a, b, preferred_element_type=F32)


def dot_nt(a, b):
    return lax.dot_general(a, b, (((1,), (1,)), ((), ())), preferred_element_type=F32)


def dot_tn(a, b):
    return lax.dot_general(a, b, (((0,), (0,)), ((), ())), preferred_element_type=F32)


def mean(v):
    return jnp.mean(v, axis=-1, keepdims=True)


def column_sum(v):
    return jnp.sum(v.astype(F32), axis=0, keepdims=True)


def normalize(v):
    centred = v - mean(v)
    inverse = lax.rsqrt(mean(centred * centred) + EPSILON)
    return centred * inverse, inverse


def norm_back(grad, normed, inverse):
    return inverse * (grad - mean(grad) - normed * mean(grad * normed))


def gelu_and_slope(u):
    phi = 0.5 + 0.5 * lax.erf(u * ROOT_HALF)
    return u * phi, phi + u * (jnp.exp(u * u * -0.5) * DENSITY)


def head_block(shape, width):
    rows = lax.broadcasted_iota(jnp.int32, shape, 0) // TILE
    lanes = lax.broadcasted_iota(jnp.int32, shape, 1) // width
    return rows == lanes


def spread_heads(rest, width):
    tiled = jnp.concatenate([rest] * HEADS, axis=0)
    return jnp.where(head_block(tiled.shape, width), tiled, jnp.zeros_like(tiled))


def fold_heads(spread, width):
    own = jnp.where(head_block(spread.shape, width), spread, 0.0)
    return own[:TILE] + own[TILE : 2 * TILE] + own[2 * TILE : 3 * TILE] + own[3 * TILE :]


def own_half(pair, h, width):
    lanes = lax.broadcasted_iota(jnp.int32, pair.shape, 1) // width
    return jnp.where(lanes == h % 2, pair, jnp.zeros_like(pair))


def softmax_keys(s, live_rest):
    main = s.shape[0] - TILE
    top, bottom = s[:main], jnp.where(live_rest, s[main:], LOW)
    peak = jnp.maximum(jnp.max(top, axis=0, keepdims=True), jnp.max(bottom, axis=0, keepdims=True))
    top, bottom = jnp.exp(top - peak), jnp.exp(bottom - peak)
    scale = 1.0 / (jnp.sum(top, axis=0, keepdims=True) + jnp.sum(bottom, axis=0, keepdims=True))
    return (top * scale).astype(BF16), (bottom * scale).astype(BF16)


def layer_forward(x, layer, w, st, rows):
    full, features = x.shape
    main = full - TILE
    width = features // HEADS

    def row(ref):
        return ref[layer : layer + 1, :]

    st.x[...] = x
    q = ((dot(x, w.w_query[0]) + row(w.b_query)) * 0.125).astype(BF16)
    k = dot(x, w.w_key[0]).astype(BF16)
    v = (dot(x, w.w_value[0]) + row(w.b_value)).astype(BF16)
    st.query[...] = q
    st.key[...] = k
    st.value[...] = v
    q_t = q[:main].T
    v_t = v[:main].T
    live_rest = lax.broadcasted_iota(jnp.int32, (TILE, 1), 0) < rows - main
    top, bottom = softmax_keys(dot_nt(k, spread_heads(q[main:], width)), live_rest)
    p_rest = jnp.concatenate([top, bottom], axis=0)
    st.prob_rest[...] = p_rest
    context_rest = fold_heads(dot_tn(p_rest, v), width).astype(BF16)
    parts, bottoms, totals = [], [], []
    ones = jnp.ones((TILE, main), BF16)
    for h in range(HEADS):
        pair = slice(2 * width * (h // 2), 2 * width * (h // 2 + 1))
        top, bottom = softmax_keys(dot(own_half(k[:, pair], h, width), q_t[pair, :]), live_rest)
        st.prob[h, :main, :] = top
        st.prob[h, main:, :] = bottom
        bottoms.append(bottom)
        part = dot(jnp.concatenate([v_t[h * width : (h + 1) * width, :], ones], axis=0), top)
        parts.append(part[:width])
        totals.append(jnp.broadcast_to(1.0 / (part[width : width + 1] + column_sum(bottom)), (width, main)))
    context_t = jnp.concatenate(parts, axis=0)
    context_t = context_t + dot_tn(spread_heads(v[main:], width), jnp.concatenate(bottoms, axis=0))
    st.context_t[...] = context_t * jnp.concatenate(totals, axis=0)
    context = jnp.concatenate([context_t.astype(BF16).T, context_rest], axis=0)
    st.context[...] = context
    normed_attn, inverse_attn = normalize(x.astype(F32) + dot(context, w.w_out[0]) + row(w.b_out))
    st.normed_attn[...] = normed_attn
    middle = normed_attn * row(w.gain_attn) + row(w.shift_attn)
    middle_low = middle.astype(BF16)
    st.middle[...] = middle_low
    total = middle + row(w.b_down)
    for c in range(w.w_up.shape[2] // features):
        part = slice(c * features, (c + 1) * features)
        u = dot(middle_low, w.w_up[0, :, part]) + w.b_up[layer : layer + 1, part]
        active, slope = gelu_and_slope(u)
        active = active.astype(BF16)
        st.active[:, part] = active
        st.slope[:, part] = slope.astype(BF16)
        total = total + dot(active, w.w_down[0, part, :])
    normed_ffn, inverse_ffn = normalize(total)
    st.normed_ffn[...] = normed_ffn
    st.inverse[:, 0:1] = inverse_attn
    st.inverse[:, 1:2] = inverse_ffn
    return normed_ffn * row(w.gain_ffn) + row(w.shift_ffn)


def layer_backward(grad_out, layer, w, st, g, rest, grad_up_ref, grad_s_ref, step, steps):
    full, features = st.x.shape
    main = full - TILE
    width = features // HEADS
    place = pl.ds(pl.multiple_of(step * TILE, TILE), TILE)

    def row(ref):
        return ref[layer : layer + 1, :]

    def add(ref, value):
        ref[...] += value

    normed_ffn = st.normed_ffn[...]
    add(g.gain_ffn, column_sum(grad_out * normed_ffn))
    add(g.shift_ffn, column_sum(grad_out))
    grad_sum = norm_back(grad_out * row(w.gain_ffn), normed_ffn, st.inverse[:, 1:2])
    grad_branch = grad_sum.astype(BF16)
    rest.branch[place, :] = grad_branch[main:]
    add(g.b_down, column_sum(grad_branch))
    grad_middle = grad_sum
    for c in range(w.w_up.shape[2] // features):
        part = slice(c * features, (c + 1) * features)
        grad_up = dot_nt(grad_branch, w.w_down[0, part, :]) * st.slope[:, part].astype(F32)
        grad_up = grad_up.astype(BF16)
        grad_up_ref[:, part] = grad_up
        g.b_up[:, part] += column_sum(grad_up)
        grad_middle = grad_middle + dot_nt(grad_up, w.w_up[0, :, part])
    add(g.w_down, dot_tn(st.active[:main, :], grad_branch[:main]))
    add(g.w_up, dot_tn(grad_up_ref[:main, :], st.middle[:main, :]))
    rest.middle[place, :] = st.middle[main:, :]
    rest.up[place, :] = grad_up_ref[main:, :]
    rest.active[place, :] = st.active[main:, :]
    normed_attn = st.normed_attn[...]
    add(g.gain_attn, column_sum(grad_middle * normed_attn))
    add(g.shift_attn, column_sum(grad_middle))
    grad_resid = norm_back(grad_middle * row(w.gain_attn), normed_attn, st.inverse[:, 0:1])
    grad_attn = grad_resid.astype(BF16)
    rest.attn[place, :] = grad_attn[main:]
    rest.context[place, :] = st.context[main:, :]
    add(g.b_out, column_sum(grad_attn))
    add(g.w_out, dot_tn(st.context[:main, :], grad_attn[:main]))
    grad_context = dot_nt(grad_attn, w.w_out[0]).astype(BF16)
    grad_context_t = grad_context[:main].T
    product = grad_context_t.astype(F32) * st.context_t[...]
    q, k, v = st.query[...], st.key[...], st.value[...]
    k_t = k[:main].T
    grad_spread = spread_heads(grad_context[main:], width)
    p_rest = st.prob_rest[...]
    p_rest_wide = p_rest.astype(F32)
    grad_p = dot_nt(v, grad_spread)
    centre = jnp.sum(p_rest_wide * grad_p, axis=0, keepdims=True) / jnp.sum(p_rest_wide, axis=0, keepdims=True)
    grad_s = p_rest_wide * (grad_p - centre)
    grad_s = grad_s.astype(BF16)
    grad_v = dot(p_rest, grad_spread)
    grad_k = dot(grad_s, spread_heads(q[main:], width))
    grad_q_rest = fold_heads(dot_tn(grad_s, k), width).astype(BF16)
    left = lax.broadcasted_iota(jnp.int32, (full, 2 * width), 1) < width
    q_parts, k_parts, v_parts, bottoms = [], [], [], []
    for h in range(0, HEADS, 2):
        pair = slice(width * h, width * (h + 2))
        for i in (h, h + 1):
            own = slice(i * width, (i + 1) * width)
            grad_p = dot(own_half(v[:, pair], i, width), grad_context_t[pair, :])
            grad_s = st.prob[i].astype(F32) * (grad_p - jnp.sum(product[own, :], axis=0, keepdims=True))
            grad_s = grad_s.astype(BF16)
            grad_s_ref[i] = grad_s
            q_parts.append(dot(k_t[own, :], grad_s[:main]))
            bottoms.append(grad_s[main:])
        both = dot(st.prob[h : h + 2].reshape(2 * full, main), grad_context[:main, pair])
        v_parts.append(jnp.where(left, both[:full], both[full:]))
        both = dot(grad_s_ref[h : h + 2].reshape(2 * full, main), q[:main, pair])
        k_parts.append(jnp.where(left, both[:full], both[full:]))
    grad_v = (grad_v + jnp.concatenate(v_parts, axis=1)).astype(BF16)
    grad_k = (grad_k + jnp.concatenate(k_parts, axis=1)).astype(BF16)
    grad_q_t = jnp.concatenate(q_parts, axis=0)
    grad_q_t = grad_q_t + dot_tn(spread_heads(k[main:], width), jnp.concatenate(bottoms, axis=0))
    grad_q = jnp.concatenate([grad_q_t.astype(BF16).T, grad_q_rest], axis=0) * BF16(0.125)
    rest.x[place, :] = st.x[main:, :]
    rest.query[place, :] = grad_q[main:]
    rest.key[place, :] = grad_k[main:]
    rest.value[place, :] = grad_v[main:]
    add(g.b_query, column_sum(grad_q))
    add(g.b_value, column_sum(grad_v))
    x_main = st.x[:main, :]
    add(g.w_query, dot_tn(x_main, grad_q[:main]))
    add(g.w_key, dot_tn(x_main, grad_k[:main]))
    add(g.w_value, dot_tn(x_main, grad_v[:main]))

    @pl.when(step == steps - 1)
    def _():
        x_rest = rest.x[...]
        add(g.w_query, dot_tn(x_rest, rest.query[...]))
        add(g.w_key, dot_tn(x_rest, rest.key[...]))
        add(g.w_value, dot_tn(x_rest, rest.value[...]))
        add(g.w_out, dot_tn(rest.context[...], rest.attn[...]))
        add(g.w_up, dot_tn(rest.up[...], rest.middle[...]))
        add(g.w_down, dot_tn(rest.active[...], rest.branch[...]))

    return (
        grad_resid
        + dot_nt(grad_q, w.w_query[0])
        + dot_nt(grad_k, w.w_key[0])
        + dot_nt(grad_v, w.w_value[0])
    )


def squares(g):
    return (g.w_query, g.w_key, g.w_value, g.w_out)


def lines(g):
    return (g.b_query, g.b_value, g.b_out, g.gain_attn, g.shift_attn, g.b_down, g.gain_ffn, g.shift_ffn)


def packed_rows(features, units):
    used = 4 * features + 2 * units + len(lines(Weights(*range(len(Weights._fields))))) + units // features
    return -(-used // (PIECES * TILE)) * PIECES * TILE


def spans(sizes, rows):
    piece = rows // PIECES
    out, at = [], 0
    for index, size in enumerate(sizes):
        done = 0
        while done < size:
            take = min(size - done, piece - at % piece)
            out.append((index, done, at // piece, at % piece, take))
            done, at = done + take, at + take
    return out


def emit(g, keep, send, ordered, me):
    units, features = g.w_down.shape
    rows = ordered.shape[0]
    piece = rows // PIECES
    chunks = units // features
    arrays = squares(g) + (g.w_up, g.w_down)
    last = [ref[...] for ref in lines(g)]
    last += [g.b_up[:, c * features : (c + 1) * features] for c in range(chunks)]
    sizes = [ref.shape[0] for ref in arrays]
    left = rows - sum(sizes)
    last.append(jnp.zeros((left - len(last), features), F32))
    tail = jnp.concatenate(last, axis=0).astype(BF16)
    for index, start, which, offset, take in spans(sizes + [left], rows):
        if index < len(arrays):
            value = arrays[index][start : start + take, :].astype(BF16)
        else:
            value = tail[start : start + take]
        at = pl.multiple_of((which ^ me) * piece, TILE) + offset
        ordered[pl.ds(pl.multiple_of(at, TILE), take), :] = value
    half = rows // 2
    keep[...] = ordered[:half, :]
    send[...] = ordered[half:, :]


def stash_shapes(full, features, units):
    main = full - TILE
    square = ((full, features), BF16)
    wide = ((full, units), BF16)
    exact = ((full, features), F32)
    return Stash(
        x=square,
        query=square,
        key=square,
        value=square,
        prob=((HEADS, full, main), BF16),
        prob_rest=((full, HEADS * TILE), BF16),
        context_t=((features, main), F32),
        context=square,
        inverse=((full, 2), F32),
        normed_attn=exact,
        middle=square,
        active=wide,
        slope=wide,
        normed_ffn=exact,
    )


def scratch(micro, full, features, units):
    square, line = (features, features), (1, features)
    sums = Weights(
        w_query=square, b_query=line, w_key=square, w_value=square, b_value=line, w_out=square, b_out=line,
        gain_attn=line, shift_attn=line, w_up=(units, features), b_up=(1, units), w_down=(units, features),
        b_down=line, gain_ffn=line, shift_ffn=line,
    )
    rest = Rest(*[(micro * TILE, features)] * 8, up=(micro * TILE, units), active=(micro * TILE, units))
    out = [pltpu.VMEM(size, F32) for size in sums] + [pltpu.VMEM(size, BF16) for size in rest]
    out.append(pltpu.VMEM((full, units), BF16))
    out.append(pltpu.VMEM((HEADS, full, full - TILE), BF16))
    out.append(pltpu.VMEM((packed_rows(features, units), features), BF16))
    return out


def take_scratch(refs):
    count = len(Weights._fields)
    g, refs = Weights(*refs[:count]), refs[count:]
    count = len(Rest._fields)
    return g, Rest(*refs[:count]), *refs[count:]


def weight_specs(weights, layer):
    specs = []
    for weight in weights:
        if weight.ndim == 3:
            specs.append(pl.BlockSpec((1,) + weight.shape[1:], lambda m: (layer, 0, 0)))
        else:
            specs.append(pl.BlockSpec(weight.shape, lambda m: (0, 0)))
    return specs


def by_micro(shape):
    rank = len(shape)
    return pl.BlockSpec((1,) + tuple(shape[1:]), lambda m: (m,) + (0,) * (rank - 1))


def fixed(shape):
    rank = len(shape)
    return pl.BlockSpec(tuple(shape), lambda m: (0,) * rank)


def smem():
    return pl.BlockSpec(memory_space=pltpu.SMEM)


PARAMS = pltpu.CompilerParams(vmem_limit_bytes=60 * 2**20)


def lower_forward_kernel(x_ref, *refs):
    w, refs = Weights(*refs[: len(Weights._fields)]), refs[len(Weights._fields) :]
    out_ref, sent_ref, *refs = refs
    st = Stash(*[ref.at[0] for ref in refs[:-1]])
    padded = refs[-1]
    rows = x_ref.shape[1]
    main = padded.shape[0] - TILE
    padded[main:, :] = jnp.zeros((TILE, padded.shape[1]), BF16)
    padded[:rows, :] = x_ref[0]
    y = layer_forward(padded[...], 0, w, st, rows).astype(BF16)
    out_ref[0] = y
    sent_ref[0] = y[main:]


def lower_forward(hidden, weights, full):
    micro, rows, features = hidden.shape
    outs = [jax.ShapeDtypeStruct((micro, full, features), BF16), jax.ShapeDtypeStruct((micro, TILE, features), BF16)]
    shapes = stash_shapes(full, features, weights.w_up.shape[2])
    outs += [jax.ShapeDtypeStruct((micro,) + shape, kind) for shape, kind in shapes]
    out, sent, *stash = pl.pallas_call(
        lower_forward_kernel,
        grid=(micro,),
        in_specs=[by_micro(hidden.shape)] + weight_specs(weights, 0),
        out_specs=[by_micro(o.shape) for o in outs],
        out_shape=outs,
        scratch_shapes=[pltpu.VMEM((full, features), BF16)],
        compiler_params=PARAMS,
        name="lower_forward",
    )(hidden, *weights)
    return out, sent, Stash(*stash)


def zero_sums(g):
    for ref in g:
        ref[...] = jnp.zeros_like(ref)


def upper_kernel(rows, place_ref, count_ref, x_ref, arrived_ref, cot_ref, target_ref, slot_ref, *refs):
    step, steps = pl.program_id(0), pl.num_programs(0)
    w, refs = Weights(*refs[: len(Weights._fields)]), refs[len(Weights._fields) :]
    out_ref, grad_ref, back_ref, keep_ref, send_ref = refs[:5]
    refs = refs[5:]
    st, refs = Stash(*refs[: len(Stash._fields)]), refs[len(Stash._fields) :]
    cot_wide, *refs = refs
    g, rest, grad_up_ref, grad_s_ref, ordered = take_scratch(refs)
    full, features = x_ref.shape[1:]
    memory = cot_ref.shape[1]
    main = full - TILE

    @pl.when(step == 0)
    def _():
        zero_sums(g)
        cot_wide[...] = jnp.zeros_like(cot_wide)

    lead = place_ref[1] != 0
    x = x_ref[0]
    is_read = lax.broadcasted_iota(jnp.int32, (TILE, features), 0) < memory
    moved = jnp.logical_and(is_read, jnp.logical_not(lead))
    x = jnp.concatenate([jnp.where(moved, arrived_ref[0], x[:TILE]), x[TILE:]], axis=0)
    y = layer_forward(x, 1, w, st, rows)
    out_ref[0] = y[:rows].astype(BF16)
    count = count_ref[step]
    slots = slot_ref.shape[2]
    slot_row = lax.broadcasted_iota(jnp.int32, (main, slots), 0) - memory
    slot_at = lax.broadcasted_iota(jnp.int32, (main, slots), 1)
    hit = jnp.logical_and(slot_row == slot_ref[0], slot_at < count)
    hit = jnp.where(hit, 1.0, 0.0).astype(BF16)
    used = dot(hit, jnp.ones((slots, features), BF16))
    wanted = dot(hit, target_ref[0])
    grad_main = (y[:main] * used - wanted) / count.astype(F32)
    cot_wide[:memory, :] = cot_ref[0].astype(F32)
    grad_out = jnp.concatenate([grad_main, cot_wide[...]], axis=0)
    grad_in = layer_backward(grad_out, 1, w, st, g, rest, grad_up_ref, grad_s_ref, step, steps)
    back_ref[0] = grad_in[:TILE].astype(BF16)
    grad_ref[0, :TILE, :] = jnp.where(moved, 0.0, grad_in[:TILE])
    grad_ref[0, TILE:, :] = grad_in[TILE:]

    @pl.when(step == steps - 1)
    def _():
        emit(g, keep_ref, send_ref, ordered, place_ref[0])


def half_packed(features, units):
    return jax.ShapeDtypeStruct((packed_rows(features, units) // 2, features), BF16)


def upper_both(place, counts, x, arrived, cotangent, targets, slots, weights, rows):
    micro, full, features = x.shape
    units = weights.w_up.shape[2]
    outs = [
        jax.ShapeDtypeStruct((micro, rows, features), BF16),
        jax.ShapeDtypeStruct(x.shape, F32),
        jax.ShapeDtypeStruct((micro, TILE, features), BF16),
        half_packed(features, units),
        half_packed(features, units),
    ]
    ins = (x, arrived, cotangent, targets, slots)
    return pl.pallas_call(
        functools.partial(upper_kernel, rows),
        grid=(micro,),
        in_specs=[smem(), smem()] + [by_micro(a.shape) for a in ins] + weight_specs(weights, 1),
        out_specs=[by_micro(o.shape) for o in outs[:3]] + [fixed(o.shape) for o in outs[3:]],
        out_shape=outs,
        scratch_shapes=[pltpu.VMEM(*shape) for shape in stash_shapes(full, features, units)]
        + [pltpu.VMEM((TILE, features), F32)]
        + scratch(micro, full, features, units),
        compiler_params=PARAMS,
        name="upper_both",
    )(place, counts, *ins, *weights)


def lower_backward_kernel(memory, place_ref, grad_ref, back_ref, *refs):
    step, steps = pl.program_id(0), pl.num_programs(0)
    w, refs = Weights(*refs[: len(Weights._fields)]), refs[len(Weights._fields) :]
    st, refs = Stash(*[ref.at[0] for ref in refs[: len(Stash._fields)]]), refs[len(Stash._fields) :]
    out_ref, keep_ref, send_ref, *refs = refs
    g, rest, grad_up_ref, grad_s_ref, ordered = take_scratch(refs)
    full, features = grad_ref.shape[1:]
    main = full - TILE

    @pl.when(step == 0)
    def _():
        zero_sums(g)

    is_write = lax.broadcasted_iota(jnp.int32, (TILE, features), 0) < memory
    returned = jnp.where(is_write, back_ref[0].astype(F32), 0.0)
    grad_out = jnp.concatenate([grad_ref[0, :main, :], grad_ref[0, main:, :] + returned], axis=0)
    grad_in = layer_backward(grad_out, 0, w, st, g, rest, grad_up_ref, grad_s_ref, step, steps)
    out_ref[0] = grad_in[: out_ref.shape[1]].astype(BF16)

    @pl.when(step == steps - 1)
    def _():
        emit(g, keep_ref, send_ref, ordered, place_ref[0])


def lower_backward(place, grad, back, weights, stash, rows, memory):
    micro, full, features = grad.shape
    units = weights.w_up.shape[2]
    outs = [
        jax.ShapeDtypeStruct((micro, rows, features), BF16),
        half_packed(features, units),
        half_packed(features, units),
    ]
    return pl.pallas_call(
        functools.partial(lower_backward_kernel, memory),
        grid=(micro,),
        in_specs=[smem(), by_micro(grad.shape), by_micro(back.shape)]
        + weight_specs(weights, 0)
        + [by_micro(a.shape) for a in stash],
        out_specs=[by_micro(outs[0].shape)] + [fixed(o.shape) for o in outs[1:]],
        out_shape=outs,
        scratch_shapes=scratch(micro, full, features, units),
        compiler_params=PARAMS,
        name="lower_backward",
    )(place, grad, back, *weights, *stash)


def unpack_kernel(place_ref, lower_keep, lower_got, upper_keep, upper_got, *refs):
    out, ordered = Weights(*refs[: len(Weights._fields)]), refs[-1]
    features, units = out.w_up.shape[1:]
    chunks = units // features
    half = lower_keep.shape[0]
    rows, piece = 2 * half, 2 * half // PIECES
    for layer, (keep, got) in enumerate(((lower_keep, lower_got), (upper_keep, upper_got))):
        me = place_ref[layer]
        ordered[:half, :] = keep[...]
        ordered[half:, :] = got[...]
        sizes = [features] * 4 + [units, units]
        sizes.append(rows - sum(sizes))
        arrays = squares(out) + (out.w_up, out.w_down)
        for index, start, which, offset, take in spans(sizes, rows):
            at = pl.multiple_of((which ^ me) * piece, TILE) + offset
            value = ordered[pl.ds(pl.multiple_of(at, TILE), take), :].astype(F32)
            if index == 4:
                out.w_up[layer, :, start : start + take] = value.T
            elif index < 6:
                arrays[index][layer, start : start + take, :] = value
            else:
                names = lines(out)
                for i, ref in enumerate(names):
                    ref[layer : layer + 1, :] = value[i : i + 1]
                for c in range(chunks):
                    i = len(names) + c
                    out.b_up[layer : layer + 1, c * features : (c + 1) * features] = value[i : i + 1]


def unpack(places, parts, weights):
    outs = [jax.ShapeDtypeStruct(weight.shape, F32) for weight in weights]
    return pl.pallas_call(
        unpack_kernel,
        in_specs=[smem()] + [pl.BlockSpec(memory_space=pltpu.VMEM)] * 4,
        out_specs=[pl.BlockSpec(memory_space=pltpu.VMEM)] * len(outs),
        out_shape=outs,
        scratch_shapes=[pltpu.VMEM((2 * parts[0].shape[0], parts[0].shape[1]), BF16)],
        compiler_params=PARAMS,
        name="unpack",
    )(places, *parts)


def from_behind(value, axis, steps):
    count = lax.axis_size(axis)
    initial, last = (max(0, -steps), min(count, count - steps))
    return lax.ppermute(value, axis, [(source, source + steps) for source in range(initial, last)])


def swap(value, bit):
    axis, step = bit
    return lax.ppermute(value, axis, [(i, i ^ step) for i in range(lax.axis_size(axis))])


def plus(a, b):
    return (a.astype(F32) + b.astype(F32)).astype(BF16)


def place_of(bits):
    me = jnp.int32(0)
    for axis, step in bits:
        me = me * 2 + (lax.axis_index(axis) // step) % 2
    return me


def sum_rest(value, bits):
    kept, halved = value, []
    for axis, step in bits:
        half = kept.shape[0] // 2
        if half % (TILE // 2):
            kept = plus(kept, swap(kept, (axis, step)))
            continue
        halved.append((axis, step))
        upper = (lax.axis_index(axis) // step) % 2
        low, high = kept[:half], kept[half:]
        got = swap(jnp.where(upper == 0, high, low), (axis, step))
        kept = plus(jnp.where(upper == 0, low, high), got)
    for axis, step in reversed(halved):
        upper = (lax.axis_index(axis) // step) % 2
        got = swap(kept, (axis, step))
        kept = jnp.where(upper == 0, jnp.concatenate([kept, got]), jnp.concatenate([got, kept]))
    return kept


def sum_all(lower, upper, lower_bits, upper_bits, rest_bits):
    chains = []
    for (keep, send), bits in ((lower, lower_bits), (upper, upper_bits)):
        chains.append((plus(keep, swap(send, bits[0])), bits))
    for level in (1, 2):
        sent = [swap(kept[kept.shape[0] // 2 :], bits[level]) for kept, bits in chains]
        chains = [(plus(kept[: kept.shape[0] // 2], got), bits) for got, (kept, bits) in zip(sent, chains)]
    size = chains[0][0].shape[0]
    both = sum_rest(jnp.concatenate([kept for kept, _ in chains], axis=0), rest_bits)
    chains = [(both[:size], lower_bits), (both[size:], upper_bits)]
    for level in (2, 1):
        sent = [swap(kept, bits[level]) for kept, bits in chains]
        chains = [(jnp.concatenate([kept, got], axis=0), bits) for got, (kept, bits) in zip(sent, chains)]
    out = []
    for kept, bits in chains:
        out += [kept, swap(kept, bits[0])]
    return out


def local(hidden, write_cotangent, targets, positions, counts, *weights):
    weights = Weights(*weights)
    micro, _, _, rows, features = hidden.shape
    memory = write_cotangent.shape[3]
    full = -(-rows // TILE) * TILE
    bits = [(axis, 1 << i) for axis in ("seg", "item") for i in range(lax.axis_size(axis).bit_length() - 1)]
    core, along, across = ("seg", 1), ("seg", 2), ("item", 1)
    lower_bits, upper_bits = (core, across, along), (core, along, across)
    rest_bits = [bit for bit in bits if bit not in lower_bits]
    lead = (lax.axis_index("seg") == 0).astype(jnp.int32)
    places = [place_of(lower_bits), place_of(upper_bits)]
    lower_place, upper_place = (jnp.stack([place, lead]) for place in places)

    hidden_rows = hidden.reshape(micro, rows, features)
    lower_out, sent, stash = lower_forward(hidden_rows, weights, full)
    arrived = from_behind(sent, "seg", 1)
    out, grad, back, *upper = upper_both(
        upper_place,
        counts.reshape(micro),
        lower_out,
        arrived,
        write_cotangent.reshape(micro, memory, features),
        targets.reshape(micro, targets.shape[3], features),
        positions.reshape(micro, 1, positions.shape[3]),
        weights,
        rows,
    )
    returned = from_behind(back, "seg", -1)
    grad_in, *lower = lower_backward(lower_place, grad, returned, weights, stash, rows, memory)
    parts = sum_all(lower, upper, lower_bits, upper_bits, rest_bits)
    grads = unpack(jnp.stack(places), parts, weights)
    return (out.reshape(hidden.shape), grad_in.reshape(hidden.shape)) + tuple(grads)


def solution(mesh):
    split = P(None, "item", "seg", None, None)
    placed = (split, split, split, P(None, "item", "seg", None), P(None, "item", "seg"))
    count = len(Weights._fields)
    return jax.shard_map(
        local,
        mesh=mesh,
        in_specs=placed + (P(),) * count,
        out_specs=(split, split) + (P(),) * count,
        check_vma=False,
    )
```

```python
import functools
from typing import Any, NamedTuple

import jax
import jax.numpy as jnp
from jax import lax
from jax.experimental import pallas as pl
from jax.experimental.pallas import tpu as pltpu
from jax.sharding import PartitionSpec as P

EPSILON = 1e-12
DENSITY = 0.3989422804014327
ROOT_HALF = 0.7071067811865476
HEADS = 4
TILE = 16
PIECES = 8
LOW = -1e30
F32, BF16 = jnp.float32, jnp.bfloat16


class Weights(NamedTuple):
    w_query: Any
    b_query: Any
    w_key: Any
    w_value: Any
    b_value: Any
    w_out: Any
    b_out: Any
    gain_attn: Any
    shift_attn: Any
    w_up: Any
    b_up: Any
    w_down: Any
    b_down: Any
    gain_ffn: Any
    shift_ffn: Any


class Stash(NamedTuple):
    x: Any
    query: Any
    key: Any
    value: Any
    prob: Any
    prob_rest: Any
    context_t: Any
    context: Any
    inverse: Any
    normed_attn: Any
    middle: Any
    active: Any
    slope: Any
    normed_ffn: Any


class Rest(NamedTuple):
    x: Any
    query: Any
    key: Any
    value: Any
    context: Any
    attn: Any
    middle: Any
    branch: Any
    up: Any
    active: Any


def dot(a, b):
    return jnp.dot(a, b, preferred_element_type=F32)


def dot_nt(a, b):
    return lax.dot_general(a, b, (((1,), (1,)), ((), ())), preferred_element_type=F32)


def dot_tn(a, b):
    return lax.dot_general(a, b, (((0,), (0,)), ((), ())), preferred_element_type=F32)


def mean(v):
    return jnp.mean(v, axis=-1, keepdims=True)


def column_sum(v):
    return jnp.sum(v.astype(F32), axis=0, keepdims=True)


def normalize(v):
    centred = v - mean(v)
    inverse = lax.rsqrt(mean(centred * centred) + EPSILON)
    return centred * inverse, inverse


def norm_back(grad, normed, inverse):
    return inverse * (grad - mean(grad) - normed * mean(grad * normed))


def gelu_and_slope(u):
    phi = 0.5 + 0.5 * lax.erf(u * ROOT_HALF)
    return u * phi, phi + u * (jnp.exp(u * u * -0.5) * DENSITY)


def head_block(shape, width):
    rows = lax.div(lax.broadcasted_iota(jnp.int32, shape, 0), TILE)
    lanes = lax.div(lax.broadcasted_iota(jnp.int32, shape, 1), width)
    return rows == lanes


def spread_heads(rest, width):
    tiled = jnp.concatenate([rest] * HEADS, axis=0)
    return jnp.where(head_block(tiled.shape, width), tiled, jnp.zeros_like(tiled))


def fold_heads(spread, width):
    own = jnp.where(head_block(spread.shape, width), spread, 0.0)
    return own[:TILE] + own[TILE : 2 * TILE] + own[2 * TILE : 3 * TILE] + own[3 * TILE :]


def own_half(pair, h, width):
    lanes = lax.div(lax.broadcasted_iota(jnp.int32, pair.shape, 1), width)
    return jnp.where(lanes == h % 2, pair, jnp.zeros_like(pair))


def softmax_keys(s, live_rest):
    main = s.shape[0] - TILE
    top, bottom = s[:main], jnp.where(live_rest, s[main:], LOW)
    peak = jnp.maximum(jnp.max(top, axis=0, keepdims=True), jnp.max(bottom, axis=0, keepdims=True))
    top, bottom = jnp.exp(top - peak), jnp.exp(bottom - peak)
    scale = 1.0 / (jnp.sum(top, axis=0, keepdims=True) + jnp.sum(bottom, axis=0, keepdims=True))
    return (top * scale).astype(BF16), (bottom * scale).astype(BF16)


def weave(*tasks):
    tasks = [[task, 0.0, total] for task, total in tasks]
    while tasks:
        task = min(tasks, key=lambda t: t[1] / t[2])
        length = next(task[0], None)
        if length is None:
            tasks.remove(task)
        else:
            task[1] += length


def layer_forward(x, layer, w, st, rows, result):
    full, features = x.shape
    main = full - TILE
    width = features // HEADS

    def row(ref):
        return ref[layer : layer + 1, :]

    st.x[...] = x
    q = ((dot(x, w.w_query[0]) + row(w.b_query)) * 0.125).astype(BF16)
    k = dot(x, w.w_key[0]).astype(BF16)
    v = (dot(x, w.w_value[0]) + row(w.b_value)).astype(BF16)
    st.query[...] = q
    st.key[...] = k
    st.value[...] = v
    yield 450
    q_t = q[:main].T
    v_t = v[:main].T
    live_rest = lax.broadcasted_iota(jnp.int32, (TILE, 1), 0) < rows - main
    top, bottom = softmax_keys(dot_nt(k, spread_heads(q[main:], width)), live_rest)
    p_rest = jnp.concatenate([top, bottom], axis=0)
    st.prob_rest[...] = p_rest
    yield 350
    context_rest = fold_heads(dot_tn(p_rest, v), width).astype(BF16)
    ones = jnp.ones((TILE, main), BF16)
    scores, weights, parts, bottoms, totals = {}, {}, [], [], []
    for h in range(-1, HEADS + 1):
        if h + 1 < HEADS:
            pair = slice(2 * width * ((h + 1) // 2), 2 * width * ((h + 1) // 2 + 1))
            scores[h + 1] = dot(own_half(k[:, pair], h + 1, width), q_t[pair, :])
        if h > 0:
            top, bottom = weights.pop(h - 1)
            part = dot(jnp.concatenate([v_t[(h - 1) * width : h * width, :], ones], axis=0), top)
            parts.append(part[:width])
            bottoms.append(bottom)
            totals.append(jnp.broadcast_to(1.0 / (part[width : width + 1] + column_sum(bottom)), (width, main)))
        if 0 <= h < HEADS:
            top, bottom = softmax_keys(scores.pop(h), live_rest)
            st.prob[h, :main, :] = top
            st.prob[h, main:, :] = bottom
            weights[h] = top, bottom
            yield 600
        else:
            yield 200
    context_t = jnp.concatenate(parts, axis=0)
    context_t = context_t + dot_tn(spread_heads(v[main:], width), jnp.concatenate(bottoms, axis=0))
    st.context_t[...] = context_t * jnp.concatenate(totals, axis=0)
    context = jnp.concatenate([context_t.astype(BF16).T, context_rest], axis=0)
    st.context[...] = context
    yield 200
    normed_attn, inverse_attn = normalize(x.astype(F32) + dot(context, w.w_out[0]) + row(w.b_out))
    st.normed_attn[...] = normed_attn
    middle = normed_attn * row(w.gain_attn) + row(w.shift_attn)
    middle_low = middle.astype(BF16)
    st.middle[...] = middle_low
    total = middle + row(w.b_down)
    yield 400
    chunks = w.w_up.shape[2] // features

    def upward(c):
        part = slice(c * features, (c + 1) * features)
        return dot(middle_low, w.w_up[0, :, part]) + w.b_up[layer : layer + 1, part]

    ahead = upward(0)
    for c in range(chunks):
        part = slice(c * features, (c + 1) * features)
        u, ahead = ahead, (upward(c + 1) if c + 1 < chunks else None)
        active, slope = gelu_and_slope(u)
        active = active.astype(BF16)
        st.active[:, part] = active
        st.slope[:, part] = slope.astype(BF16)
        total = total + dot(active, w.w_down[0, part, :])
        yield 550
    normed_ffn, inverse_ffn = normalize(total)
    st.normed_ffn[...] = normed_ffn
    st.inverse[:, 0:1] = inverse_attn
    st.inverse[:, 1:2] = inverse_ffn
    result.append(normed_ffn * row(w.gain_ffn) + row(w.shift_ffn))
    yield 400


def layer_backward(grad_out, layer, w, st, g, rest, grad_up_ref, grad_s_ref, step, result):
    full, features = st.x.shape
    main = full - TILE
    width = features // HEADS
    place = pl.ds(pl.multiple_of(step * TILE, TILE), TILE)

    def row(ref):
        return ref[layer : layer + 1, :]

    def add(ref, value):
        ref[...] += value

    normed_ffn = st.normed_ffn[...]
    add(g.gain_ffn, column_sum(grad_out * normed_ffn))
    add(g.shift_ffn, column_sum(grad_out))
    grad_sum = norm_back(grad_out * row(w.gain_ffn), normed_ffn, st.inverse[:, 1:2])
    grad_branch = grad_sum.astype(BF16)
    rest.branch[place, :] = grad_branch[main:]
    add(g.b_down, column_sum(grad_branch))
    grad_middle = grad_sum
    yield 500
    for c in range(w.w_up.shape[2] // features):
        part = slice(c * features, (c + 1) * features)
        grad_up = dot_nt(grad_branch, w.w_down[0, part, :]) * st.slope[:, part].astype(F32)
        grad_up = grad_up.astype(BF16)
        grad_up_ref[:, part] = grad_up
        g.b_up[:, part] += column_sum(grad_up)
        grad_middle = grad_middle + dot_nt(grad_up, w.w_up[0, :, part])
        yield 300
    add(g.w_down, dot_tn(st.active[:main, :], grad_branch[:main]))
    yield 400
    add(g.w_up, dot_tn(grad_up_ref[:main, :], st.middle[:main, :]))
    rest.middle[place, :] = st.middle[main:, :]
    rest.up[place, :] = grad_up_ref[main:, :]
    rest.active[place, :] = st.active[main:, :]
    yield 400
    normed_attn = st.normed_attn[...]
    add(g.gain_attn, column_sum(grad_middle * normed_attn))
    add(g.shift_attn, column_sum(grad_middle))
    grad_resid = norm_back(grad_middle * row(w.gain_attn), normed_attn, st.inverse[:, 0:1])
    grad_attn = grad_resid.astype(BF16)
    rest.attn[place, :] = grad_attn[main:]
    rest.context[place, :] = st.context[main:, :]
    add(g.b_out, column_sum(grad_attn))
    yield 500
    add(g.w_out, dot_tn(st.context[:main, :], grad_attn[:main]))
    grad_context = dot_nt(grad_attn, w.w_out[0]).astype(BF16)
    grad_context_t = grad_context[:main].T
    product = grad_context_t.astype(F32) * st.context_t[...]
    q, k, v = st.query[...], st.key[...], st.value[...]
    k_t = k[:main].T
    yield 400
    grad_spread = spread_heads(grad_context[main:], width)
    p_rest = st.prob_rest[...]
    p_rest_wide = p_rest.astype(F32)
    grad_p = dot_nt(v, grad_spread)
    centre = jnp.sum(p_rest_wide * grad_p, axis=0, keepdims=True) / jnp.sum(p_rest_wide, axis=0, keepdims=True)
    grad_s = p_rest_wide * (grad_p - centre)
    grad_s = grad_s.astype(BF16)
    grad_v = dot(p_rest, grad_spread)
    grad_k = dot(grad_s, spread_heads(q[main:], width))
    grad_q_rest = fold_heads(dot_tn(grad_s, k), width).astype(BF16)
    yield 400
    left = lax.broadcasted_iota(jnp.int32, (full, 2 * width), 1) < width
    q_parts, k_parts, v_parts, bottoms = [], [], [], []
    for h in range(0, HEADS, 2):
        pair = slice(width * h, width * (h + 2))
        for i in (h, h + 1):
            own = slice(i * width, (i + 1) * width)
            grad_p = dot(own_half(v[:, pair], i, width), grad_context_t[pair, :])
            grad_s = st.prob[i].astype(F32) * (grad_p - jnp.sum(product[own, :], axis=0, keepdims=True))
            grad_s = grad_s.astype(BF16)
            grad_s_ref[i] = grad_s
            q_parts.append(dot(k_t[own, :], grad_s[:main]))
            bottoms.append(grad_s[main:])
            yield 400
        both = dot(st.prob[h : h + 2].reshape(2 * full, main), grad_context[:main, pair])
        v_parts.append(jnp.where(left, both[:full], both[full:]))
        yield 350
        both = dot(grad_s_ref[h : h + 2].reshape(2 * full, main), q[:main, pair])
        k_parts.append(jnp.where(left, both[:full], both[full:]))
        yield 350
    grad_v = (grad_v + jnp.concatenate(v_parts, axis=1)).astype(BF16)
    grad_k = (grad_k + jnp.concatenate(k_parts, axis=1)).astype(BF16)
    grad_q_t = jnp.concatenate(q_parts, axis=0)
    grad_q_t = grad_q_t + dot_tn(spread_heads(k[main:], width), jnp.concatenate(bottoms, axis=0))
    grad_q = jnp.concatenate([grad_q_t.astype(BF16).T, grad_q_rest], axis=0) * BF16(0.125)
    rest.x[place, :] = st.x[main:, :]
    rest.query[place, :] = grad_q[main:]
    rest.key[place, :] = grad_k[main:]
    rest.value[place, :] = grad_v[main:]
    add(g.b_query, column_sum(grad_q))
    add(g.b_value, column_sum(grad_v))
    yield 400
    x_main = st.x[:main, :]
    add(g.w_query, dot_tn(x_main, grad_q[:main]))
    add(g.w_key, dot_tn(x_main, grad_k[:main]))
    add(g.w_value, dot_tn(x_main, grad_v[:main]))
    yield 400
    result.append(
        grad_resid
        + dot_nt(grad_q, w.w_query[0])
        + dot_nt(grad_k, w.w_key[0])
        + dot_nt(grad_v, w.w_value[0])
    )
    yield 300


def add_rest(g, rest):
    def add(ref, left, right):
        ref[...] += dot_tn(left[...], right[...])

    add(g.w_query, rest.x, rest.query)
    add(g.w_key, rest.x, rest.key)
    add(g.w_value, rest.x, rest.value)
    add(g.w_out, rest.context, rest.attn)
    add(g.w_up, rest.up, rest.middle)
    add(g.w_down, rest.active, rest.branch)


FORWARD, BACKWARD = 6950, 8650


def squares(g):
    return (g.w_query, g.w_key, g.w_value, g.w_out)


def lines(g):
    return (g.b_query, g.b_value, g.b_out, g.gain_attn, g.shift_attn, g.b_down, g.gain_ffn, g.shift_ffn)


def packed_rows(features, units):
    used = 4 * features + 2 * units + len(lines(Weights(*range(len(Weights._fields))))) + units // features
    return -(-used // (PIECES * TILE)) * PIECES * TILE


def spans(sizes, rows):
    piece = rows // PIECES
    out, at = [], 0
    for index, size in enumerate(sizes):
        done = 0
        while done < size:
            take = min(size - done, piece - at % piece)
            out.append((index, done, at // piece, at % piece, take))
            done, at = done + take, at + take
    return out


def emit(g, keep, send, ordered, me):
    units, features = g.w_down.shape
    rows = ordered.shape[0]
    piece = rows // PIECES
    chunks = units // features
    arrays = squares(g) + (g.w_up, g.w_down)
    last = [ref[...] for ref in lines(g)]
    last += [g.b_up[:, c * features : (c + 1) * features] for c in range(chunks)]
    sizes = [ref.shape[0] for ref in arrays]
    left = rows - sum(sizes)
    last.append(jnp.zeros((left - len(last), features), F32))
    tail = jnp.concatenate(last, axis=0).astype(BF16)
    for index, start, which, offset, take in spans(sizes + [left], rows):
        if index < len(arrays):
            value = arrays[index][start : start + take, :].astype(BF16)
        else:
            value = tail[start : start + take]
        at = pl.multiple_of((which ^ me) * piece, TILE) + offset
        ordered[pl.ds(pl.multiple_of(at, TILE), take), :] = value
    half = rows // 2
    keep[...] = ordered[:half, :]
    send[...] = ordered[half:, :]


def stash_shapes(full, features, units):
    main = full - TILE
    square = ((full, features), BF16)
    wide = ((full, units), BF16)
    exact = ((full, features), F32)
    return Stash(
        x=square,
        query=square,
        key=square,
        value=square,
        prob=((HEADS, full, main), BF16),
        prob_rest=((full, HEADS * TILE), BF16),
        context_t=((features, main), F32),
        context=square,
        inverse=((full, 2), F32),
        normed_attn=exact,
        middle=square,
        active=wide,
        slope=wide,
        normed_ffn=exact,
    )


def scratch(micro, full, features, units):
    square, line = (features, features), (1, features)
    sums = Weights(
        w_query=square, b_query=line, w_key=square, w_value=square, b_value=line, w_out=square, b_out=line,
        gain_attn=line, shift_attn=line, w_up=(units, features), b_up=(1, units), w_down=(units, features),
        b_down=line, gain_ffn=line, shift_ffn=line,
    )
    rest = Rest(*[(micro * TILE, features)] * 8, up=(micro * TILE, units), active=(micro * TILE, units))
    out = [pltpu.VMEM(size, F32) for size in sums] + [pltpu.VMEM(size, BF16) for size in rest]
    out.append(pltpu.VMEM((full, units), BF16))
    out.append(pltpu.VMEM((HEADS, full, full - TILE), BF16))
    out.append(pltpu.VMEM((packed_rows(features, units), features), BF16))
    return out


def take_scratch(refs):
    count = len(Weights._fields)
    g, refs = Weights(*refs[:count]), refs[count:]
    count = len(Rest._fields)
    return g, Rest(*refs[:count]), *refs[count:]


def weight_specs(weights, layer):
    specs = []
    for weight in weights:
        if weight.ndim == 3:
            specs.append(pl.BlockSpec((1,) + weight.shape[1:], lambda m: (layer, 0, 0)))
        else:
            specs.append(pl.BlockSpec(weight.shape, lambda m: (0, 0)))
    return specs


def by_micro(shape):
    rank = len(shape)
    return pl.BlockSpec((1,) + tuple(shape[1:]), lambda m: (m,) + (0,) * (rank - 1))


def ahead(shape):
    rank, last = len(shape), shape[0] - 1
    return pl.BlockSpec((1,) + tuple(shape[1:]), lambda m: (jnp.minimum(m, last),) + (0,) * (rank - 1))


def behind(shape):
    rank = len(shape)
    return pl.BlockSpec((1,) + tuple(shape[1:]), lambda m: (jnp.maximum(m - 1, 0),) + (0,) * (rank - 1))


def fixed(shape):
    rank = len(shape)
    return pl.BlockSpec(tuple(shape), lambda m: (0,) * rank)


def smem():
    return pl.BlockSpec(memory_space=pltpu.SMEM)


PARAMS = pltpu.CompilerParams(vmem_limit_bytes=60 * 2**20)


def lower_forward_kernel(x_ref, *refs):
    w, refs = Weights(*refs[: len(Weights._fields)]), refs[len(Weights._fields) :]
    out_ref, sent_ref, *refs = refs
    st = Stash(*[ref.at[0] for ref in refs[:-1]])
    padded = refs[-1]
    rows = x_ref.shape[1]
    main = padded.shape[0] - TILE
    padded[main:, :] = jnp.zeros((TILE, padded.shape[1]), BF16)
    padded[:rows, :] = x_ref[0]
    result = []
    weave((layer_forward(padded[...], 0, w, st, rows, result), 1))
    y = result[0].astype(BF16)
    out_ref[0] = y
    sent_ref[0] = y[main:]


def lower_forward(hidden, weights, full):
    micro, rows, features = hidden.shape
    outs = [jax.ShapeDtypeStruct((micro, full, features), BF16), jax.ShapeDtypeStruct((micro, TILE, features), BF16)]
    shapes = stash_shapes(full, features, weights.w_up.shape[2])
    outs += [jax.ShapeDtypeStruct((micro,) + shape, kind) for shape, kind in shapes]
    out, sent, *stash = pl.pallas_call(
        lower_forward_kernel,
        grid=(micro,),
        in_specs=[by_micro(hidden.shape)] + weight_specs(weights, 0),
        out_specs=[by_micro(o.shape) for o in outs],
        out_shape=outs,
        scratch_shapes=[pltpu.VMEM((full, features), BF16)],
        compiler_params=PARAMS,
        name="lower_forward",
    )(hidden, *weights)
    return out, sent, Stash(*stash)


def zero_sums(g):
    for ref in g:
        ref[...] = jnp.zeros_like(ref)


def upper_forward(rows, lead, arrived_ref, cot_ref, target_ref, slot_ref, count, x_ref, out_ref, grad_out, w, st):
    full, features = x_ref.shape[1:]
    memory = cot_ref.shape[1]
    main = full - TILE
    x = x_ref[0]
    is_read = lax.broadcasted_iota(jnp.int32, (TILE, features), 0) < memory
    moved = jnp.logical_and(is_read, jnp.logical_not(lead))
    x = jnp.concatenate([jnp.where(moved, arrived_ref[0], x[:TILE]), x[TILE:]], axis=0)
    result = []
    yield from layer_forward(x, 1, w, st, rows, result)
    y = result[0]
    out_ref[0] = y[:rows].astype(BF16)
    slots = slot_ref.shape[2]
    slot_row = lax.broadcasted_iota(jnp.int32, (main, slots), 0) - memory
    slot_at = lax.broadcasted_iota(jnp.int32, (main, slots), 1)
    hit = jnp.logical_and(slot_row == slot_ref[0], slot_at < count)
    hit = jnp.where(hit, 1.0, 0.0).astype(BF16)
    used = dot(hit, jnp.ones((slots, features), BF16))
    wanted = dot(hit, target_ref[0])
    grad_out[:main, :] = (y[:main] * used - wanted) / count.astype(F32)
    grad_out[main : main + memory, :] = cot_ref[0].astype(F32)
    yield 300


def upper_backward(lead, memory, grad_out, grad_ref, back_ref, w, st, *refs):
    result = []
    yield from layer_backward(grad_out[...], 1, w, st, *refs, result)
    grad_in = result[0]
    is_read = lax.broadcasted_iota(jnp.int32, (TILE, grad_in.shape[1]), 0) < memory
    moved = jnp.logical_and(is_read, jnp.logical_not(lead))
    back_ref[0] = grad_in[:TILE].astype(BF16)
    grad_ref[0, :TILE, :] = jnp.where(moved, 0.0, grad_in[:TILE])
    grad_ref[0, TILE:, :] = grad_in[TILE:]


def upper_kernel(rows, micro, place_ref, count_ref, x_ref, arrived_ref, cot_ref, target_ref, slot_ref, *refs):
    step = pl.program_id(0)
    w, refs = Weights(*refs[: len(Weights._fields)]), refs[len(Weights._fields) :]
    out_ref, grad_ref, back_ref, keep_ref, send_ref = refs[:5]
    refs = refs[5:]
    st, refs = Stash(*refs[: len(Stash._fields)]), refs[len(Stash._fields) :]
    grad_out, *refs = refs
    g, rest, grad_up_ref, grad_s_ref, ordered = take_scratch(refs)
    memory = cot_ref.shape[1]
    lead = place_ref[1] != 0

    def turn(slot):
        twice = Stash(*[ref if ref.shape[0] != 2 else ref.at[slot] for ref in st])
        return twice

    def forward(slot):
        count = count_ref[jnp.minimum(step, micro - 1)]
        return upper_forward(
            rows, lead, arrived_ref, cot_ref, target_ref, slot_ref, count, x_ref, out_ref, grad_out, w, turn(slot)
        )

    def backward(slot):
        return upper_backward(
            lead, memory, grad_out, grad_ref, back_ref, w, turn(slot), g, rest, grad_up_ref, grad_s_ref, step - 1
        )

    @pl.when(step == 0)
    def _():
        zero_sums(g)
        grad_out[grad_out.shape[0] - TILE :, :] = jnp.zeros((TILE, grad_out.shape[1]), F32)
        weave((forward(0), FORWARD))

    @pl.when(jnp.logical_and(step > 0, step < micro))
    def _():
        slot = lax.rem(step, 2)
        weave((forward(slot), FORWARD), (backward(1 - slot), BACKWARD))

    @pl.when(step == micro)
    def _():
        weave((backward((micro - 1) % 2), BACKWARD))
        add_rest(g, rest)
        emit(g, keep_ref, send_ref, ordered, place_ref[0])


def half_packed(features, units):
    return jax.ShapeDtypeStruct((packed_rows(features, units) // 2, features), BF16)


def upper_both(place, counts, x, arrived, cotangent, targets, slots, weights, rows):
    micro, full, features = x.shape
    units = weights.w_up.shape[2]
    outs = [
        jax.ShapeDtypeStruct((micro, rows, features), BF16),
        jax.ShapeDtypeStruct(x.shape, F32),
        jax.ShapeDtypeStruct((micro, TILE, features), BF16),
        half_packed(features, units),
        half_packed(features, units),
    ]
    ins = (x, arrived, cotangent, targets, slots)
    shapes = stash_shapes(full, features, units)
    once = (shapes.inverse, shapes.normed_attn, shapes.middle, shapes.active, shapes.slope, shapes.normed_ffn)
    stash = [pltpu.VMEM(s if (s, k) in once and (s, k) != shapes.x else (2,) + s, k) for s, k in shapes] + [pltpu.VMEM((full, features), F32)]
    return pl.pallas_call(
        functools.partial(upper_kernel, rows, micro),
        grid=(micro + 1,),
        in_specs=[smem(), smem()] + [ahead(a.shape) for a in ins] + weight_specs(weights, 1),
        out_specs=[ahead(outs[0].shape), behind(outs[1].shape), behind(outs[2].shape)]
        + [fixed(o.shape) for o in outs[3:]],
        out_shape=outs,
        scratch_shapes=stash + scratch(micro, full, features, units),
        compiler_params=PARAMS,
        name="upper_both",
    )(place, counts, *ins, *weights)


def lower_backward_kernel(memory, place_ref, grad_ref, back_ref, *refs):
    step, steps = pl.program_id(0), pl.num_programs(0)
    w, refs = Weights(*refs[: len(Weights._fields)]), refs[len(Weights._fields) :]
    st, refs = Stash(*[ref.at[0] for ref in refs[: len(Stash._fields)]]), refs[len(Stash._fields) :]
    out_ref, keep_ref, send_ref, *refs = refs
    g, rest, grad_up_ref, grad_s_ref, ordered = take_scratch(refs)
    full, features = grad_ref.shape[1:]
    main = full - TILE

    @pl.when(step == 0)
    def _():
        zero_sums(g)

    is_write = lax.broadcasted_iota(jnp.int32, (TILE, features), 0) < memory
    returned = jnp.where(is_write, back_ref[0].astype(F32), 0.0)
    grad_out = jnp.concatenate([grad_ref[0, :main, :], grad_ref[0, main:, :] + returned], axis=0)
    result = []
    weave((layer_backward(grad_out, 0, w, st, g, rest, grad_up_ref, grad_s_ref, step, result), 1))
    out_ref[0] = result[0][: out_ref.shape[1]].astype(BF16)

    @pl.when(step == steps - 1)
    def _():
        add_rest(g, rest)
        emit(g, keep_ref, send_ref, ordered, place_ref[0])


def lower_backward(place, grad, back, weights, stash, rows, memory):
    micro, full, features = grad.shape
    units = weights.w_up.shape[2]
    outs = [
        jax.ShapeDtypeStruct((micro, rows, features), BF16),
        half_packed(features, units),
        half_packed(features, units),
    ]
    return pl.pallas_call(
        functools.partial(lower_backward_kernel, memory),
        grid=(micro,),
        in_specs=[smem(), by_micro(grad.shape), by_micro(back.shape)]
        + weight_specs(weights, 0)
        + [by_micro(a.shape) for a in stash],
        out_specs=[by_micro(outs[0].shape)] + [fixed(o.shape) for o in outs[1:]],
        out_shape=outs,
        scratch_shapes=scratch(micro, full, features, units),
        compiler_params=PARAMS,
        name="lower_backward",
    )(place, grad, back, *weights, *stash)


def unpack_kernel(place_ref, lower_keep, lower_got, upper_keep, upper_got, *refs):
    out, ordered = Weights(*refs[: len(Weights._fields)]), refs[-1]
    features, units = out.w_up.shape[1:]
    chunks = units // features
    half = lower_keep.shape[0]
    rows, piece = 2 * half, 2 * half // PIECES
    for layer, (keep, got) in enumerate(((lower_keep, lower_got), (upper_keep, upper_got))):
        me = place_ref[layer]
        ordered[:half, :] = keep[...]
        ordered[half:, :] = got[...]
        sizes = [features] * 4 + [units, units]
        sizes.append(rows - sum(sizes))
        arrays = squares(out) + (out.w_up, out.w_down)
        for index, start, which, offset, take in spans(sizes, rows):
            at = pl.multiple_of((which ^ me) * piece, TILE) + offset
            value = ordered[pl.ds(pl.multiple_of(at, TILE), take), :].astype(F32)
            if index == 4:
                out.w_up[layer, :, start : start + take] = value.T
            elif index < 6:
                arrays[index][layer, start : start + take, :] = value
            else:
                names = lines(out)
                for i, ref in enumerate(names):
                    ref[layer : layer + 1, :] = value[i : i + 1]
                for c in range(chunks):
                    i = len(names) + c
                    out.b_up[layer : layer + 1, c * features : (c + 1) * features] = value[i : i + 1]


def unpack(places, parts, weights):
    outs = [jax.ShapeDtypeStruct(weight.shape, F32) for weight in weights]
    return pl.pallas_call(
        unpack_kernel,
        in_specs=[smem()] + [pl.BlockSpec(memory_space=pltpu.VMEM)] * 4,
        out_specs=[pl.BlockSpec(memory_space=pltpu.VMEM)] * len(outs),
        out_shape=outs,
        scratch_shapes=[pltpu.VMEM((2 * parts[0].shape[0], parts[0].shape[1]), BF16)],
        compiler_params=PARAMS,
        name="unpack",
    )(places, *parts)


def from_behind(value, axis, steps):
    count = lax.axis_size(axis)
    initial, last = (max(0, -steps), min(count, count - steps))
    return lax.ppermute(value, axis, [(source, source + steps) for source in range(initial, last)])


def swap(value, bit):
    axis, step = bit
    return lax.ppermute(value, axis, [(i, i ^ step) for i in range(lax.axis_size(axis))])


def plus(a, b):
    return (a.astype(F32) + b.astype(F32)).astype(BF16)


def place_of(bits):
    me = jnp.int32(0)
    for axis, step in bits:
        me = me * 2 + (lax.axis_index(axis) // step) % 2
    return me


def sum_rest(value, bits):
    kept, halved = value, []
    for axis, step in bits:
        half = kept.shape[0] // 2
        if half % (TILE // 2):
            kept = plus(kept, swap(kept, (axis, step)))
            continue
        halved.append((axis, step))
        upper = (lax.axis_index(axis) // step) % 2
        low, high = kept[:half], kept[half:]
        got = swap(jnp.where(upper == 0, high, low), (axis, step))
        kept = plus(jnp.where(upper == 0, low, high), got)
    for axis, step in reversed(halved):
        upper = (lax.axis_index(axis) // step) % 2
        got = swap(kept, (axis, step))
        kept = jnp.where(upper == 0, jnp.concatenate([kept, got]), jnp.concatenate([got, kept]))
    return kept


def sum_all(lower, upper, lower_bits, upper_bits, rest_bits):
    chains = []
    for (keep, send), bits in ((lower, lower_bits), (upper, upper_bits)):
        chains.append((plus(keep, swap(send, bits[0])), bits))
    for level in (1, 2):
        sent = [swap(kept[kept.shape[0] // 2 :], bits[level]) for kept, bits in chains]
        chains = [(plus(kept[: kept.shape[0] // 2], got), bits) for got, (kept, bits) in zip(sent, chains)]
    size = chains[0][0].shape[0]
    both = sum_rest(jnp.concatenate([kept for kept, _ in chains], axis=0), rest_bits)
    chains = [(both[:size], lower_bits), (both[size:], upper_bits)]
    for level in (2, 1):
        sent = [swap(kept, bits[level]) for kept, bits in chains]
        chains = [(jnp.concatenate([kept, got], axis=0), bits) for got, (kept, bits) in zip(sent, chains)]
    out = []
    for kept, bits in chains:
        out += [kept, swap(kept, bits[0])]
    return out


def local(hidden, write_cotangent, targets, positions, counts, *weights):
    weights = Weights(*weights)
    micro, _, _, rows, features = hidden.shape
    memory = write_cotangent.shape[3]
    full = -(-rows // TILE) * TILE
    bits = [(axis, 1 << i) for axis in ("seg", "item") for i in range(lax.axis_size(axis).bit_length() - 1)]
    core, along, across = ("seg", 1), ("seg", 2), ("item", 1)
    lower_bits, upper_bits = (core, across, along), (core, along, across)
    rest_bits = [bit for bit in bits if bit not in lower_bits]
    lead = (lax.axis_index("seg") == 0).astype(jnp.int32)
    places = [place_of(lower_bits), place_of(upper_bits)]
    lower_place, upper_place = (jnp.stack([place, lead]) for place in places)

    hidden_rows = hidden.reshape(micro, rows, features)
    lower_out, sent, stash = lower_forward(hidden_rows, weights, full)
    arrived = from_behind(sent, "seg", 1)
    out, grad, back, *upper = upper_both(
        upper_place,
        counts.reshape(micro),
        lower_out,
        arrived,
        write_cotangent.reshape(micro, memory, features),
        targets.reshape(micro, targets.shape[3], features),
        positions.reshape(micro, 1, positions.shape[3]),
        weights,
        rows,
    )
    returned = from_behind(back, "seg", -1)
    grad_in, *lower = lower_backward(lower_place, grad, returned, weights, stash, rows, memory)
    parts = sum_all(lower, upper, lower_bits, upper_bits, rest_bits)
    grads = unpack(jnp.stack(places), parts, weights)
    return (out.reshape(hidden.shape), grad_in.reshape(hidden.shape)) + tuple(grads)


def solution(mesh):
    split = P(None, "item", "seg", None, None)
    placed = (split, split, split, P(None, "item", "seg", None), P(None, "item", "seg"))
    count = len(Weights._fields)
    return jax.shard_map(
        local,
        mesh=mesh,
        in_specs=placed + (P(),) * count,
        out_specs=(split, split) + (P(),) * count,
        check_vma=False,
    )
```

```python
import functools
from typing import Any, NamedTuple

import jax
import jax.numpy as jnp
from jax import lax
from jax.experimental import pallas as pl
from jax.experimental.layout import Layout, with_layout_constraint
from jax.experimental.pallas import tpu as pltpu
from jax.sharding import PartitionSpec as P

EPSILON = 1e-12
DENSITY = 0.3989422804014327
ROOT_HALF = 0.7071067811865476
BELL = -0.7213475204444817
HEADS = 4
TILE = 16
STRIP = 64
PIECES = 8
LOW = -1e30
F32, BF16 = jnp.float32, jnp.bfloat16
LINE, PAIR = "seg", "item"


class Weights(NamedTuple):
    w_query: Any
    b_query: Any
    w_key: Any
    w_value: Any
    b_value: Any
    w_out: Any
    b_out: Any
    gain_attn: Any
    shift_attn: Any
    w_up: Any
    b_up: Any
    w_down: Any
    b_down: Any
    gain_ffn: Any
    shift_ffn: Any


class Stash(NamedTuple):
    x: Any
    query: Any
    key: Any
    value: Any
    prob: Any
    prob_rest: Any
    scale: Any
    context_t: Any
    context: Any
    inverse: Any
    normed_attn: Any
    middle: Any
    active: Any
    slope: Any
    normed_ffn: Any


class Rest(NamedTuple):
    x: Any
    query: Any
    key: Any
    value: Any
    context: Any
    attn: Any
    middle: Any
    branch: Any
    up: Any
    active: Any


def dot(a, b):
    return jnp.dot(a, b, preferred_element_type=F32)


def dot_nt(a, b):
    return lax.dot_general(a, b, (((1,), (1,)), ((), ())), preferred_element_type=F32)


def dot_tn(a, b):
    return lax.dot_general(a, b, (((0,), (0,)), ((), ())), preferred_element_type=F32)


def mean(v):
    return jnp.mean(v, axis=-1, keepdims=True)


def column_sum(v):
    return jnp.sum(v.astype(F32), axis=0, keepdims=True)


def normalize(v):
    centred = v - mean(v)
    inverse = lax.rsqrt(mean(centred * centred) + EPSILON)
    return centred * inverse, inverse


def norm_back(grad, normed, inverse):
    return inverse * (grad - mean(grad) - normed * mean(grad * normed))


def head_block(shape, width):
    rows = lax.div(lax.broadcasted_iota(jnp.int32, shape, 0), TILE)
    lanes = lax.div(lax.broadcasted_iota(jnp.int32, shape, 1), width)
    return rows == lanes


def spread_heads(rest, width):
    tiled = jnp.concatenate([rest] * HEADS, axis=0)
    return jnp.where(head_block(tiled.shape, width), tiled, jnp.zeros_like(tiled))


def fold_heads(spread, width):
    own = jnp.where(head_block(spread.shape, width), spread, 0.0)
    return own[:TILE] + own[TILE : 2 * TILE] + own[2 * TILE : 3 * TILE] + own[3 * TILE :]


def own_half(pair, h, width):
    lanes = lax.div(lax.broadcasted_iota(jnp.int32, pair.shape, 1), width)
    return jnp.where(lanes == h % 2, pair, jnp.zeros_like(pair))


def weigh_keys(s, live_rest):
    main = s.shape[0] - TILE
    top, bottom = s[:main], jnp.where(live_rest, s[main:], LOW)
    peak = jnp.maximum(jnp.max(top, axis=0, keepdims=True), jnp.max(bottom, axis=0, keepdims=True))
    yield 120
    top = jnp.exp(top - peak).astype(BF16)
    yield 220
    return top, jnp.exp(bottom - peak).astype(BF16)


def weave(*tasks):
    tasks = [[task, 0.0, total] for task, total in tasks]
    while tasks:
        task = min(tasks, key=lambda t: t[1] / t[2])
        length = next(task[0], None)
        if length is None:
            tasks.remove(task)
        else:
            task[1] += length


def layer_forward(x, layer, w, st, rows, result):
    full, features = x.shape
    main = full - TILE
    width = features // HEADS

    def row(ref):
        return ref[layer : layer + 1, :]

    st.x[...] = x
    q = ((dot(x, w.w_query[0]) + row(w.b_query)) * 0.125).astype(BF16)
    yield 150
    k = dot(x, w.w_key[0]).astype(BF16)
    yield 150
    v = (dot(x, w.w_value[0]) + row(w.b_value)).astype(BF16)
    st.query[...] = q
    st.key[...] = k
    st.value[...] = v
    yield 150
    q_t = q[:main].T
    v_t = v[:main].T
    live_rest = lax.broadcasted_iota(jnp.int32, (TILE, 1), 0) < rows - main
    top, bottom = yield from weigh_keys(dot_nt(k, spread_heads(q[main:], width)), live_rest)
    p_rest = jnp.concatenate([top, bottom], axis=0)
    p_rest = (p_rest.astype(F32) * (1.0 / column_sum(p_rest))).astype(BF16)
    st.prob_rest[...] = p_rest
    yield 50
    context_rest = fold_heads(dot_tn(p_rest, v), width).astype(BF16)
    ones = jnp.ones((TILE, main), BF16)
    scores, weights, parts, bottoms, scales = {}, {}, [], [], []
    for h in range(-1, HEADS + 1):
        if h + 1 < HEADS:
            pair = slice(2 * width * ((h + 1) // 2), 2 * width * ((h + 1) // 2 + 1))
            scores[h + 1] = dot(own_half(k[:, pair], h + 1, width), q_t[pair, :])
            yield 80
        if h > 0:
            top, bottom = weights.pop(h - 1)
            part = dot(jnp.concatenate([v_t[(h - 1) * width : h * width, :], ones], axis=0), top)
            parts.append(part[:width])
            bottoms.append(bottom)
            scale = 1.0 / (part[width : width + 1] + column_sum(bottom))
            st.scale[h - 1 : h, :] = scale
            scales.append(jnp.broadcast_to(scale, (width, main)))
            yield 80
        if 0 <= h < HEADS:
            top, bottom = yield from weigh_keys(scores.pop(h), live_rest)
            st.prob[h, :main, :] = top
            st.prob[h, main:, :] = bottom
            weights[h] = top, bottom
            yield 60
    context_t = jnp.concatenate(parts, axis=0)
    context_t = context_t + dot_tn(spread_heads(v[main:], width), jnp.concatenate(bottoms, axis=0))
    context_t = context_t * jnp.concatenate(scales, axis=0)
    st.context_t[...] = context_t
    context = jnp.concatenate([context_t.astype(BF16).T, context_rest], axis=0)
    st.context[...] = context
    yield 200
    normed_attn, inverse_attn = normalize(x.astype(F32) + dot(context, w.w_out[0]) + row(w.b_out))
    st.normed_attn[...] = normed_attn
    middle = normed_attn * row(w.gain_attn) + row(w.shift_attn)
    middle_low = middle.astype(BF16)
    st.middle[...] = middle_low
    total = middle + row(w.b_down)
    yield 400
    chunks = w.w_up.shape[2] // features

    def upward(c):
        part = slice(c * features, (c + 1) * features)
        return dot(middle_low, w.w_up[0, :, part]) + w.b_up[layer : layer + 1, part]

    ahead = upward(0)
    for c in range(chunks):
        part = slice(c * features, (c + 1) * features)
        u, ahead = ahead, (upward(c + 1) if c + 1 < chunks else None)
        yield 50
        phi = 0.5 + 0.5 * lax.erf(u * ROOT_HALF)
        active = (u * phi).astype(BF16)
        st.active[:, part] = active
        yield 200
        slope = phi + u * (jnp.exp2(u * u * BELL) * DENSITY)
        st.slope[:, part] = slope.astype(BF16)
        yield 220
        total = total + dot(active, w.w_down[0, part, :])
        yield 80
    normed_ffn, inverse_ffn = normalize(total)
    st.normed_ffn[...] = normed_ffn
    st.inverse[:, 0:1] = inverse_attn
    st.inverse[:, 1:2] = inverse_ffn
    result.append(normed_ffn * row(w.gain_ffn) + row(w.shift_ffn))
    yield 400


def layer_backward(grad_out, layer, w, st, g, rest, grad_up_ref, grad_s_ref, step, result):
    full, features = st.x.shape
    main = full - TILE
    width = features // HEADS
    place = pl.ds(pl.multiple_of(step * TILE, TILE), TILE)

    def row(ref):
        return ref[layer : layer + 1, :]

    def add(ref, value):
        ref[...] += value

    normed_ffn = st.normed_ffn[...]
    add(g.gain_ffn, column_sum(grad_out * normed_ffn))
    add(g.shift_ffn, column_sum(grad_out))
    grad_sum = norm_back(grad_out * row(w.gain_ffn), normed_ffn, st.inverse[:, 1:2])
    grad_branch = grad_sum.astype(BF16)
    rest.branch[place, :] = grad_branch[main:]
    add(g.b_down, column_sum(grad_branch))
    grad_middle = grad_sum
    yield 500
    for c in range(w.w_up.shape[2] // features):
        part = slice(c * features, (c + 1) * features)
        grad_up = dot_nt(grad_branch, w.w_down[0, part, :]) * st.slope[:, part].astype(F32)
        grad_up = grad_up.astype(BF16)
        yield 150
        grad_up_ref[:, part] = grad_up
        g.b_up[:, part] += column_sum(grad_up)
        grad_middle = grad_middle + dot_nt(grad_up, w.w_up[0, :, part])
        yield 150
    add(g.w_down, dot_tn(st.active[:main, :], grad_branch[:main]))
    yield 400
    add(g.w_up, dot_tn(grad_up_ref[:main, :], st.middle[:main, :]))
    rest.middle[place, :] = st.middle[main:, :]
    rest.up[place, :] = grad_up_ref[main:, :]
    rest.active[place, :] = st.active[main:, :]
    yield 400
    normed_attn = st.normed_attn[...]
    add(g.gain_attn, column_sum(grad_middle * normed_attn))
    add(g.shift_attn, column_sum(grad_middle))
    grad_resid = norm_back(grad_middle * row(w.gain_attn), normed_attn, st.inverse[:, 0:1])
    grad_attn = grad_resid.astype(BF16)
    rest.attn[place, :] = grad_attn[main:]
    rest.context[place, :] = st.context[main:, :]
    add(g.b_out, column_sum(grad_attn))
    yield 500
    add(g.w_out, dot_tn(st.context[:main, :], grad_attn[:main]))
    scale = jnp.concatenate([jnp.broadcast_to(st.scale[h : h + 1, :], (width, main)) for h in range(HEADS)], axis=0)
    grad_context_t = (dot_nt(w.w_out[0], grad_attn[:main]) * scale).astype(BF16)
    grad_context = grad_context_t.T
    product = grad_context_t.astype(F32) * st.context_t[...]
    q, k, v = st.query[...], st.key[...], st.value[...]
    k_t = k[:main].T
    yield 400
    grad_spread = spread_heads(dot_nt(grad_attn[main:], w.w_out[0]).astype(BF16), width)
    p_rest = st.prob_rest[...]
    p_rest_wide = p_rest.astype(F32)
    grad_p = dot_nt(v, grad_spread)
    centre = jnp.sum(p_rest_wide * grad_p, axis=0, keepdims=True) / jnp.sum(p_rest_wide, axis=0, keepdims=True)
    grad_s = p_rest_wide * (grad_p - centre)
    grad_s = grad_s.astype(BF16)
    grad_v = dot(p_rest, grad_spread)
    grad_k = dot(grad_s, spread_heads(q[main:], width))
    grad_q_rest = fold_heads(dot_tn(grad_s, k), width).astype(BF16)
    yield 400
    left = lax.broadcasted_iota(jnp.int32, (full, 2 * width), 1) < width
    q_parts, k_parts, v_parts, bottoms = [], [], [], []
    for h in range(0, HEADS, 2):
        pair = slice(width * h, width * (h + 2))
        for i in (h, h + 1):
            own = slice(i * width, (i + 1) * width)
            grad_p = dot(own_half(v[:, pair], i, width), grad_context_t[pair, :])
            yield 130
            grad_s = st.prob[i].astype(F32) * (grad_p - jnp.sum(product[own, :], axis=0, keepdims=True))
            grad_s = grad_s.astype(BF16)
            grad_s_ref[i] = grad_s
            yield 140
            q_parts.append(dot(k_t[own, :], grad_s[:main]))
            bottoms.append(grad_s[main:])
            yield 130
        both = dot(st.prob[h : h + 2].reshape(2 * full, main), grad_context[:, pair])
        v_parts.append(jnp.where(left, both[:full], both[full:]))
        yield 350
        both = dot(grad_s_ref[h : h + 2].reshape(2 * full, main), q[:main, pair])
        k_parts.append(jnp.where(left, both[:full], both[full:]))
        yield 350
    grad_v = (grad_v + jnp.concatenate(v_parts, axis=1)).astype(BF16)
    grad_k = (grad_k + jnp.concatenate(k_parts, axis=1)).astype(BF16)
    grad_q_t = jnp.concatenate(q_parts, axis=0)
    grad_q_t = grad_q_t + dot_tn(spread_heads(k[main:], width), jnp.concatenate(bottoms, axis=0))
    grad_q = jnp.concatenate([grad_q_t.astype(BF16).T, grad_q_rest], axis=0) * BF16(0.125)
    rest.x[place, :] = st.x[main:, :]
    rest.query[place, :] = grad_q[main:]
    rest.key[place, :] = grad_k[main:]
    rest.value[place, :] = grad_v[main:]
    add(g.b_query, column_sum(grad_q))
    add(g.b_value, column_sum(grad_v))
    yield 400
    x_main = st.x[:main, :]
    add(g.w_query, dot_tn(x_main, grad_q[:main]))
    add(g.w_key, dot_tn(x_main, grad_k[:main]))
    add(g.w_value, dot_tn(x_main, grad_v[:main]))
    yield 400
    result.append(
        grad_resid
        + dot_nt(grad_q, w.w_query[0])
        + dot_nt(grad_k, w.w_key[0])
        + dot_nt(grad_v, w.w_value[0])
    )
    yield 300


def add_rest(g, rest):
    def add(ref, left, right):
        ref[...] += dot_tn(left[...], right[...])

    add(g.w_query, rest.x, rest.query)
    add(g.w_key, rest.x, rest.key)
    add(g.w_value, rest.x, rest.value)
    add(g.w_out, rest.context, rest.attn)
    units, features = g.w_down.shape

    @pl.loop(0, units // features)
    def _(c):
        part = pl.ds(pl.multiple_of(c * features, features), features)
        g.w_up[part, :] += dot_tn(rest.up[:, part], rest.middle[...])
        g.w_down[part, :] += dot_tn(rest.active[:, part], rest.branch[...])


FORWARD, BACKWARD = 6000, 8650


def squares(g):
    return (g.w_query, g.w_key, g.w_value, g.w_out)


def lines(g):
    return (g.b_query, g.b_value, g.b_out, g.gain_attn, g.shift_attn, g.b_down, g.gain_ffn, g.shift_ffn)


def packed_rows(features, units):
    used = 4 * features + 2 * units + len(lines(Weights(*range(len(Weights._fields))))) + units // features
    return -(-used // (PIECES * TILE)) * PIECES * TILE


def spans(sizes, rows):
    piece = rows // PIECES
    out, at = [], 0
    for index, size in enumerate(sizes):
        done = 0
        while done < size:
            take = min(size - done, piece - at % piece)
            out.append((index, done, at // piece, at % piece, take))
            done, at = done + take, at + take
    return out


def emit(g, keep, send, ordered, me):
    units, features = g.w_down.shape
    rows = ordered.shape[0]
    piece = rows // PIECES
    chunks = units // features
    arrays = squares(g) + (g.w_up, g.w_down)
    last = [ref[...] for ref in lines(g)]
    last += [g.b_up[:, c * features : (c + 1) * features] for c in range(chunks)]
    sizes = [ref.shape[0] for ref in arrays]
    left = rows - sum(sizes)
    last.append(jnp.zeros((left - len(last), features), F32))
    tail = jnp.concatenate(last, axis=0).astype(BF16)
    for index, start, which, offset, take in spans(sizes + [left], rows):
        if index < len(arrays):
            value = arrays[index][start : start + take, :].astype(BF16)
        else:
            value = tail[start : start + take]
        at = pl.multiple_of((which ^ me) * piece, TILE) + offset
        ordered[pl.ds(pl.multiple_of(at, TILE), take), :] = value
    half = rows // 2
    keep[...] = ordered[:half, :]
    send[...] = ordered[half:, :]


def stash_shapes(full, features, units):
    main = full - TILE
    square = ((full, features), BF16)
    wide = ((full, units), BF16)
    exact = ((full, features), F32)
    return Stash(
        x=square,
        query=square,
        key=square,
        value=square,
        prob=((HEADS, full, main), BF16),
        prob_rest=((full, HEADS * TILE), BF16),
        scale=((HEADS, main), F32),
        context_t=((features, main), F32),
        context=square,
        inverse=((full, 2), F32),
        normed_attn=exact,
        middle=square,
        active=wide,
        slope=wide,
        normed_ffn=exact,
    )


def scratch(micro, full, features, units):
    square, line = (features, features), (1, features)
    sums = Weights(
        w_query=square, b_query=line, w_key=square, w_value=square, b_value=line, w_out=square, b_out=line,
        gain_attn=line, shift_attn=line, w_up=(units, features), b_up=(1, units), w_down=(units, features),
        b_down=line, gain_ffn=line, shift_ffn=line,
    )
    rest = Rest(*[(micro * TILE, features)] * 8, up=(micro * TILE, units), active=(micro * TILE, units))
    out = [pltpu.VMEM(size, F32) for size in sums] + [pltpu.VMEM(size, BF16) for size in rest]
    out.append(pltpu.VMEM((full, units), BF16))
    out.append(pltpu.VMEM((HEADS, full, full - TILE), BF16))
    out.append(pltpu.VMEM((packed_rows(features, units), features), BF16))
    return out


def take_scratch(refs):
    count = len(Weights._fields)
    g, refs = Weights(*refs[:count]), refs[count:]
    count = len(Rest._fields)
    return g, Rest(*refs[:count]), *refs[count:]


def weight_specs(weights, layer):
    specs = []
    for weight in weights:
        if weight.ndim == 3:
            specs.append(pl.BlockSpec((1,) + weight.shape[1:], lambda m: (layer, 0, 0)))
        else:
            specs.append(pl.BlockSpec(weight.shape, lambda m: (0, 0)))
    return specs


def by_micro(shape):
    rank = len(shape)
    return pl.BlockSpec((1,) + tuple(shape[1:]), lambda m: (m,) + (0,) * (rank - 1))


def ahead(shape):
    rank, last = len(shape), shape[0] - 1
    return pl.BlockSpec((1,) + tuple(shape[1:]), lambda m: (jnp.minimum(m, last),) + (0,) * (rank - 1))


def behind(shape):
    rank = len(shape)
    return pl.BlockSpec((1,) + tuple(shape[1:]), lambda m: (jnp.maximum(m - 1, 0),) + (0,) * (rank - 1))


def fixed(shape):
    rank = len(shape)
    return pl.BlockSpec(tuple(shape), lambda m: (0,) * rank)


def smem():
    return pl.BlockSpec(memory_space=pltpu.SMEM)


PARAMS = pltpu.CompilerParams(vmem_limit_bytes=60 * 2**20)


def lower_forward_kernel(x_ref, *refs):
    w, refs = Weights(*refs[: len(Weights._fields)]), refs[len(Weights._fields) :]
    out_ref, sent_ref, *refs = refs
    st = Stash(*[ref.at[0] for ref in refs[:-1]])
    padded = refs[-1]
    rows = x_ref.shape[1]
    main = padded.shape[0] - TILE
    padded[main:, :] = jnp.zeros((TILE, padded.shape[1]), BF16)
    padded[:rows, :] = x_ref[0]
    result = []
    weave((layer_forward(padded[...], 0, w, st, rows, result), 1))
    y = result[0].astype(BF16)
    out_ref[0] = y
    sent_ref[0] = y[main:]


def lower_forward(hidden, weights, full):
    micro, rows, features = hidden.shape
    outs = [jax.ShapeDtypeStruct((micro, full, features), BF16), jax.ShapeDtypeStruct((micro, TILE, features), BF16)]
    shapes = stash_shapes(full, features, weights.w_up.shape[2])
    outs += [jax.ShapeDtypeStruct((micro,) + shape, kind) for shape, kind in shapes]
    out, sent, *stash = pl.pallas_call(
        lower_forward_kernel,
        grid=(micro,),
        in_specs=[by_micro(hidden.shape)] + weight_specs(weights, 0),
        out_specs=[by_micro(o.shape) for o in outs],
        out_shape=outs,
        scratch_shapes=[pltpu.VMEM((full, features), BF16)],
        compiler_params=PARAMS,
        name="lower_forward",
    )(hidden, *weights)
    return out, sent, Stash(*stash)


def zero_sums(g):
    for ref in g:
        rows, features = ref.shape
        if rows == 1:
            ref[...] = jnp.zeros_like(ref)
        else:

            @pl.loop(0, rows // STRIP)
            def _(i, ref=ref, features=features):
                ref[pl.ds(pl.multiple_of(i * STRIP, STRIP), STRIP), :] = jnp.zeros((STRIP, features), F32)


def upper_forward(rows, lead, arrived_ref, cot_ref, target_ref, slot_ref, count, x_ref, out_ref, grad_out, w, st):
    full, features = x_ref.shape[1:]
    memory = cot_ref.shape[1]
    main = full - TILE
    x = x_ref[0]
    is_read = lax.broadcasted_iota(jnp.int32, (TILE, features), 0) < memory
    moved = jnp.logical_and(is_read, jnp.logical_not(lead))
    x = jnp.concatenate([jnp.where(moved, arrived_ref[0], x[:TILE]), x[TILE:]], axis=0)
    result = []
    yield from layer_forward(x, 1, w, st, rows, result)
    y = result[0]
    out_ref[0] = y[:rows].astype(BF16)
    slots = slot_ref.shape[2]
    slot_row = lax.broadcasted_iota(jnp.int32, (main, slots), 0) - memory
    slot_at = lax.broadcasted_iota(jnp.int32, (main, slots), 1)
    hit = jnp.logical_and(slot_row == slot_ref[0], slot_at < count)
    hit = jnp.where(hit, 1.0, 0.0).astype(BF16)
    used = dot(hit, jnp.ones((slots, features), BF16))
    wanted = dot(hit, target_ref[0])
    grad_out[:main, :] = (y[:main] * used - wanted) / count.astype(F32)
    grad_out[main : main + memory, :] = cot_ref[0].astype(F32)
    yield 300


def upper_backward(lead, memory, grad_out, grad_ref, back_ref, w, st, *refs):
    result = []
    yield from layer_backward(grad_out[...], 1, w, st, *refs, result)
    grad_in = result[0]
    is_read = lax.broadcasted_iota(jnp.int32, (TILE, grad_in.shape[1]), 0) < memory
    moved = jnp.logical_and(is_read, jnp.logical_not(lead))
    back_ref[0] = grad_in[:TILE].astype(BF16)
    grad_ref[0, :TILE, :] = jnp.where(moved, 0.0, grad_in[:TILE])
    grad_ref[0, TILE:, :] = grad_in[TILE:]


def upper_kernel(rows, micro, bits, count_ref, x_ref, arrived_ref, cot_ref, target_ref, slot_ref, *refs):
    step = pl.program_id(0)
    w, refs = Weights(*refs[: len(Weights._fields)]), refs[len(Weights._fields) :]
    out_ref, grad_ref, back_ref, keep_ref, send_ref = refs[:5]
    refs = refs[5:]
    st, refs = Stash(*refs[: len(Stash._fields)]), refs[len(Stash._fields) :]
    grad_out, *refs = refs
    g, rest, grad_up_ref, grad_s_ref, ordered = take_scratch(refs)
    memory = cot_ref.shape[1]
    lead = lax.axis_index(LINE) == 0

    def turn(slot):
        twice = Stash(*[ref if ref.shape[0] != 2 else ref.at[slot] for ref in st])
        return twice

    def forward(slot):
        count = count_ref[jnp.minimum(step, micro - 1)]
        return upper_forward(
            rows, lead, arrived_ref, cot_ref, target_ref, slot_ref, count, x_ref, out_ref, grad_out, w, turn(slot)
        )

    def backward(slot):
        return upper_backward(
            lead, memory, grad_out, grad_ref, back_ref, w, turn(slot), g, rest, grad_up_ref, grad_s_ref, step - 1
        )

    @pl.when(step == 0)
    def _():
        zero_sums(g)
        grad_out[grad_out.shape[0] - TILE :, :] = jnp.zeros((TILE, grad_out.shape[1]), F32)
        weave((forward(0), FORWARD))

    @pl.when(jnp.logical_and(step > 0, step < micro))
    def _():
        slot = lax.rem(step, 2)
        weave((forward(slot), FORWARD), (backward(1 - slot), BACKWARD))

    @pl.when(step == micro)
    def _():
        weave((backward((micro - 1) % 2), BACKWARD))
        add_rest(g, rest)
        emit(g, keep_ref, send_ref, ordered, place_of(bits))


def half_packed(features, units):
    return jax.ShapeDtypeStruct((packed_rows(features, units) // 2, features), BF16)


def upper_both(bits, counts, x, arrived, cotangent, targets, slots, weights, rows):
    micro, full, features = x.shape
    units = weights.w_up.shape[2]
    outs = [
        jax.ShapeDtypeStruct((micro, rows, features), BF16),
        jax.ShapeDtypeStruct(x.shape, F32),
        jax.ShapeDtypeStruct((micro, TILE, features), BF16),
        half_packed(features, units),
        half_packed(features, units),
    ]
    ins = (x, arrived, cotangent, targets, slots)
    shapes = stash_shapes(full, features, units)
    once = (shapes.inverse, shapes.normed_attn, shapes.middle, shapes.active, shapes.slope, shapes.normed_ffn)
    stash = [pltpu.VMEM(s if (s, k) in once and (s, k) != shapes.x else (2,) + s, k) for s, k in shapes] + [pltpu.VMEM((full, features), F32)]
    return pl.pallas_call(
        functools.partial(upper_kernel, rows, micro, bits),
        grid=(micro + 1,),
        in_specs=[smem()] + [ahead(a.shape) for a in ins] + weight_specs(weights, 1),
        out_specs=[ahead(outs[0].shape), behind(outs[1].shape), behind(outs[2].shape)]
        + [fixed(o.shape) for o in outs[3:]],
        out_shape=outs,
        scratch_shapes=stash + scratch(micro, full, features, units),
        compiler_params=PARAMS,
        name="upper_both",
    )(counts, *ins, *weights)


def lower_backward_kernel(memory, bits, grad_ref, back_ref, *refs):
    step, steps = pl.program_id(0), pl.num_programs(0)
    w, refs = Weights(*refs[: len(Weights._fields)]), refs[len(Weights._fields) :]
    st, refs = Stash(*[ref.at[0] for ref in refs[: len(Stash._fields)]]), refs[len(Stash._fields) :]
    out_ref, keep_ref, send_ref, *refs = refs
    g, rest, grad_up_ref, grad_s_ref, ordered = take_scratch(refs)
    full, features = grad_ref.shape[1:]
    main = full - TILE

    @pl.when(step == 0)
    def _():
        zero_sums(g)

    is_write = lax.broadcasted_iota(jnp.int32, (TILE, features), 0) < memory
    returned = jnp.where(is_write, back_ref[0].astype(F32), 0.0)
    grad_out = jnp.concatenate([grad_ref[0, :main, :], grad_ref[0, main:, :] + returned], axis=0)
    result = []
    weave((layer_backward(grad_out, 0, w, st, g, rest, grad_up_ref, grad_s_ref, step, result), 1))
    out_ref[0] = result[0][: out_ref.shape[1]].astype(BF16)

    @pl.when(step == steps - 1)
    def _():
        add_rest(g, rest)
        emit(g, keep_ref, send_ref, ordered, place_of(bits))


def lower_backward(bits, grad, back, weights, stash, rows, memory):
    micro, full, features = grad.shape
    units = weights.w_up.shape[2]
    outs = [
        jax.ShapeDtypeStruct((micro, rows, features), BF16),
        half_packed(features, units),
        half_packed(features, units),
    ]
    return pl.pallas_call(
        functools.partial(lower_backward_kernel, memory, bits),
        grid=(micro,),
        in_specs=[by_micro(grad.shape), by_micro(back.shape)]
        + weight_specs(weights, 0)
        + [by_micro(a.shape) for a in stash],
        out_specs=[by_micro(outs[0].shape)] + [fixed(o.shape) for o in outs[1:]],
        out_shape=outs,
        scratch_shapes=scratch(micro, full, features, units),
        compiler_params=PARAMS,
        name="lower_backward",
    )(grad, back, *weights, *stash)


def unpack_kernel(place_of_layer, *refs):
    sources, refs = refs[:4], refs[4:]
    out, refs = Weights(*refs[: len(Weights._fields)]), refs[len(Weights._fields) :]
    ordered, *staged, in_sems, out_sems = refs
    features, units = out.w_up.shape[1:]
    chunks = units // features
    half = sources[0].shape[0]
    rows, piece = 2 * half, 2 * half // PIECES
    arrays = squares(out) + (out.w_up, out.w_down)
    loads = [
        pltpu.make_async_copy(source, ordered.at[i // 2, (i % 2) * half : (i % 2 + 1) * half], in_sems.at[i])
        for i, source in enumerate(sources)
    ]
    for load in loads:
        load.start()
    for load in loads:
        load.wait()
    sizes = [features] * 4 + [units, units]
    sizes.append(rows - sum(sizes))
    me = [place_of_layer(layer) for layer in range(2)]

    def store(index, layer):
        return pltpu.make_async_copy(staged[index].at[layer], arrays[index].at[layer], out_sems.at[layer, index])

    @pl.loop(0, 2)
    def _(layer):
        mine = jnp.where(layer == 0, me[0], me[1])
        for index, start, which, offset, take in spans(sizes, rows):
            at = pl.multiple_of((which ^ mine) * piece, TILE) + offset
            value = ordered[layer, pl.ds(pl.multiple_of(at, TILE), take), :]
            if index == 4:
                staged[index][layer, :, start : start + take] = value.T.astype(F32)
            elif index < 6:
                staged[index][layer, start : start + take, :] = value.astype(F32)
            else:
                value = value.astype(F32)
                names = lines(out)
                for i, ref in enumerate(names):
                    ref[pl.ds(layer, 1), :] = value[i : i + 1]
                for c in range(chunks):
                    i = len(names) + c
                    out.b_up[pl.ds(layer, 1), c * features : (c + 1) * features] = value[i : i + 1]
            if index < 6 and start + take == sizes[index]:
                store(index, layer).start()

    for layer in range(2):
        for index in range(6):
            store(index, layer).wait()


def unpack(bits, parts, weights):
    outs = [jax.ShapeDtypeStruct(weight.shape, F32) for weight in weights]
    shapes = Weights(*outs)
    large = squares(shapes) + (shapes.w_up, shapes.w_down)
    return pl.pallas_call(
        functools.partial(unpack_kernel, lambda layer: place_of(bits[layer])),
        in_specs=[pl.BlockSpec(memory_space=pl.ANY)] * 4,
        out_specs=[pl.BlockSpec(memory_space=pl.ANY if len(o.shape) == 3 else pltpu.VMEM) for o in outs],
        out_shape=outs,
        scratch_shapes=[pltpu.VMEM((2, 2 * parts[0].shape[0], parts[0].shape[1]), BF16)]
        + [pltpu.VMEM(o.shape, F32) for o in large]
        + [pltpu.SemaphoreType.DMA((4,)), pltpu.SemaphoreType.DMA((2, 6))],
        compiler_params=pltpu.CompilerParams(vmem_limit_bytes=20 * 2**20),
        name="unpack",
    )(*parts)


def from_behind(value, axis, steps):
    count = lax.axis_size(axis)
    initial, last = (max(0, -steps), min(count, count - steps))
    return lax.ppermute(value, axis, [(source, source + steps) for source in range(initial, last)])


def swap(value, bit):
    axis, step = bit
    return lax.ppermute(value, axis, [(i, i ^ step) for i in range(lax.axis_size(axis))])


def plus(a, b):
    return (a.astype(F32) + b.astype(F32)).astype(BF16)


def place_of(bits):
    me = jnp.int32(0)
    for axis, step in bits:
        me = me * 2 + lax.rem(lax.div(lax.axis_index(axis), step), 2)
    return me


def sum_rest(value, bits):
    axis, step = bits[0]
    me = (lax.axis_index(axis) // step) % 4

    def across(part, k):
        return lax.ppermute(part, axis, [(i, i ^ (k * step)) for i in range(lax.axis_size(axis))])

    rows = value.shape[0] // 4
    quarter = [lax.dynamic_slice_in_dim(value, (me ^ k) * rows, rows) for k in range(4)]
    got = [across(quarter[k], k) for k in (1, 2, 3)]
    kept = quarter[0].astype(F32)
    for part in got:
        kept = kept + part.astype(F32)
    kept = kept.astype(BF16)
    for bit in bits[2:]:
        kept = plus(kept, swap(kept, bit))
    a, b, c, d = [kept] + [across(kept, k) for k in (1, 2, 3)]
    odd, high = me % 2 == 1, me >= 2
    first, second = jnp.where(odd, b, a), jnp.where(odd, a, b)
    third, fourth = jnp.where(odd, d, c), jnp.where(odd, c, d)
    lower, upper = jnp.concatenate([first, second], axis=0), jnp.concatenate([third, fourth], axis=0)
    return jnp.where(high, jnp.concatenate([upper, lower], axis=0), jnp.concatenate([lower, upper], axis=0))


def sum_all(lower, upper, lower_bits, upper_bits, rest_bits, others):
    chains = []
    for (keep, send), bits in ((lower, lower_bits), (upper, upper_bits)):
        chains.append((plus(keep, swap(send, bits[0])), bits))
    for level in (1, 2):
        sent = [swap(kept[kept.shape[0] // 2 :], bits[level]) for kept, bits in chains]
        chains = [(plus(kept[: kept.shape[0] // 2], got), bits) for got, (kept, bits) in zip(sent, chains)]
        if level == 1:
            others = [with_layout_constraint(jnp.transpose(v, (1, 0, 2)), Layout((0, 1, 2))) for v in others]
            others, tied = lax.optimization_barrier((others, [kept for kept, _ in chains]))
            chains = [(kept, bits) for kept, (_, bits) in zip(tied, chains)]
    size = chains[0][0].shape[0]
    both = sum_rest(jnp.concatenate([kept for kept, _ in chains], axis=0), rest_bits)
    chains = [(both[:size], lower_bits), (both[size:], upper_bits)]
    for level in (2, 1):
        sent = [swap(kept, bits[level]) for kept, bits in chains]
        chains = [(jnp.concatenate([kept, got], axis=0), bits) for got, (kept, bits) in zip(sent, chains)]
    out = []
    for kept, bits in chains:
        out += [kept, swap(kept, bits[0])]
    return out, others


def local(hidden, write_cotangent, targets, positions, counts, *weights):
    weights = Weights(*weights)
    micro, _, _, rows, features = hidden.shape
    memory = write_cotangent.shape[3]
    full = -(-rows // TILE) * TILE
    bits = [(axis, 1 << i) for axis in (LINE, PAIR) for i in range(lax.axis_size(axis).bit_length() - 1)]
    core, along, across = (LINE, 1), (LINE, 2), (PAIR, 1)
    lower_bits, upper_bits = (core, across, along), (core, along, across)
    rest_bits = [bit for bit in bits if bit not in lower_bits]

    hidden_rows = hidden.reshape(micro, rows, features)
    lower_out, sent, stash = lower_forward(hidden_rows, weights, full)
    arrived = from_behind(sent, LINE, 1)
    out, grad, back, *upper = upper_both(
        upper_bits,
        counts.reshape(micro),
        lower_out,
        arrived,
        write_cotangent.reshape(micro, memory, features),
        targets.reshape(micro, targets.shape[3], features),
        positions.reshape(micro, 1, positions.shape[3]),
        weights,
        rows,
    )
    returned = from_behind(back, LINE, -1)
    grad_in, *lower = lower_backward(lower_bits, grad, returned, weights, stash, rows, memory)
    parts, (out, grad_in) = sum_all(lower, upper, lower_bits, upper_bits, rest_bits, (out, grad_in))
    grads = unpack((lower_bits, upper_bits), parts, weights)
    out, grad_in = (jnp.transpose(v, (1, 0, 2)).reshape(hidden.shape) for v in (out, grad_in))
    return (out, grad_in) + tuple(grads)


def solution(mesh):
    split = P(None, PAIR, LINE, None, None)
    placed = (split, split, split, P(None, PAIR, LINE, None), P(None, PAIR, LINE))
    count = len(Weights._fields)
    return jax.shard_map(
        local,
        mesh=mesh,
        in_specs=placed + (P(),) * count,
        out_specs=(split, split) + (P(),) * count,
        check_vma=False,
    )
```

```python
import functools
from typing import Any, NamedTuple

import jax
import jax.numpy as jnp
from jax import lax
from jax.experimental import pallas as pl
from jax.experimental.layout import Layout, with_layout_constraint
from jax.experimental.pallas import tpu as pltpu
from jax.sharding import PartitionSpec as P

EPSILON = 1e-12
DENSITY = 0.3989422804014327
ROOT_HALF = 0.7071067811865476
BELL = -0.7213475204444817
HEADS = 4
TILE = 16
STRIP = 64
PIECES = 8
LOW = -1e30
F32, BF16 = jnp.float32, jnp.bfloat16
LINE, PAIR = "seg", "item"


class Weights(NamedTuple):
    w_query: Any
    b_query: Any
    w_key: Any
    w_value: Any
    b_value: Any
    w_out: Any
    b_out: Any
    gain_attn: Any
    shift_attn: Any
    w_up: Any
    b_up: Any
    w_down: Any
    b_down: Any
    gain_ffn: Any
    shift_ffn: Any


class Stash(NamedTuple):
    x: Any
    query: Any
    key: Any
    value: Any
    prob: Any
    prob_rest: Any
    scale: Any
    context_t: Any
    context: Any
    inverse: Any
    normed_attn: Any
    middle: Any
    active: Any
    slope: Any
    normed_ffn: Any


class Rest(NamedTuple):
    x: Any
    query: Any
    key: Any
    value: Any
    context: Any
    attn: Any
    middle: Any
    branch: Any
    up: Any
    active: Any


def dot(a, b):
    return jnp.dot(a, b, preferred_element_type=F32)


def dot_nt(a, b):
    return lax.dot_general(a, b, (((1,), (1,)), ((), ())), preferred_element_type=F32)


def dot_tn(a, b):
    return lax.dot_general(a, b, (((0,), (0,)), ((), ())), preferred_element_type=F32)


def mean(v):
    return jnp.mean(v, axis=-1, keepdims=True)


def column_sum(v):
    return jnp.sum(v.astype(F32), axis=0, keepdims=True)


def normalize(v):
    centred = v - mean(v)
    inverse = lax.rsqrt(mean(centred * centred) + EPSILON)
    return centred * inverse, inverse


def norm_back(grad, normed, inverse):
    return inverse * (grad - mean(grad) - normed * mean(grad * normed))


def head_block(shape, width):
    rows = lax.div(lax.broadcasted_iota(jnp.int32, shape, 0), TILE)
    lanes = lax.div(lax.broadcasted_iota(jnp.int32, shape, 1), width)
    return rows == lanes


def spread_heads(rest, width):
    tiled = jnp.concatenate([rest] * HEADS, axis=0)
    return jnp.where(head_block(tiled.shape, width), tiled, jnp.zeros_like(tiled))


def fold_heads(spread, width):
    own = jnp.where(head_block(spread.shape, width), spread, 0.0)
    return own[:TILE] + own[TILE : 2 * TILE] + own[2 * TILE : 3 * TILE] + own[3 * TILE :]


def own_half(pair, h, width):
    lanes = lax.div(lax.broadcasted_iota(jnp.int32, pair.shape, 1), width)
    return jnp.where(lanes == h % 2, pair, jnp.zeros_like(pair))


def weigh_keys(s, live_rest):
    main = s.shape[0] - TILE
    top, bottom = s[:main], jnp.where(live_rest, s[main:], LOW)
    peak = jnp.maximum(jnp.max(top, axis=0, keepdims=True), jnp.max(bottom, axis=0, keepdims=True))
    yield 120
    top = jnp.exp(top - peak).astype(BF16)
    yield 220
    return top, jnp.exp(bottom - peak).astype(BF16)


def woven(*tasks):
    tasks = [[task, 0.0, total] for task, total in tasks]
    while tasks:
        task = min(tasks, key=lambda t: t[1] / t[2])
        length = next(task[0], None)
        if length is None:
            tasks.remove(task)
        else:
            task[1] += length
            yield length


def weave(*tasks):
    for _ in woven(*tasks):
        pass


def at(w, layer):
    return layer if w.w_query.shape[0] > 1 else 0


def layer_forward(x, layer, w, st, rows, result):
    full, features = x.shape
    main = full - TILE
    width = features // HEADS

    def row(ref):
        return ref[layer : layer + 1, :]

    st.x[...] = x
    q = ((dot(x, w.w_query[at(w, layer)]) + row(w.b_query)) * 0.125).astype(BF16)
    yield 150
    k = dot(x, w.w_key[at(w, layer)]).astype(BF16)
    yield 150
    v = (dot(x, w.w_value[at(w, layer)]) + row(w.b_value)).astype(BF16)
    st.query[...] = q
    st.key[...] = k
    st.value[...] = v
    yield 150
    q_t = q[:main].T
    v_t = v[:main].T
    live_rest = lax.broadcasted_iota(jnp.int32, (TILE, 1), 0) < rows - main
    def last_rows(out):
        top, bottom = yield from weigh_keys(dot_nt(k, spread_heads(q[main:], width)), live_rest)
        p_rest = jnp.concatenate([top, bottom], axis=0)
        p_rest = (p_rest.astype(F32) * (1.0 / column_sum(p_rest))).astype(BF16)
        st.prob_rest[...] = p_rest
        yield 50
        out.append(fold_heads(dot_tn(p_rest, v), width).astype(BF16))
        yield 50

    ones = jnp.ones((TILE, main), BF16)
    scores, weights, parts, bottoms, scales = {}, {}, [], [], []

    def first_rows():
        for h in range(-1, HEADS + 1):
            if h + 1 < HEADS:
                pair = slice(2 * width * ((h + 1) // 2), 2 * width * ((h + 1) // 2 + 1))
                scores[h + 1] = dot(own_half(k[:, pair], h + 1, width), q_t[pair, :])
                yield 80
            if h > 0:
                top, bottom = weights.pop(h - 1)
                part = dot(jnp.concatenate([v_t[(h - 1) * width : h * width, :], ones], axis=0), top)
                parts.append(part[:width])
                bottoms.append(bottom)
                scale = 1.0 / (part[width : width + 1] + column_sum(bottom))
                st.scale[h - 1 : h, :] = scale
                scales.append(jnp.broadcast_to(scale, (width, main)))
                yield 80
            if 0 <= h < HEADS:
                top, bottom = yield from weigh_keys(scores.pop(h), live_rest)
                st.prob[h, :main, :] = top
                st.prob[h, main:, :] = bottom
                weights[h] = top, bottom
                yield 60

    at_last = []
    yield from woven((last_rows(at_last), 450), (first_rows(), 2600))
    (context_rest,) = at_last
    context_t = jnp.concatenate(parts, axis=0)
    context_t = context_t + dot_tn(spread_heads(v[main:], width), jnp.concatenate(bottoms, axis=0))
    context_t = context_t * jnp.concatenate(scales, axis=0)
    st.context_t[...] = context_t
    context = jnp.concatenate([context_t.astype(BF16).T, context_rest], axis=0)
    st.context[...] = context
    yield 200
    normed_attn, inverse_attn = normalize(x.astype(F32) + dot(context, w.w_out[at(w, layer)]) + row(w.b_out))
    st.normed_attn[...] = normed_attn
    middle = normed_attn * row(w.gain_attn) + row(w.shift_attn)
    middle_low = middle.astype(BF16)
    st.middle[...] = middle_low
    total = middle + row(w.b_down)
    yield 400
    chunks = w.w_up.shape[2] // features

    def upward(c):
        part = slice(c * features, (c + 1) * features)
        return dot(middle_low, w.w_up[at(w, layer), :, part]) + w.b_up[layer : layer + 1, part]

    ahead = upward(0)
    for c in range(chunks):
        part = slice(c * features, (c + 1) * features)
        u, ahead = ahead, (upward(c + 1) if c + 1 < chunks else None)
        yield 50
        phi = 0.5 + 0.5 * lax.erf(u * ROOT_HALF)
        active = (u * phi).astype(BF16)
        st.active[:, part] = active
        yield 200
        slope = phi + u * (jnp.exp2(u * u * BELL) * DENSITY)
        st.slope[:, part] = slope.astype(BF16)
        yield 220
        total = total + dot(active, w.w_down[at(w, layer), part, :])
        yield 80
    normed_ffn, inverse_ffn = normalize(total)
    st.normed_ffn[...] = normed_ffn
    st.inverse[:, 0:1] = inverse_attn
    st.inverse[:, 1:2] = inverse_ffn
    result.append(normed_ffn * row(w.gain_ffn) + row(w.shift_ffn))
    yield 400


def layer_backward(grad_out, layer, w, st, g, rest, grad_up_ref, grad_s_ref, step, result, fill=False):
    full, features = st.x.shape
    main = full - TILE
    width = features // HEADS
    place = pl.ds(pl.multiple_of(step * TILE, TILE), TILE)

    def row(ref):
        return ref[layer : layer + 1, :]

    def add(ref, value):
        ref[...] += value

    normed_ffn = st.normed_ffn[...]
    add(g.gain_ffn, column_sum(grad_out * normed_ffn))
    add(g.shift_ffn, column_sum(grad_out))
    grad_sum = norm_back(grad_out * row(w.gain_ffn), normed_ffn, st.inverse[:, 1:2])
    grad_branch = grad_sum.astype(BF16)
    rest.branch[place, :] = grad_branch[main:]
    add(g.b_down, column_sum(grad_branch))
    grad_middle = grad_sum
    yield 500
    for c in range(w.w_up.shape[2] // features):
        part = slice(c * features, (c + 1) * features)
        grad_up = dot_nt(grad_branch, w.w_down[at(w, layer), part, :]) * st.slope[:, part].astype(F32)
        grad_up = grad_up.astype(BF16)
        yield 150
        grad_up_ref[:, part] = grad_up
        g.b_up[:, part] += column_sum(grad_up)
        grad_middle = grad_middle + dot_nt(grad_up, w.w_up[at(w, layer), :, part])
        yield 150
    rest.middle[place, :] = st.middle[main:, :]
    rest.up[place, :] = grad_up_ref[main:, :]
    rest.active[place, :] = st.active[main:, :]
    rest.context[place, :] = st.context[main:, :]

    def grad_ffn(cuts):
        for cut in range(cuts):
            part = slice(cut * units // cuts, (cut + 1) * units // cuts)
            g.w_down[part, :] += dot_tn(st.active[:main, part], grad_branch[:main])
            yield 360 // cuts
            g.w_up[part, :] += dot_tn(grad_up_ref[:main, part], st.middle[:main, :])
            yield 360 // cuts

    units = w.w_up.shape[2]
    filler = grad_ffn(2 if fill else 1)
    if not fill:
        yield from filler
    normed_attn = st.normed_attn[...]
    yield next(filler, 0)
    add(g.gain_attn, column_sum(grad_middle * normed_attn))
    add(g.shift_attn, column_sum(grad_middle))
    if fill:
        yield 100
        yield next(filler, 0)
    grad_normed = grad_middle * row(w.gain_attn)
    mean_grad, mean_both = mean(grad_normed), mean(grad_normed * normed_attn)
    if fill:
        yield 150
        yield next(filler, 0)
    grad_resid = st.inverse[:, 0:1] * (grad_normed - mean_grad - normed_attn * mean_both)
    grad_attn = grad_resid.astype(BF16)
    if fill:
        yield 150
    yield from filler
    rest.attn[place, :] = grad_attn[main:]
    add(g.b_out, column_sum(grad_attn))
    yield 50
    add(g.w_out, dot_tn(st.context[:main, :], grad_attn[:main]))
    scale = jnp.concatenate([jnp.broadcast_to(st.scale[h : h + 1, :], (width, main)) for h in range(HEADS)], axis=0)
    grad_context_t = (dot_nt(w.w_out[at(w, layer)], grad_attn[:main]) * scale).astype(BF16)
    grad_context = grad_context_t.T
    product = grad_context_t.astype(F32) * st.context_t[...]
    q, k, v = st.query[...], st.key[...], st.value[...]
    k_t = k[:main].T
    yield 400
    def last_rows(out):
        grad_spread = spread_heads(dot_nt(grad_attn[main:], w.w_out[at(w, layer)]).astype(BF16), width)
        p_rest = st.prob_rest[...]
        p_rest_wide = p_rest.astype(F32)
        yield 60
        grad_p = dot_nt(v, grad_spread)
        out.append(dot(p_rest, grad_spread))
        yield 100
        centre = jnp.sum(p_rest_wide * grad_p, axis=0, keepdims=True) / jnp.sum(p_rest_wide, axis=0, keepdims=True)
        yield 100
        grad_s = (p_rest_wide * (grad_p - centre)).astype(BF16)
        yield 60
        out.append(dot(grad_s, spread_heads(q[main:], width)))
        yield 60
        out.append(fold_heads(dot_tn(grad_s, k), width).astype(BF16))
        yield 60

    left = lax.broadcasted_iota(jnp.int32, (full, 2 * width), 1) < width
    q_parts, k_parts, v_parts, bottoms = [], [], [], []

    def first_rows():
        for h in range(0, HEADS, 2):
            pair = slice(width * h, width * (h + 2))
            for i in (h, h + 1):
                own = slice(i * width, (i + 1) * width)
                grad_p = dot(own_half(v[:, pair], i, width), grad_context_t[pair, :])
                yield 130
                grad_s = st.prob[i].astype(F32) * (grad_p - jnp.sum(product[own, :], axis=0, keepdims=True))
                grad_s = grad_s.astype(BF16)
                grad_s_ref[i] = grad_s
                yield 140
                q_parts.append(dot(k_t[own, :], grad_s[:main]))
                bottoms.append(grad_s[main:])
                yield 130
            both = dot(st.prob[h : h + 2].reshape(2 * full, main), grad_context[:, pair])
            v_parts.append(jnp.where(left, both[:full], both[full:]))
            yield 350
            both = dot(grad_s_ref[h : h + 2].reshape(2 * full, main), q[:main, pair])
            k_parts.append(jnp.where(left, both[:full], both[full:]))
            yield 350

    at_last = []
    yield from woven((last_rows(at_last), 500), (first_rows(), 3000))
    grad_v, grad_k, grad_q_rest = at_last
    grad_v = (grad_v + jnp.concatenate(v_parts, axis=1)).astype(BF16)
    grad_k = (grad_k + jnp.concatenate(k_parts, axis=1)).astype(BF16)
    grad_q_t = jnp.concatenate(q_parts, axis=0)
    grad_q_t = grad_q_t + dot_tn(spread_heads(k[main:], width), jnp.concatenate(bottoms, axis=0))
    grad_q = jnp.concatenate([grad_q_t.astype(BF16).T, grad_q_rest], axis=0) * BF16(0.125)
    rest.x[place, :] = st.x[main:, :]
    rest.query[place, :] = grad_q[main:]
    rest.key[place, :] = grad_k[main:]
    rest.value[place, :] = grad_v[main:]
    add(g.b_query, column_sum(grad_q))
    add(g.b_value, column_sum(grad_v))
    yield 400
    x_main = st.x[:main, :]
    add(g.w_query, dot_tn(x_main, grad_q[:main]))
    add(g.w_key, dot_tn(x_main, grad_k[:main]))
    add(g.w_value, dot_tn(x_main, grad_v[:main]))
    yield 400
    result.append(
        grad_resid
        + dot_nt(grad_q, w.w_query[at(w, layer)])
        + dot_nt(grad_k, w.w_key[at(w, layer)])
        + dot_nt(grad_v, w.w_value[at(w, layer)])
    )
    yield 300


def add_rest(g, rest):
    def add(ref, left, right):
        ref[...] += dot_tn(left[...], right[...])

    add(g.w_query, rest.x, rest.query)
    add(g.w_key, rest.x, rest.key)
    add(g.w_value, rest.x, rest.value)
    add(g.w_out, rest.context, rest.attn)
    units, features = g.w_down.shape

    @pl.loop(0, units // features)
    def _(c):
        part = pl.ds(pl.multiple_of(c * features, features), features)
        g.w_up[part, :] += dot_tn(rest.up[:, part], rest.middle[...])
        g.w_down[part, :] += dot_tn(rest.active[:, part], rest.branch[...])


FORWARD, BACKWARD = 7600, 8650


def squares(g):
    return (g.w_query, g.w_key, g.w_value, g.w_out)


def lines(g):
    return (g.b_query, g.b_value, g.b_out, g.gain_attn, g.shift_attn, g.b_down, g.gain_ffn, g.shift_ffn)


def packed_rows(features, units):
    used = 4 * features + 2 * units + len(lines(Weights(*range(len(Weights._fields))))) + units // features
    return -(-used // (PIECES * TILE)) * PIECES * TILE


def spans(sizes, rows):
    piece = rows // PIECES
    out, at = [], 0
    for index, size in enumerate(sizes):
        done = 0
        while done < size:
            take = min(size - done, piece - at % piece)
            out.append((index, done, at // piece, at % piece, take))
            done, at = done + take, at + take
    return out


def emit(g, keep, send, ordered, me):
    units, features = g.w_down.shape
    rows = ordered.shape[0]
    piece = rows // PIECES
    chunks = units // features
    arrays = squares(g) + (g.w_up, g.w_down)
    last = [ref[...] for ref in lines(g)]
    last += [g.b_up[:, c * features : (c + 1) * features] for c in range(chunks)]
    sizes = [ref.shape[0] for ref in arrays]
    left = rows - sum(sizes)
    last.append(jnp.zeros((left - len(last), features), F32))
    tail = jnp.concatenate(last, axis=0).astype(BF16)
    for index, start, which, offset, take in spans(sizes + [left], rows):
        if index < len(arrays):
            value = arrays[index][start : start + take, :].astype(BF16)
        else:
            value = tail[start : start + take]
        at = pl.multiple_of((which ^ me) * piece, TILE) + offset
        ordered[pl.ds(pl.multiple_of(at, TILE), take), :] = value
    half = rows // 2
    keep[...] = ordered[:half, :]
    send[...] = ordered[half:, :]


def stash_shapes(full, features, units):
    main = full - TILE
    square = ((full, features), BF16)
    wide = ((full, units), BF16)
    exact = ((full, features), F32)
    return Stash(
        x=square,
        query=square,
        key=square,
        value=square,
        prob=((HEADS, full, main), BF16),
        prob_rest=((full, HEADS * TILE), BF16),
        scale=((HEADS, main), F32),
        context_t=((features, main), F32),
        context=square,
        inverse=((full, 2), F32),
        normed_attn=exact,
        middle=square,
        active=wide,
        slope=wide,
        normed_ffn=exact,
    )


def scratch(micro, full, features, units):
    square, line = (features, features), (1, features)
    sums = Weights(
        w_query=square, b_query=line, w_key=square, w_value=square, b_value=line, w_out=square, b_out=line,
        gain_attn=line, shift_attn=line, w_up=(units, features), b_up=(1, units), w_down=(units, features),
        b_down=line, gain_ffn=line, shift_ffn=line,
    )
    rest = Rest(*[(micro * TILE, features)] * 8, up=(micro * TILE, units), active=(micro * TILE, units))
    out = [pltpu.VMEM(size, F32) for size in sums] + [pltpu.VMEM(size, BF16) for size in rest]
    out.append(pltpu.VMEM((full, units), BF16))
    out.append(pltpu.VMEM((HEADS, full, full - TILE), BF16))
    out.append(pltpu.VMEM((packed_rows(features, units), features), BF16))
    return out


def take_scratch(refs):
    count = len(Weights._fields)
    g, refs = Weights(*refs[:count]), refs[count:]
    count = len(Rest._fields)
    return g, Rest(*refs[:count]), *refs[count:]


def weight_specs(weights, layer=None):
    specs = []
    for weight in weights:
        if layer is None:
            specs.append(whole())
        elif weight.ndim == 3:
            specs.append(pl.BlockSpec((1,) + weight.shape[1:], lambda m: (layer, 0, 0)))
        else:
            specs.append(pl.BlockSpec(weight.shape, lambda m: (0, 0)))
    return specs


def by_micro(shape):
    rank = len(shape)
    return pl.BlockSpec((1,) + tuple(shape[1:]), lambda m: (m,) + (0,) * (rank - 1))


def ahead(shape):
    rank, last = len(shape), shape[0] - 1
    return pl.BlockSpec((1,) + tuple(shape[1:]), lambda m: (jnp.minimum(m, last),) + (0,) * (rank - 1))


def behind(shape):
    rank = len(shape)
    return pl.BlockSpec((1,) + tuple(shape[1:]), lambda m: (jnp.maximum(m - 1, 0),) + (0,) * (rank - 1))


def fixed(shape):
    rank = len(shape)
    return pl.BlockSpec(tuple(shape), lambda m: (0,) * rank)


def whole():
    return pl.BlockSpec(memory_space=pltpu.VMEM)


def smem():
    return pl.BlockSpec(memory_space=pltpu.SMEM)


def lower_forward_kernel(x_ref, *refs):
    w, refs = Weights(*refs[: len(Weights._fields)]), refs[len(Weights._fields) :]
    out_ref, sent_ref, *refs = refs
    st = Stash(*[ref.at[0] for ref in refs[:-1]])
    padded = refs[-1]
    rows = x_ref.shape[1]
    main = padded.shape[0] - TILE
    padded[main:, :] = jnp.zeros((TILE, padded.shape[1]), BF16)
    padded[:rows, :] = x_ref[0]
    result = []
    weave((layer_forward(padded[...], 0, w, st, rows, result), 1))
    y = result[0].astype(BF16)
    out_ref[0] = y
    sent_ref[0] = y[main:]


def lower_forward(hidden, weights, full):
    micro, rows, features = hidden.shape
    outs = [jax.ShapeDtypeStruct((micro, full, features), BF16), jax.ShapeDtypeStruct((micro, TILE, features), BF16)]
    shapes = stash_shapes(full, features, weights.w_up.shape[2])
    outs += [jax.ShapeDtypeStruct((micro,) + shape, kind) for shape, kind in shapes]
    out, sent, *stash = pl.pallas_call(
        lower_forward_kernel,
        grid=(micro,),
        in_specs=[by_micro(hidden.shape)] + weight_specs(weights, 0),
        out_specs=[by_micro(o.shape) for o in outs],
        out_shape=outs,
        scratch_shapes=[pltpu.VMEM((full, features), BF16)],
        compiler_params=pltpu.CompilerParams(vmem_limit_bytes=60 * 2**20),
        name="lower_forward",
    )(hidden, *weights)
    return out, sent, Stash(*stash)


def zero_sums(g):
    for ref in g:
        rows, features = ref.shape
        if rows == 1:
            ref[...] = jnp.zeros_like(ref)
        else:

            @pl.loop(0, rows // STRIP)
            def _(i, ref=ref, features=features):
                ref[pl.ds(pl.multiple_of(i * STRIP, STRIP), STRIP), :] = jnp.zeros((STRIP, features), F32)


def upper_forward(rows, lead, arrived, cot_ref, target_ref, slot_ref, count, x_ref, out_ref, grad_out, w, st):
    full, features = x_ref.shape[1:]
    memory = cot_ref.shape[1]
    main = full - TILE
    x = x_ref[0]
    is_read = lax.broadcasted_iota(jnp.int32, (TILE, features), 0) < memory
    moved = jnp.logical_and(is_read, jnp.logical_not(lead))
    x = jnp.concatenate([jnp.where(moved, arrived, x[:TILE]), x[TILE:]], axis=0)
    result = []
    yield from layer_forward(x, 1, w, st, rows, result)
    y = result[0]
    out_ref[0] = y[:rows].astype(BF16)
    slots = slot_ref.shape[2]
    slot_row = lax.broadcasted_iota(jnp.int32, (main, slots), 0) - memory
    slot_at = lax.broadcasted_iota(jnp.int32, (main, slots), 1)
    hit = jnp.logical_and(slot_row == slot_ref[0], slot_at < count)
    hit = jnp.where(hit, 1.0, 0.0).astype(BF16)
    used = dot(hit, jnp.ones((slots, features), BF16))
    wanted = dot(hit, target_ref[0])
    grad_out[:main, :] = (y[:main] * used - wanted) / count.astype(F32)
    grad_out[main : main + memory, :] = cot_ref[0].astype(F32)
    yield 300


def upper_backward(lead, memory, grad_out, grad_ref, back_ref, w, st, *refs, fill):
    result = []
    yield from layer_backward(grad_out[...], 1, w, st, *refs, result, fill)
    grad_in = result[0]
    is_read = lax.broadcasted_iota(jnp.int32, (TILE, grad_in.shape[1]), 0) < memory
    moved = jnp.logical_and(is_read, jnp.logical_not(lead))
    back_ref[0] = grad_in[:TILE].astype(BF16)
    grad_ref[0, :TILE, :] = jnp.where(moved, 0.0, grad_in[:TILE])
    grad_ref[0, TILE:, :] = grad_in[TILE:]


def upper_kernel(rows, micro, bits, count_ref, x_ref, arrived_ref, cot_ref, target_ref, slot_ref, *refs):
    step = pl.program_id(0)
    w, refs = Weights(*refs[: len(Weights._fields)]), refs[len(Weights._fields) :]
    out_ref, grad_ref, back_ref, keep_ref, send_ref = refs[:5]
    refs = refs[5:]
    st, refs = Stash(*refs[: len(Stash._fields)]), refs[len(Stash._fields) :]
    grad_out, *refs = refs
    g, rest, grad_up_ref, grad_s_ref, ordered = take_scratch(refs)
    memory = cot_ref.shape[1]
    lead = lax.axis_index(LINE) == 0

    def turn(slot):
        twice = Stash(*[ref if ref.shape[0] != 2 else ref.at[slot] for ref in st])
        return twice

    def forward(slot):
        now = jnp.minimum(step, micro - 1)
        count, arrived = count_ref[now], arrived_ref[now]
        return upper_forward(
            rows, lead, arrived, cot_ref, target_ref, slot_ref, count, x_ref, out_ref, grad_out, w, turn(slot)
        )

    def backward(slot, fill):
        refs = (g, rest, grad_up_ref, grad_s_ref, step - 1)
        return upper_backward(lead, memory, grad_out, grad_ref, back_ref, w, turn(slot), *refs, fill=fill)

    @pl.when(step == 0)
    def _():
        zero_sums(g)
        grad_out[grad_out.shape[0] - TILE :, :] = jnp.zeros((TILE, grad_out.shape[1]), F32)
        weave((forward(0), FORWARD))

    @pl.when(jnp.logical_and(step > 0, step < micro))
    def _():
        slot = lax.rem(step, 2)
        weave((forward(slot), FORWARD), (backward(1 - slot, True), BACKWARD))

    @pl.when(step == micro)
    def _():
        weave((backward((micro - 1) % 2, False), BACKWARD))
        add_rest(g, rest)
        emit(g, keep_ref, send_ref, ordered, place_of(bits))


def half_packed(features, units):
    return jax.ShapeDtypeStruct((packed_rows(features, units) // 2, features), BF16)


def upper_both(bits, counts, x, arrived, cotangent, targets, slots, weights, rows):
    micro, full, features = x.shape
    units = weights.w_up.shape[2]
    outs = [
        jax.ShapeDtypeStruct((micro, rows, features), BF16),
        jax.ShapeDtypeStruct(x.shape, F32),
        jax.ShapeDtypeStruct((micro, TILE, features), BF16),
        half_packed(features, units),
        half_packed(features, units),
    ]
    ins = (x, arrived, cotangent, targets, slots)
    shapes = stash_shapes(full, features, units)
    once = (shapes.inverse, shapes.normed_attn, shapes.middle, shapes.active, shapes.slope, shapes.normed_ffn)
    stash = [pltpu.VMEM(s if (s, k) in once and (s, k) != shapes.x else (2,) + s, k) for s, k in shapes] + [pltpu.VMEM((full, features), F32)]
    return pl.pallas_call(
        functools.partial(upper_kernel, rows, micro, bits),
        grid=(micro + 1,),
        in_specs=[smem()] + [whole() if a is arrived else ahead(a.shape) for a in ins] + weight_specs(weights),
        out_specs=[ahead(outs[0].shape), behind(outs[1].shape), behind(outs[2].shape)]
        + [fixed(o.shape) for o in outs[3:]],
        out_shape=outs,
        scratch_shapes=stash + scratch(micro, full, features, units),
        compiler_params=pltpu.CompilerParams(vmem_limit_bytes=48 * 2**20),
        name="upper_both",
    )(counts, *ins, *weights)


def lower_backward_kernel(memory, bits, grad_ref, back_ref, *refs):
    step, steps = pl.program_id(0), pl.num_programs(0)
    w, refs = Weights(*refs[: len(Weights._fields)]), refs[len(Weights._fields) :]
    st, refs = Stash(*[ref.at[0] for ref in refs[: len(Stash._fields)]]), refs[len(Stash._fields) :]
    out_ref, keep_ref, send_ref, *refs = refs
    g, rest, grad_up_ref, grad_s_ref, ordered = take_scratch(refs)
    full, features = grad_ref.shape[1:]
    main = full - TILE

    @pl.when(step == 0)
    def _():
        zero_sums(g)

    is_write = lax.broadcasted_iota(jnp.int32, (TILE, features), 0) < memory
    returned = jnp.where(is_write, back_ref[step].astype(F32), 0.0)
    grad_out = jnp.concatenate([grad_ref[0, :main, :], grad_ref[0, main:, :] + returned], axis=0)
    result = []
    weave((layer_backward(grad_out, 0, w, st, g, rest, grad_up_ref, grad_s_ref, step, result), 1))
    out_ref[0] = result[0][: out_ref.shape[1]].astype(BF16)

    @pl.when(step == steps - 1)
    def _():
        add_rest(g, rest)
        emit(g, keep_ref, send_ref, ordered, place_of(bits))


def lower_backward(bits, grad, back, weights, stash, rows, memory):
    micro, full, features = grad.shape
    units = weights.w_up.shape[2]
    outs = [
        jax.ShapeDtypeStruct((micro, rows, features), BF16),
        half_packed(features, units),
        half_packed(features, units),
    ]
    return pl.pallas_call(
        functools.partial(lower_backward_kernel, memory, bits),
        grid=(micro,),
        in_specs=[by_micro(grad.shape), whole()]
        + weight_specs(weights)
        + [by_micro(a.shape) for a in stash],
        out_specs=[by_micro(outs[0].shape)] + [fixed(o.shape) for o in outs[1:]],
        out_shape=outs,
        scratch_shapes=scratch(micro, full, features, units),
        compiler_params=pltpu.CompilerParams(vmem_limit_bytes=48 * 2**20),
        name="lower_backward",
    )(grad, back, *weights, *stash)


def unpack_kernel(place_of_layer, *refs):
    sources, refs = refs[:4], refs[4:]
    out, refs = Weights(*refs[: len(Weights._fields)]), refs[len(Weights._fields) :]
    ordered, *staged, in_sems, out_sems = refs
    features, units = out.w_up.shape[1:]
    chunks = units // features
    half = sources[0].shape[0]
    rows, piece = 2 * half, 2 * half // PIECES
    arrays = squares(out) + (out.w_up, out.w_down)
    loads = [
        pltpu.make_async_copy(source, ordered.at[i // 2, (i % 2) * half : (i % 2 + 1) * half], in_sems.at[i])
        for i, source in enumerate(sources)
    ]
    for load in loads:
        load.start()
    sizes = [features] * 4 + [units, units]
    sizes.append(rows - sum(sizes))
    me = [place_of_layer(layer) for layer in range(2)]

    def store(index, layer):
        return pltpu.make_async_copy(staged[index].at[layer], arrays[index].at[layer], out_sems.at[layer, index])

    @pl.loop(0, 2)
    def _(layer):
        for i in range(2):

            @pl.when(layer == i)
            def _(i=i):
                loads[2 * i].wait()
                loads[2 * i + 1].wait()

        mine = jnp.where(layer == 0, me[0], me[1])
        for index, start, which, offset, take in spans(sizes, rows):
            at = pl.multiple_of((which ^ mine) * piece, TILE) + offset
            value = ordered[layer, pl.ds(pl.multiple_of(at, TILE), take), :]
            if index == 4:
                staged[index][layer, :, start : start + take] = value.T.astype(F32)
            elif index < 6:
                staged[index][layer, start : start + take, :] = value.astype(F32)
            else:
                value = value.astype(F32)
                names = lines(out)
                for i, ref in enumerate(names):
                    ref[pl.ds(layer, 1), :] = value[i : i + 1]
                for c in range(chunks):
                    i = len(names) + c
                    out.b_up[pl.ds(layer, 1), c * features : (c + 1) * features] = value[i : i + 1]
            if index < 6 and start + take == sizes[index]:
                store(index, layer).start()

    for layer in range(2):
        for index in range(6):
            store(index, layer).wait()


def unpack(bits, parts, weights):
    outs = [jax.ShapeDtypeStruct(weight.shape, F32) for weight in weights]
    shapes = Weights(*outs)
    large = squares(shapes) + (shapes.w_up, shapes.w_down)
    return pl.pallas_call(
        functools.partial(unpack_kernel, lambda layer: place_of(bits[layer])),
        in_specs=[pl.BlockSpec(memory_space=pl.ANY)] * 4,
        out_specs=[pl.BlockSpec(memory_space=pl.ANY if len(o.shape) == 3 else pltpu.VMEM) for o in outs],
        out_shape=outs,
        scratch_shapes=[pltpu.VMEM((2, 2 * parts[0].shape[0], parts[0].shape[1]), BF16)]
        + [pltpu.VMEM(o.shape, F32) for o in large]
        + [pltpu.SemaphoreType.DMA((4,)), pltpu.SemaphoreType.DMA((2, 6))],
        compiler_params=pltpu.CompilerParams(vmem_limit_bytes=20 * 2**20),
        name="unpack",
    )(*parts)


def from_behind(value, axis, steps):
    count = lax.axis_size(axis)
    initial, last = (max(0, -steps), min(count, count - steps))
    return lax.ppermute(value, axis, [(source, source + steps) for source in range(initial, last)])


def swap(value, bit):
    axis, step = bit
    return lax.ppermute(value, axis, [(i, i ^ step) for i in range(lax.axis_size(axis))])


def plus(a, b):
    return (a.astype(F32) + b.astype(F32)).astype(BF16)


def place_of(bits):
    me = jnp.int32(0)
    for axis, step in bits:
        me = me * 2 + lax.rem(lax.div(lax.axis_index(axis), step), 2)
    return me


def sum_rest(value, bits):
    axis, step = bits[0]
    me = (lax.axis_index(axis) // step) % 4

    def across(part, k):
        return lax.ppermute(part, axis, [(i, i ^ (k * step)) for i in range(lax.axis_size(axis))])

    rows = value.shape[0] // 4
    quarter = [lax.dynamic_slice_in_dim(value, (me ^ k) * rows, rows) for k in range(4)]
    got = [across(quarter[k], k) for k in (1, 2, 3)]
    kept = quarter[0].astype(F32)
    for part in got:
        kept = kept + part.astype(F32)
    kept = kept.astype(BF16)
    for bit in bits[2:]:
        kept = plus(kept, swap(kept, bit))
    a, b, c, d = [kept] + [across(kept, k) for k in (1, 2, 3)]
    odd, high = me % 2 == 1, me >= 2
    first, second = jnp.where(odd, b, a), jnp.where(odd, a, b)
    third, fourth = jnp.where(odd, d, c), jnp.where(odd, c, d)
    lower, upper = jnp.concatenate([first, second], axis=0), jnp.concatenate([third, fourth], axis=0)
    return jnp.where(high, jnp.concatenate([upper, lower], axis=0), jnp.concatenate([lower, upper], axis=0))


def sum_all(lower, upper, lower_bits, upper_bits, rest_bits, others):
    chains = []
    for (keep, send), bits in ((lower, lower_bits), (upper, upper_bits)):
        chains.append((plus(keep, swap(send, bits[0])), bits))
    for level in (1, 2):
        sent = [swap(kept[kept.shape[0] // 2 :], bits[level]) for kept, bits in chains]
        chains = [(plus(kept[: kept.shape[0] // 2], got), bits) for got, (kept, bits) in zip(sent, chains)]
        if level == 1:
            others = [with_layout_constraint(jnp.transpose(v, (1, 0, 2)), Layout((0, 1, 2))) for v in others]
            others, tied = lax.optimization_barrier((others, [kept for kept, _ in chains]))
            chains = [(kept, bits) for kept, (_, bits) in zip(tied, chains)]
    size = chains[0][0].shape[0]
    both = sum_rest(jnp.concatenate([kept for kept, _ in chains], axis=0), rest_bits)
    chains = [(both[:size], lower_bits), (both[size:], upper_bits)]
    for level in (2, 1):
        sent = [swap(kept, bits[level]) for kept, bits in chains]
        chains = [(jnp.concatenate([kept, got], axis=0), bits) for got, (kept, bits) in zip(sent, chains)]
    out = []
    for kept, bits in chains:
        out += [kept, swap(kept, bits[0])]
    return out, others


def local(hidden, write_cotangent, targets, positions, counts, *weights):
    weights = Weights(*weights)
    micro, _, _, rows, features = hidden.shape
    memory = write_cotangent.shape[3]
    full = -(-rows // TILE) * TILE
    bits = [(axis, 1 << i) for axis in (LINE, PAIR) for i in range(lax.axis_size(axis).bit_length() - 1)]
    core, along, across = (LINE, 1), (LINE, 2), (PAIR, 1)
    lower_bits, upper_bits = (core, across, along), (core, along, across)
    rest_bits = [bit for bit in bits if bit not in lower_bits]

    hidden_rows = hidden.reshape(micro, rows, features)
    lower_out, sent, stash = lower_forward(hidden_rows, weights, full)
    arrived = from_behind(sent, LINE, 1)
    out, grad, back, *upper = upper_both(
        upper_bits,
        counts.reshape(micro),
        lower_out,
        arrived,
        write_cotangent.reshape(micro, memory, features),
        targets.reshape(micro, targets.shape[3], features),
        positions.reshape(micro, 1, positions.shape[3]),
        weights,
        rows,
    )
    returned = from_behind(back, LINE, -1)
    grad_in, *lower = lower_backward(lower_bits, grad, returned, weights, stash, rows, memory)
    parts, (out, grad_in) = sum_all(lower, upper, lower_bits, upper_bits, rest_bits, (out, grad_in))
    grads = unpack((lower_bits, upper_bits), parts, weights)
    out, grad_in = (jnp.transpose(v, (1, 0, 2)).reshape(hidden.shape) for v in (out, grad_in))
    return (out, grad_in) + tuple(grads)


def solution(mesh):
    split = P(None, PAIR, LINE, None, None)
    placed = (split, split, split, P(None, PAIR, LINE, None), P(None, PAIR, LINE))
    count = len(Weights._fields)
    return jax.shard_map(
        local,
        mesh=mesh,
        in_specs=placed + (P(),) * count,
        out_specs=(split, split) + (P(),) * count,
        check_vma=False,
    )
```

```python
import functools
from typing import Any, NamedTuple

import jax
import jax.numpy as jnp
from jax import lax
from jax.experimental import pallas as pl
from jax.experimental.layout import Layout, with_layout_constraint
from jax.experimental.pallas import tpu as pltpu
from jax.sharding import PartitionSpec as P

EPSILON = 1e-12
DENSITY = 0.3989422804014327
ROOT_HALF = 0.7071067811865476
BELL = -0.7213475204444817
HEADS = 4
TILE = 16
STRIP = 64
PIECES = 8
LOW = -1e30
F32, BF16 = jnp.float32, jnp.bfloat16
LINE, PAIR = "seg", "item"


class Weights(NamedTuple):
    w_query: Any
    b_query: Any
    w_key: Any
    w_value: Any
    b_value: Any
    w_out: Any
    b_out: Any
    gain_attn: Any
    shift_attn: Any
    w_up: Any
    b_up: Any
    w_down: Any
    b_down: Any
    gain_ffn: Any
    shift_ffn: Any


class Stash(NamedTuple):
    x: Any
    query: Any
    key: Any
    value: Any
    prob: Any
    prob_rest: Any
    scale: Any
    context_t: Any
    context: Any
    inverse: Any
    normed_attn: Any
    middle: Any
    active: Any
    slope: Any
    normed_ffn: Any


class Rest(NamedTuple):
    x: Any
    query: Any
    key: Any
    value: Any
    context: Any
    attn: Any
    middle: Any
    branch: Any
    up: Any
    active: Any


def dot(a, b):
    return jnp.dot(a, b, preferred_element_type=F32)


def dot_nt(a, b):
    return lax.dot_general(a, b, (((1,), (1,)), ((), ())), preferred_element_type=F32)


def dot_tn(a, b):
    return lax.dot_general(a, b, (((0,), (0,)), ((), ())), preferred_element_type=F32)


def mean(v):
    return jnp.mean(v, axis=-1, keepdims=True)


def column_sum(v):
    return jnp.sum(v.astype(F32), axis=0, keepdims=True)


def normalize(v):
    centred = v - mean(v)
    inverse = lax.rsqrt(mean(centred * centred) + EPSILON)
    return centred * inverse, inverse


def norm_back(grad, normed, inverse):
    return inverse * (grad - mean(grad) - normed * mean(grad * normed))


def head_block(shape, width):
    rows = lax.div(lax.broadcasted_iota(jnp.int32, shape, 0), TILE)
    lanes = lax.div(lax.broadcasted_iota(jnp.int32, shape, 1), width)
    return rows == lanes


def spread_heads(rest, width):
    tiled = jnp.concatenate([rest] * HEADS, axis=0)
    return jnp.where(head_block(tiled.shape, width), tiled, jnp.zeros_like(tiled))


def fold_heads(spread, width):
    own = jnp.where(head_block(spread.shape, width), spread, 0.0)
    return own[:TILE] + own[TILE : 2 * TILE] + own[2 * TILE : 3 * TILE] + own[3 * TILE :]


def own_half(pair, h, width):
    lanes = lax.div(lax.broadcasted_iota(jnp.int32, pair.shape, 1), width)
    return jnp.where(lanes == h % 2, pair, jnp.zeros_like(pair))


def weigh_keys(s, live_rest):
    main = s.shape[0] - TILE
    top, bottom = s[:main], jnp.where(live_rest, s[main:], LOW)
    peak = jnp.maximum(jnp.max(top, axis=0, keepdims=True), jnp.max(bottom, axis=0, keepdims=True))
    yield 120
    top = jnp.exp(top - peak).astype(BF16)
    yield 220
    return top, jnp.exp(bottom - peak).astype(BF16)


def woven(*tasks):
    tasks = [[task, 0.0, total] for task, total in tasks]
    while tasks:
        task = min(tasks, key=lambda t: t[1] / t[2])
        length = next(task[0], None)
        if length is None:
            tasks.remove(task)
        else:
            task[1] += length
            yield length


def weave(*tasks):
    for _ in woven(*tasks):
        pass


def at(w, layer):
    return layer if w.w_query.shape[0] > 1 else 0


def layer_forward(x, layer, w, st, rows, result):
    full, features = x.shape
    main = full - TILE
    width = features // HEADS

    def row(ref):
        return ref[layer : layer + 1, :]

    st.x[...] = x
    q = ((dot(x, w.w_query[at(w, layer)]) + row(w.b_query)) * 0.125).astype(BF16)
    yield 150
    k = dot(x, w.w_key[at(w, layer)]).astype(BF16)
    yield 150
    v = (dot(x, w.w_value[at(w, layer)]) + row(w.b_value)).astype(BF16)
    st.query[...] = q
    st.key[...] = k
    st.value[...] = v
    yield 150
    q_t = q[:main].T
    v_t = v[:main].T
    live_rest = lax.broadcasted_iota(jnp.int32, (TILE, 1), 0) < rows - main
    def last_rows(out):
        top, bottom = yield from weigh_keys(dot_nt(k, spread_heads(q[main:], width)), live_rest)
        p_rest = jnp.concatenate([top, bottom], axis=0)
        p_rest = (p_rest.astype(F32) * (1.0 / column_sum(p_rest))).astype(BF16)
        st.prob_rest[...] = p_rest
        yield 50
        out.append(fold_heads(dot_tn(p_rest, v), width).astype(BF16))
        yield 50

    ones = jnp.ones((TILE, main), BF16)
    scores, weights, parts, bottoms, scales = {}, {}, [], [], []

    def first_rows():
        for h in range(-1, HEADS + 1):
            if h + 1 < HEADS:
                pair = slice(2 * width * ((h + 1) // 2), 2 * width * ((h + 1) // 2 + 1))
                scores[h + 1] = dot(own_half(k[:, pair], h + 1, width), q_t[pair, :])
                yield 80
            if h > 0:
                top, bottom = weights.pop(h - 1)
                part = dot(jnp.concatenate([v_t[(h - 1) * width : h * width, :], ones], axis=0), top)
                parts.append(part[:width])
                bottoms.append(bottom)
                scale = 1.0 / (part[width : width + 1] + column_sum(bottom))
                st.scale[h - 1 : h, :] = scale
                scales.append(jnp.broadcast_to(scale, (width, main)))
                yield 80
            if 0 <= h < HEADS:
                top, bottom = yield from weigh_keys(scores.pop(h), live_rest)
                st.prob[h, :main, :] = top
                st.prob[h, main:, :] = bottom
                weights[h] = top, bottom
                yield 60

    at_last = []
    yield from woven((last_rows(at_last), 450), (first_rows(), 2600))
    (context_rest,) = at_last
    context_t = jnp.concatenate(parts, axis=0)
    context_t = context_t + dot_tn(spread_heads(v[main:], width), jnp.concatenate(bottoms, axis=0))
    context_t = context_t * jnp.concatenate(scales, axis=0)
    st.context_t[...] = context_t
    context = jnp.concatenate([context_t.astype(BF16).T, context_rest], axis=0)
    st.context[...] = context
    yield 200
    normed_attn, inverse_attn = normalize(x.astype(F32) + dot(context, w.w_out[at(w, layer)]) + row(w.b_out))
    st.normed_attn[...] = normed_attn
    middle = normed_attn * row(w.gain_attn) + row(w.shift_attn)
    middle_low = middle.astype(BF16)
    st.middle[...] = middle_low
    total = middle + row(w.b_down)
    yield 400
    chunks = w.w_up.shape[2] // features

    def upward(c):
        part = slice(c * features, (c + 1) * features)
        return dot(middle_low, w.w_up[at(w, layer), :, part]) + w.b_up[layer : layer + 1, part]

    ahead = upward(0)
    for c in range(chunks):
        part = slice(c * features, (c + 1) * features)
        u, ahead = ahead, (upward(c + 1) if c + 1 < chunks else None)
        yield 50
        phi = 0.5 + 0.5 * lax.erf(u * ROOT_HALF)
        active = (u * phi).astype(BF16)
        st.active[:, part] = active
        yield 200
        slope = phi + u * (jnp.exp2(u * u * BELL) * DENSITY)
        st.slope[:, part] = slope.astype(BF16)
        yield 220
        total = total + dot(active, w.w_down[at(w, layer), part, :])
        yield 80
    normed_ffn, inverse_ffn = normalize(total)
    st.normed_ffn[...] = normed_ffn
    st.inverse[:, 0:1] = inverse_attn
    st.inverse[:, 1:2] = inverse_ffn
    result.append(normed_ffn * row(w.gain_ffn) + row(w.shift_ffn))
    yield 400


def layer_backward(grad_out, layer, w, st, g, rest, grad_up_ref, grad_s_ref, step, result, fill=False):
    full, features = st.x.shape
    main = full - TILE
    width = features // HEADS
    place = pl.ds(pl.multiple_of(step * TILE, TILE), TILE)

    def row(ref):
        return ref[layer : layer + 1, :]

    def add(ref, value):
        ref[...] += value

    normed_ffn = st.normed_ffn[...]
    add(g.gain_ffn, column_sum(grad_out * normed_ffn))
    add(g.shift_ffn, column_sum(grad_out))
    grad_sum = norm_back(grad_out * row(w.gain_ffn), normed_ffn, st.inverse[:, 1:2])
    grad_branch = grad_sum.astype(BF16)
    rest.branch[place, :] = grad_branch[main:]
    add(g.b_down, column_sum(grad_branch))
    grad_middle = grad_sum
    yield 500
    for c in range(w.w_up.shape[2] // features):
        part = slice(c * features, (c + 1) * features)
        grad_up = dot_nt(grad_branch, w.w_down[at(w, layer), part, :]) * st.slope[:, part].astype(F32)
        grad_up = grad_up.astype(BF16)
        yield 150
        grad_up_ref[:, part] = grad_up
        g.b_up[:, part] += column_sum(grad_up)
        grad_middle = grad_middle + dot_nt(grad_up, w.w_up[at(w, layer), :, part])
        yield 150
    rest.middle[place, :] = st.middle[main:, :]
    rest.up[place, :] = grad_up_ref[main:, :]
    rest.active[place, :] = st.active[main:, :]
    rest.context[place, :] = st.context[main:, :]

    def grad_ffn(cuts):
        for cut in range(cuts):
            part = slice(cut * units // cuts, (cut + 1) * units // cuts)
            g.w_down[part, :] += dot_tn(st.active[:main, part], grad_branch[:main])
            yield 360 // cuts
            g.w_up[part, :] += dot_tn(grad_up_ref[:main, part], st.middle[:main, :])
            yield 360 // cuts

    units = w.w_up.shape[2]
    filler = grad_ffn(2 if fill else 1)
    if not fill:
        yield from filler
    normed_attn = st.normed_attn[...]
    yield next(filler, 0)
    add(g.gain_attn, column_sum(grad_middle * normed_attn))
    add(g.shift_attn, column_sum(grad_middle))
    if fill:
        yield 100
        yield next(filler, 0)
    grad_normed = grad_middle * row(w.gain_attn)
    mean_grad, mean_both = mean(grad_normed), mean(grad_normed * normed_attn)
    if fill:
        yield 150
        yield next(filler, 0)
    grad_resid = st.inverse[:, 0:1] * (grad_normed - mean_grad - normed_attn * mean_both)
    grad_attn = grad_resid.astype(BF16)
    if fill:
        yield 150
    yield from filler
    rest.attn[place, :] = grad_attn[main:]
    add(g.b_out, column_sum(grad_attn))
    yield 50
    add(g.w_out, dot_tn(st.context[:main, :], grad_attn[:main]))
    scale = jnp.concatenate([jnp.broadcast_to(st.scale[h : h + 1, :], (width, main)) for h in range(HEADS)], axis=0)
    grad_context_t = (dot_nt(w.w_out[at(w, layer)], grad_attn[:main]) * scale).astype(BF16)
    grad_context = grad_context_t.T
    product = grad_context_t.astype(F32) * st.context_t[...]
    q, k, v = st.query[...], st.key[...], st.value[...]
    k_t = k[:main].T
    yield 400
    def last_rows(out):
        grad_spread = spread_heads(dot_nt(grad_attn[main:], w.w_out[at(w, layer)]).astype(BF16), width)
        p_rest = st.prob_rest[...]
        p_rest_wide = p_rest.astype(F32)
        yield 60
        grad_p = dot_nt(v, grad_spread)
        out.append(dot(p_rest, grad_spread))
        yield 100
        centre = jnp.sum(p_rest_wide * grad_p, axis=0, keepdims=True) / jnp.sum(p_rest_wide, axis=0, keepdims=True)
        yield 100
        grad_s = (p_rest_wide * (grad_p - centre)).astype(BF16)
        yield 60
        out.append(dot(grad_s, spread_heads(q[main:], width)))
        yield 60
        out.append(fold_heads(dot_tn(grad_s, k), width).astype(BF16))
        yield 60

    left = lax.broadcasted_iota(jnp.int32, (full, 2 * width), 1) < width
    q_parts, k_parts, v_parts, bottoms = [], [], [], []

    def first_rows():
        for h in range(0, HEADS, 2):
            pair = slice(width * h, width * (h + 2))
            for i in (h, h + 1):
                own = slice(i * width, (i + 1) * width)
                grad_p = dot(own_half(v[:, pair], i, width), grad_context_t[pair, :])
                yield 130
                grad_s = st.prob[i].astype(F32) * (grad_p - jnp.sum(product[own, :], axis=0, keepdims=True))
                grad_s = grad_s.astype(BF16)
                grad_s_ref[i] = grad_s
                yield 140
                q_parts.append(dot(k_t[own, :], grad_s[:main]))
                bottoms.append(grad_s[main:])
                yield 130
            both = dot(st.prob[h : h + 2].reshape(2 * full, main), grad_context[:, pair])
            v_parts.append(jnp.where(left, both[:full], both[full:]))
            yield 350
            both = dot(grad_s_ref[h : h + 2].reshape(2 * full, main), q[:main, pair])
            k_parts.append(jnp.where(left, both[:full], both[full:]))
            yield 350

    at_last = []
    yield from woven((last_rows(at_last), 500), (first_rows(), 3000))
    grad_v, grad_k, grad_q_rest = at_last
    grad_v = (grad_v + jnp.concatenate(v_parts, axis=1)).astype(BF16)
    grad_k = (grad_k + jnp.concatenate(k_parts, axis=1)).astype(BF16)
    grad_q_t = jnp.concatenate(q_parts, axis=0)
    grad_q_t = grad_q_t + dot_tn(spread_heads(k[main:], width), jnp.concatenate(bottoms, axis=0))
    grad_q = jnp.concatenate([grad_q_t.astype(BF16).T, grad_q_rest], axis=0) * BF16(0.125)
    rest.x[place, :] = st.x[main:, :]
    rest.query[place, :] = grad_q[main:]
    rest.key[place, :] = grad_k[main:]
    rest.value[place, :] = grad_v[main:]
    add(g.b_query, column_sum(grad_q))
    add(g.b_value, column_sum(grad_v))
    yield 400
    x_main = st.x[:main, :]
    add(g.w_query, dot_tn(x_main, grad_q[:main]))
    add(g.w_key, dot_tn(x_main, grad_k[:main]))
    add(g.w_value, dot_tn(x_main, grad_v[:main]))
    yield 400
    result.append(
        grad_resid
        + dot_nt(grad_q, w.w_query[at(w, layer)])
        + dot_nt(grad_k, w.w_key[at(w, layer)])
        + dot_nt(grad_v, w.w_value[at(w, layer)])
    )
    yield 300


def add_rest(g, rest):
    def add(ref, left, right):
        ref[...] += dot_tn(left[...], right[...])

    add(g.w_query, rest.x, rest.query)
    add(g.w_key, rest.x, rest.key)
    add(g.w_value, rest.x, rest.value)
    add(g.w_out, rest.context, rest.attn)
    units, features = g.w_down.shape

    @pl.loop(0, units // features)
    def _(c):
        part = pl.ds(pl.multiple_of(c * features, features), features)
        g.w_up[part, :] += dot_tn(rest.up[:, part], rest.middle[...])
        g.w_down[part, :] += dot_tn(rest.active[:, part], rest.branch[...])


FORWARD, BACKWARD = 7600, 8650


def squares(g):
    return (g.w_query, g.w_key, g.w_value, g.w_out)


def lines(g):
    return (g.b_query, g.b_value, g.b_out, g.gain_attn, g.shift_attn, g.b_down, g.gain_ffn, g.shift_ffn)


def packed_rows(features, units):
    used = 4 * features + 2 * units + len(lines(Weights(*range(len(Weights._fields))))) + units // features
    return -(-used // (PIECES * TILE)) * PIECES * TILE


def spans(sizes, rows):
    piece = rows // PIECES
    out, at = [], 0
    for index, size in enumerate(sizes):
        done = 0
        while done < size:
            take = min(size - done, piece - at % piece)
            out.append((index, done, at // piece, at % piece, take))
            done, at = done + take, at + take
    return out


def emit(g, keep, send, ordered, me):
    units, features = g.w_down.shape
    rows = ordered.shape[0]
    piece = rows // PIECES
    chunks = units // features
    arrays = squares(g) + (g.w_up, g.w_down)
    last = [ref[...] for ref in lines(g)]
    last += [g.b_up[:, c * features : (c + 1) * features] for c in range(chunks)]
    sizes = [ref.shape[0] for ref in arrays]
    left = rows - sum(sizes)
    last.append(jnp.zeros((left - len(last), features), F32))
    tail = jnp.concatenate(last, axis=0).astype(BF16)
    for index, start, which, offset, take in spans(sizes + [left], rows):
        if index < len(arrays):
            value = arrays[index][start : start + take, :].astype(BF16)
        else:
            value = tail[start : start + take]
        at = pl.multiple_of((which ^ me) * piece, TILE) + offset
        ordered[pl.ds(pl.multiple_of(at, TILE), take), :] = value
    half = rows // 2
    keep[...] = ordered[:half, :]
    send[...] = ordered[half:, :]


def stash_shapes(full, features, units):
    main = full - TILE
    square = ((full, features), BF16)
    wide = ((full, units), BF16)
    exact = ((full, features), F32)
    return Stash(
        x=square,
        query=square,
        key=square,
        value=square,
        prob=((HEADS, full, main), BF16),
        prob_rest=((full, HEADS * TILE), BF16),
        scale=((HEADS, main), F32),
        context_t=((features, main), F32),
        context=square,
        inverse=((full, 2), F32),
        normed_attn=exact,
        middle=square,
        active=wide,
        slope=wide,
        normed_ffn=exact,
    )


def scratch(micro, full, features, units):
    square, line = (features, features), (1, features)
    sums = Weights(
        w_query=square, b_query=line, w_key=square, w_value=square, b_value=line, w_out=square, b_out=line,
        gain_attn=line, shift_attn=line, w_up=(units, features), b_up=(1, units), w_down=(units, features),
        b_down=line, gain_ffn=line, shift_ffn=line,
    )
    rest = Rest(*[(micro * TILE, features)] * 8, up=(micro * TILE, units), active=(micro * TILE, units))
    out = [pltpu.VMEM(size, F32) for size in sums] + [pltpu.VMEM(size, BF16) for size in rest]
    out.append(pltpu.VMEM((full, units), BF16))
    out.append(pltpu.VMEM((HEADS, full, full - TILE), BF16))
    out.append(pltpu.VMEM((packed_rows(features, units), features), BF16))
    return out


def take_scratch(refs):
    count = len(Weights._fields)
    g, refs = Weights(*refs[:count]), refs[count:]
    count = len(Rest._fields)
    return g, Rest(*refs[:count]), *refs[count:]


def weight_specs(weights, layer=None):
    specs = []
    for weight in weights:
        if layer is None:
            specs.append(whole())
        elif weight.ndim == 3:
            specs.append(pl.BlockSpec((1,) + weight.shape[1:], lambda m: (layer, 0, 0)))
        else:
            specs.append(pl.BlockSpec(weight.shape, lambda m: (0, 0)))
    return specs


def by_micro(shape):
    rank = len(shape)
    return pl.BlockSpec((1,) + tuple(shape[1:]), lambda m: (m,) + (0,) * (rank - 1))


def ahead(shape):
    rank, last = len(shape), shape[0] - 1
    return pl.BlockSpec((1,) + tuple(shape[1:]), lambda m: (jnp.minimum(m, last),) + (0,) * (rank - 1))


def behind(shape):
    rank = len(shape)
    return pl.BlockSpec((1,) + tuple(shape[1:]), lambda m: (jnp.maximum(m - 1, 0),) + (0,) * (rank - 1))


def fixed(shape):
    rank = len(shape)
    return pl.BlockSpec(tuple(shape), lambda m: (0,) * rank)


def whole():
    return pl.BlockSpec(memory_space=pltpu.VMEM)


def smem():
    return pl.BlockSpec(memory_space=pltpu.SMEM)


def lower_forward_kernel(x_ref, *refs):
    w, refs = Weights(*refs[: len(Weights._fields)]), refs[len(Weights._fields) :]
    out_ref, sent_ref, *refs = refs
    st = Stash(*[ref.at[0] for ref in refs[:-1]])
    padded = refs[-1]
    rows = x_ref.shape[1]
    main = padded.shape[0] - TILE
    padded[main:, :] = jnp.zeros((TILE, padded.shape[1]), BF16)
    padded[:rows, :] = x_ref[0]
    result = []
    weave((layer_forward(padded[...], 0, w, st, rows, result), 1))
    y = result[0].astype(BF16)
    out_ref[0] = y
    sent_ref[0] = y[main:]


def lower_forward(hidden, weights, full):
    micro, rows, features = hidden.shape
    outs = [jax.ShapeDtypeStruct((micro, full, features), BF16), jax.ShapeDtypeStruct((micro, TILE, features), BF16)]
    shapes = stash_shapes(full, features, weights.w_up.shape[2])
    outs += [jax.ShapeDtypeStruct((micro,) + shape, kind) for shape, kind in shapes]
    out, sent, *stash = pl.pallas_call(
        lower_forward_kernel,
        grid=(micro,),
        in_specs=[by_micro(hidden.shape)] + weight_specs(weights, 0),
        out_specs=[by_micro(o.shape) for o in outs],
        out_shape=outs,
        scratch_shapes=[pltpu.VMEM((full, features), BF16)],
        compiler_params=pltpu.CompilerParams(vmem_limit_bytes=60 * 2**20),
        name="lower_forward",
    )(hidden, *weights)
    return out, sent, Stash(*stash)


def zero_sums(g):
    for ref in g:
        rows, features = ref.shape
        if rows == 1:
            ref[...] = jnp.zeros_like(ref)
        else:

            @pl.loop(0, rows // STRIP)
            def _(i, ref=ref, features=features):
                ref[pl.ds(pl.multiple_of(i * STRIP, STRIP), STRIP), :] = jnp.zeros((STRIP, features), F32)


def upper_forward(rows, lead, arrived, cot_ref, target_ref, slot_ref, count, x_ref, out_ref, grad_out, w, st):
    full, features = x_ref.shape[1:]
    memory = cot_ref.shape[1]
    main = full - TILE
    x = x_ref[0]
    is_read = lax.broadcasted_iota(jnp.int32, (TILE, features), 0) < memory
    moved = jnp.logical_and(is_read, jnp.logical_not(lead))
    x = jnp.concatenate([jnp.where(moved, arrived, x[:TILE]), x[TILE:]], axis=0)
    result = []
    yield from layer_forward(x, 1, w, st, rows, result)
    y = result[0]
    out_ref[0] = y[:rows].astype(BF16)
    slots = slot_ref.shape[2]
    slot_row = lax.broadcasted_iota(jnp.int32, (main, slots), 0) - memory
    slot_at = lax.broadcasted_iota(jnp.int32, (main, slots), 1)
    hit = jnp.logical_and(slot_row == slot_ref[0], slot_at < count)
    hit = jnp.where(hit, 1.0, 0.0).astype(BF16)
    used = dot(hit, jnp.ones((slots, features), BF16))
    wanted = dot(hit, target_ref[0])
    grad_out[:main, :] = (y[:main] * used - wanted) / count.astype(F32)
    grad_out[main : main + memory, :] = cot_ref[0].astype(F32)
    yield 300


def upper_backward(lead, memory, grad_out, grad_ref, back_ref, w, st, *refs, fill):
    result = []
    yield from layer_backward(grad_out[...], 1, w, st, *refs, result, fill)
    grad_in = result[0]
    is_read = lax.broadcasted_iota(jnp.int32, (TILE, grad_in.shape[1]), 0) < memory
    moved = jnp.logical_and(is_read, jnp.logical_not(lead))
    back_ref[0] = grad_in[:TILE].astype(BF16)
    grad_ref[0, :TILE, :] = jnp.where(moved, 0.0, grad_in[:TILE])
    grad_ref[0, TILE:, :] = grad_in[TILE:]


def upper_kernel(rows, micro, bits, count_ref, x_ref, arrived_ref, cot_ref, target_ref, slot_ref, *refs):
    step = pl.program_id(0)
    w, refs = Weights(*refs[: len(Weights._fields)]), refs[len(Weights._fields) :]
    out_ref, grad_ref, back_ref, keep_ref, send_ref = refs[:5]
    refs = refs[5:]
    st, refs = Stash(*refs[: len(Stash._fields)]), refs[len(Stash._fields) :]
    grad_out, *refs = refs
    g, rest, grad_up_ref, grad_s_ref, ordered = take_scratch(refs)
    memory = cot_ref.shape[1]
    lead = lax.axis_index(LINE) == 0

    def turn(slot):
        twice = Stash(*[ref if ref.shape[0] != 2 else ref.at[slot] for ref in st])
        return twice

    def forward(slot):
        now = jnp.minimum(step, micro - 1)
        count, arrived = count_ref[now], arrived_ref[now]
        return upper_forward(
            rows, lead, arrived, cot_ref, target_ref, slot_ref, count, x_ref, out_ref, grad_out, w, turn(slot)
        )

    def backward(slot, fill):
        refs = (g, rest, grad_up_ref, grad_s_ref, step - 1)
        return upper_backward(lead, memory, grad_out, grad_ref, back_ref, w, turn(slot), *refs, fill=fill)

    @pl.when(step == 0)
    def _():
        zero_sums(g)
        grad_out[grad_out.shape[0] - TILE :, :] = jnp.zeros((TILE, grad_out.shape[1]), F32)
        weave((forward(0), FORWARD))

    @pl.when(jnp.logical_and(step > 0, step < micro))
    def _():
        slot = lax.rem(step, 2)
        weave((forward(slot), FORWARD), (backward(1 - slot, True), BACKWARD))

    @pl.when(step == micro)
    def _():
        weave((backward((micro - 1) % 2, False), BACKWARD))
        add_rest(g, rest)
        emit(g, keep_ref, send_ref, ordered, place_of(bits))


def half_packed(features, units):
    return jax.ShapeDtypeStruct((packed_rows(features, units) // 2, features), BF16)


def upper_both(bits, counts, x, arrived, cotangent, targets, slots, weights, rows):
    micro, full, features = x.shape
    units = weights.w_up.shape[2]
    outs = [
        jax.ShapeDtypeStruct((micro, rows, features), BF16),
        jax.ShapeDtypeStruct(x.shape, F32),
        jax.ShapeDtypeStruct((micro, TILE, features), BF16),
        half_packed(features, units),
        half_packed(features, units),
    ]
    ins = (x, arrived, cotangent, targets, slots)
    shapes = stash_shapes(full, features, units)
    once = (shapes.inverse, shapes.normed_attn, shapes.middle, shapes.active, shapes.slope, shapes.normed_ffn)
    stash = [pltpu.VMEM(s if (s, k) in once and (s, k) != shapes.x else (2,) + s, k) for s, k in shapes] + [pltpu.VMEM((full, features), F32)]
    return pl.pallas_call(
        functools.partial(upper_kernel, rows, micro, bits),
        grid=(micro + 1,),
        in_specs=[smem()] + [whole() if a is arrived else ahead(a.shape) for a in ins] + weight_specs(weights),
        out_specs=[ahead(outs[0].shape), behind(outs[1].shape), behind(outs[2].shape)]
        + [fixed(o.shape) for o in outs[3:]],
        out_shape=outs,
        scratch_shapes=stash + scratch(micro, full, features, units),
        compiler_params=pltpu.CompilerParams(vmem_limit_bytes=52 * 2**20),
        name="upper_both",
    )(counts, *ins, *weights)


def lower_backward_kernel(memory, bits, grad_ref, back_ref, *refs):
    step, steps = pl.program_id(0), pl.num_programs(0)
    w, refs = Weights(*refs[: len(Weights._fields)]), refs[len(Weights._fields) :]
    st, refs = Stash(*[ref.at[0] for ref in refs[: len(Stash._fields)]]), refs[len(Stash._fields) :]
    out_ref, keep_ref, send_ref, *refs = refs
    g, rest, grad_up_ref, grad_s_ref, ordered = take_scratch(refs)
    full, features = grad_ref.shape[1:]
    main = full - TILE

    @pl.when(step == 0)
    def _():
        zero_sums(g)

    is_write = lax.broadcasted_iota(jnp.int32, (TILE, features), 0) < memory
    returned = jnp.where(is_write, back_ref[step].astype(F32), 0.0)
    grad_out = jnp.concatenate([grad_ref[0, :main, :], grad_ref[0, main:, :] + returned], axis=0)
    result = []
    weave((layer_backward(grad_out, 0, w, st, g, rest, grad_up_ref, grad_s_ref, step, result), 1))
    out_ref[0] = result[0][: out_ref.shape[1]].astype(BF16)

    @pl.when(step == steps - 1)
    def _():
        add_rest(g, rest)
        emit(g, keep_ref, send_ref, ordered, place_of(bits))


def lower_backward(bits, grad, back, weights, stash, rows, memory):
    micro, full, features = grad.shape
    units = weights.w_up.shape[2]
    outs = [
        jax.ShapeDtypeStruct((micro, rows, features), BF16),
        half_packed(features, units),
        half_packed(features, units),
    ]
    return pl.pallas_call(
        functools.partial(lower_backward_kernel, memory, bits),
        grid=(micro,),
        in_specs=[by_micro(grad.shape), whole()]
        + weight_specs(weights)
        + [by_micro(a.shape) for a in stash],
        out_specs=[by_micro(outs[0].shape)] + [fixed(o.shape) for o in outs[1:]],
        out_shape=outs,
        scratch_shapes=scratch(micro, full, features, units),
        compiler_params=pltpu.CompilerParams(vmem_limit_bytes=52 * 2**20),
        name="lower_backward",
    )(grad, back, *weights, *stash)


def unpack_kernel(bits, *refs):
    sources, refs = refs[:4], refs[4:]
    out, refs = Weights(*refs[: len(Weights._fields)]), refs[len(Weights._fields) :]
    ordered, *staged, in_sems, out_sems = refs
    features, units = out.w_up.shape[1:]
    chunks = units // features
    half = sources[0].shape[0]
    rows, piece = 2 * half, 2 * half // PIECES
    arrays = squares(out) + (out.w_up, out.w_down)
    loads = [
        pltpu.make_async_copy(source, ordered.at[i // 2, (i % 2) * half : (i % 2 + 1) * half], in_sems.at[i])
        for i, source in enumerate(sources)
    ]
    for load in loads:
        load.start()
    sizes = [features] * 4 + [units, units]
    sizes.append(rows - sum(sizes))
    me = place_of(bits)

    def store(index, layer):
        return pltpu.make_async_copy(staged[index].at[layer], arrays[index].at[layer], out_sems.at[layer, index])

    @pl.loop(0, 2)
    def _(layer):
        for i in range(2):

            @pl.when(layer == i)
            def _(i=i):
                loads[2 * i].wait()
                loads[2 * i + 1].wait()

        for index, start, which, offset, take in spans(sizes, rows):
            at = pl.multiple_of((which ^ me) * piece, TILE) + offset
            value = ordered[layer, pl.ds(pl.multiple_of(at, TILE), take), :]
            if index == 4:
                staged[index][layer, :, start : start + take] = value.T.astype(F32)
            elif index < 6:
                staged[index][layer, start : start + take, :] = value.astype(F32)
            else:
                value = value.astype(F32)
                names = lines(out)
                for i, ref in enumerate(names):
                    ref[pl.ds(layer, 1), :] = value[i : i + 1]
                for c in range(chunks):
                    i = len(names) + c
                    out.b_up[pl.ds(layer, 1), c * features : (c + 1) * features] = value[i : i + 1]
            if index < 6 and start + take == sizes[index]:
                store(index, layer).start()

    for layer in range(2):
        for index in range(6):
            store(index, layer).wait()


def unpack(bits, parts, weights):
    outs = [jax.ShapeDtypeStruct(weight.shape, F32) for weight in weights]
    shapes = Weights(*outs)
    large = squares(shapes) + (shapes.w_up, shapes.w_down)
    return pl.pallas_call(
        functools.partial(unpack_kernel, bits),
        in_specs=[pl.BlockSpec(memory_space=pl.ANY)] * 4,
        out_specs=[pl.BlockSpec(memory_space=pl.ANY if len(o.shape) == 3 else pltpu.VMEM) for o in outs],
        out_shape=outs,
        scratch_shapes=[pltpu.VMEM((2, 2 * parts[0].shape[0], parts[0].shape[1]), BF16)]
        + [pltpu.VMEM(o.shape, F32) for o in large]
        + [pltpu.SemaphoreType.DMA((4,)), pltpu.SemaphoreType.DMA((2, 6))],
        compiler_params=pltpu.CompilerParams(vmem_limit_bytes=20 * 2**20),
        name="unpack",
    )(*parts)


def from_behind(value, axis, steps):
    count = lax.axis_size(axis)
    initial, last = (max(0, -steps), min(count, count - steps))
    return lax.ppermute(value, axis, [(source, source + steps) for source in range(initial, last)])


def swap(value, bit):
    axis, step = bit
    return lax.ppermute(value, axis, [(i, i ^ step) for i in range(lax.axis_size(axis))])


def plus(a, b):
    return (a.astype(F32) + b.astype(F32)).astype(BF16)


def place_of(bits):
    me = jnp.int32(0)
    for axis, step in bits:
        me = me * 2 + lax.rem(lax.div(lax.axis_index(axis), step), 2)
    return me


def sum_rest(value, bits):
    axis, step = bits[0]
    me = (lax.axis_index(axis) // step) % 4

    def across(part, k):
        return lax.ppermute(part, axis, [(i, i ^ (k * step)) for i in range(lax.axis_size(axis))])

    rows = value.shape[0] // 4
    quarter = [lax.dynamic_slice_in_dim(value, (me ^ k) * rows, rows) for k in range(4)]
    got = [across(quarter[k], k) for k in (1, 2, 3)]
    kept = quarter[0].astype(F32)
    for part in got:
        kept = kept + part.astype(F32)
    kept = kept.astype(BF16)
    for bit in bits[2:]:
        kept = plus(kept, swap(kept, bit))
    a, b, c, d = [kept] + [across(kept, k) for k in (1, 2, 3)]
    odd, high = me % 2 == 1, me >= 2
    first, second = jnp.where(odd, b, a), jnp.where(odd, a, b)
    third, fourth = jnp.where(odd, d, c), jnp.where(odd, c, d)
    lower, upper = jnp.concatenate([first, second], axis=0), jnp.concatenate([third, fourth], axis=0)
    return jnp.where(high, jnp.concatenate([upper, lower], axis=0), jnp.concatenate([lower, upper], axis=0))


def sum_all(halves, core, along, across, rest_bits, others):
    def to(part, j):
        swaps = [(axis, step) for (axis, step), used in ((across, j % 2), (along, j // 2)) if used]
        sizes = [lax.axis_size(axis) for axis in (LINE, PAIR)]
        line = sum(step for axis, step in swaps if axis == LINE)
        pair = sum(step for axis, step in swaps if axis == PAIR)
        perm = [(i * sizes[1] + k, (i ^ line) * sizes[1] + (k ^ pair)) for i in range(sizes[0]) for k in range(sizes[1])]
        return lax.ppermute(part, (LINE, PAIR), perm)

    chains = [plus(keep, swap(send, core)) for keep, send in halves]
    rows = chains[0].shape[0] // 4
    for i, kept in enumerate(chains):
        got = [to(kept[j * rows : (j + 1) * rows], j) for j in (1, 2, 3)]
        chains[i] = sum([part.astype(F32) for part in got], kept[:rows].astype(F32)).astype(BF16)
    chains = [sum_rest(kept, rest_bits) for kept in chains]
    others, chains[0] = lax.optimization_barrier((others, chains[0]))
    chains = [jnp.concatenate([kept] + [to(kept, j) for j in (1, 2, 3)], axis=0) for kept in chains]
    others = [with_layout_constraint(jnp.transpose(v, (1, 0, 2)), Layout((0, 1, 2))) for v in others]
    others, chains[0] = lax.optimization_barrier((others, chains[0]))
    return [part for kept in chains for part in (kept, swap(kept, core))], others


def local(hidden, write_cotangent, targets, positions, counts, *weights):
    weights = Weights(*weights)
    micro, _, _, rows, features = hidden.shape
    memory = write_cotangent.shape[3]
    full = -(-rows // TILE) * TILE
    bits = [(axis, 1 << i) for axis in (LINE, PAIR) for i in range(lax.axis_size(axis).bit_length() - 1)]
    core, along, across = (LINE, 1), (LINE, 2), (PAIR, 1)
    piece_bits = (core, along, across)
    rest_bits = [bit for bit in bits if bit not in piece_bits]

    hidden_rows = hidden.reshape(micro, rows, features)
    lower_out, sent, stash = lower_forward(hidden_rows, weights, full)
    arrived = from_behind(sent, LINE, 1)
    out, grad, back, *upper = upper_both(
        piece_bits,
        counts.reshape(micro),
        lower_out,
        arrived,
        write_cotangent.reshape(micro, memory, features),
        targets.reshape(micro, targets.shape[3], features),
        positions.reshape(micro, 1, positions.shape[3]),
        weights,
        rows,
    )
    returned = from_behind(back, LINE, -1)
    grad_in, *lower = lower_backward(piece_bits, grad, returned, weights, stash, rows, memory)
    parts, (out, grad_in) = sum_all((lower, upper), core, along, across, rest_bits, (out, grad_in))
    grads = unpack(piece_bits, parts, weights)
    out, grad_in = (jnp.transpose(v, (1, 0, 2)).reshape(hidden.shape) for v in (out, grad_in))
    return (out, grad_in) + tuple(grads)


def solution(mesh):
    split = P(None, PAIR, LINE, None, None)
    placed = (split, split, split, P(None, PAIR, LINE, None), P(None, PAIR, LINE))
    count = len(Weights._fields)
    return jax.shard_map(
        local,
        mesh=mesh,
        in_specs=placed + (P(),) * count,
        out_specs=(split, split) + (P(),) * count,
        check_vma=False,
    )
```

```python
import functools
from typing import Any, NamedTuple

import jax
import jax.numpy as jnp
from jax import lax
from jax.experimental import pallas as pl
from jax.experimental.layout import Layout, with_layout_constraint
from jax.experimental.pallas import tpu as pltpu
from jax.sharding import PartitionSpec as P

EPSILON = 1e-12
DENSITY = 0.3989422804014327
ROOT_HALF = 0.7071067811865476
BELL = -0.7213475204444817
HEADS = 4
TILE = 16
STRIP = 64
PIECES = 8
LOW = -1e30
F32, BF16 = jnp.float32, jnp.bfloat16
LINE, PAIR = "seg", "item"


class Weights(NamedTuple):
    w_query: Any
    b_query: Any
    w_key: Any
    w_value: Any
    b_value: Any
    w_out: Any
    b_out: Any
    gain_attn: Any
    shift_attn: Any
    w_up: Any
    b_up: Any
    w_down: Any
    b_down: Any
    gain_ffn: Any
    shift_ffn: Any


class Stash(NamedTuple):
    x: Any
    query: Any
    key: Any
    value: Any
    prob: Any
    prob_rest: Any
    scale: Any
    context_t: Any
    context: Any
    inverse: Any
    normed_attn: Any
    middle: Any
    active: Any
    slope: Any
    normed_ffn: Any


class Rest(NamedTuple):
    x: Any
    query: Any
    key: Any
    value: Any
    context: Any
    attn: Any
    middle: Any
    branch: Any
    up: Any
    active: Any


def dot(a, b):
    return jnp.dot(a, b, preferred_element_type=F32)


def dot_nt(a, b):
    return lax.dot_general(a, b, (((1,), (1,)), ((), ())), preferred_element_type=F32)


def dot_tn(a, b):
    return lax.dot_general(a, b, (((0,), (0,)), ((), ())), preferred_element_type=F32)


def mean(v):
    return jnp.mean(v, axis=-1, keepdims=True)


def column_sum(v):
    return jnp.sum(v.astype(F32), axis=0, keepdims=True)


def normalize(v):
    centred = v - mean(v)
    inverse = lax.rsqrt(mean(centred * centred) + EPSILON)
    return centred * inverse, inverse


def norm_back(grad, normed, inverse):
    return inverse * (grad - mean(grad) - normed * mean(grad * normed))


def head_block(shape, width):
    rows = lax.div(lax.broadcasted_iota(jnp.int32, shape, 0), TILE)
    lanes = lax.div(lax.broadcasted_iota(jnp.int32, shape, 1), width)
    return rows == lanes


def spread_heads(rest, width):
    tiled = jnp.concatenate([rest] * HEADS, axis=0)
    return jnp.where(head_block(tiled.shape, width), tiled, jnp.zeros_like(tiled))


def fold_heads(spread, width):
    own = jnp.where(head_block(spread.shape, width), spread, 0.0)
    return own[:TILE] + own[TILE : 2 * TILE] + own[2 * TILE : 3 * TILE] + own[3 * TILE :]


def own_half(pair, h, width):
    lanes = lax.div(lax.broadcasted_iota(jnp.int32, pair.shape, 1), width)
    return jnp.where(lanes == h % 2, pair, jnp.zeros_like(pair))


def weigh_keys(s, live_rest):
    main = s.shape[0] - TILE
    top, bottom = s[:main], jnp.where(live_rest, s[main:], LOW)
    peak = jnp.maximum(jnp.max(top, axis=0, keepdims=True), jnp.max(bottom, axis=0, keepdims=True))
    yield 120
    top = jnp.exp(top - peak).astype(BF16)
    yield 220
    return top, jnp.exp(bottom - peak).astype(BF16)


def woven(*tasks):
    tasks = [[task, 0.0, total] for task, total in tasks]
    while tasks:
        task = min(tasks, key=lambda t: t[1] / t[2])
        length = next(task[0], None)
        if length is None:
            tasks.remove(task)
        else:
            task[1] += length
            yield length


def weave(*tasks):
    for _ in woven(*tasks):
        pass


def at(w, layer):
    return layer if w.w_query.shape[0] > 1 else 0


def layer_forward(x, layer, w, st, rows, result):
    full, features = x.shape
    main = full - TILE
    width = features // HEADS

    def row(ref):
        return ref[layer : layer + 1, :]

    st.x[...] = x
    q = ((dot(x, w.w_query[at(w, layer)]) + row(w.b_query)) * 0.125).astype(BF16)
    yield 150
    k = dot(x, w.w_key[at(w, layer)]).astype(BF16)
    yield 150
    v = (dot(x, w.w_value[at(w, layer)]) + row(w.b_value)).astype(BF16)
    st.query[...] = q
    st.key[...] = k
    st.value[...] = v
    yield 150
    q_t = q[:main].T
    v_t = v[:main].T
    live_rest = lax.broadcasted_iota(jnp.int32, (TILE, 1), 0) < rows - main
    def last_rows(out):
        top, bottom = yield from weigh_keys(dot_nt(k, spread_heads(q[main:], width)), live_rest)
        p_rest = jnp.concatenate([top, bottom], axis=0)
        p_rest = (p_rest.astype(F32) * (1.0 / column_sum(p_rest))).astype(BF16)
        st.prob_rest[...] = p_rest
        yield 50
        out.append(fold_heads(dot_tn(p_rest, v), width).astype(BF16))
        yield 50

    ones = jnp.ones((TILE, main), BF16)
    scores, weights, parts, bottoms, scales = {}, {}, [], [], []

    def first_rows():
        for h in range(-1, HEADS + 1):
            if h + 1 < HEADS:
                pair = slice(2 * width * ((h + 1) // 2), 2 * width * ((h + 1) // 2 + 1))
                scores[h + 1] = dot(own_half(k[:, pair], h + 1, width), q_t[pair, :])
                yield 80
            if h > 0:
                top, bottom = weights.pop(h - 1)
                part = dot(jnp.concatenate([v_t[(h - 1) * width : h * width, :], ones], axis=0), top)
                parts.append(part[:width])
                bottoms.append(bottom)
                scale = 1.0 / (part[width : width + 1] + column_sum(bottom))
                st.scale[h - 1 : h, :] = scale
                scales.append(jnp.broadcast_to(scale, (width, main)))
                yield 80
            if 0 <= h < HEADS:
                top, bottom = yield from weigh_keys(scores.pop(h), live_rest)
                st.prob[h, :main, :] = top
                st.prob[h, main:, :] = bottom
                weights[h] = top, bottom
                yield 60

    at_last = []
    yield from woven((last_rows(at_last), 450), (first_rows(), 2600))
    (context_rest,) = at_last
    context_t = jnp.concatenate(parts, axis=0)
    context_t = context_t + dot_tn(spread_heads(v[main:], width), jnp.concatenate(bottoms, axis=0))
    context_t = context_t * jnp.concatenate(scales, axis=0)
    st.context_t[...] = context_t
    context = jnp.concatenate([context_t.astype(BF16).T, context_rest], axis=0)
    st.context[...] = context
    yield 200
    normed_attn, inverse_attn = normalize(x.astype(F32) + dot(context, w.w_out[at(w, layer)]) + row(w.b_out))
    st.normed_attn[...] = normed_attn
    middle = normed_attn * row(w.gain_attn) + row(w.shift_attn)
    middle_low = middle.astype(BF16)
    st.middle[...] = middle_low
    total = middle + row(w.b_down)
    yield 400
    chunks = w.w_up.shape[2] // features

    def upward(c):
        part = slice(c * features, (c + 1) * features)
        return dot(middle_low, w.w_up[at(w, layer), :, part]) + w.b_up[layer : layer + 1, part]

    ahead = upward(0)
    for c in range(chunks):
        part = slice(c * features, (c + 1) * features)
        u, ahead = ahead, (upward(c + 1) if c + 1 < chunks else None)
        yield 50
        phi = 0.5 + 0.5 * lax.erf(u * ROOT_HALF)
        active = (u * phi).astype(BF16)
        st.active[:, part] = active
        yield 200
        slope = phi + u * (jnp.exp2(u * u * BELL) * DENSITY)
        st.slope[:, part] = slope.astype(BF16)
        yield 220
        total = total + dot(active, w.w_down[at(w, layer), part, :])
        yield 80
    normed_ffn, inverse_ffn = normalize(total)
    st.normed_ffn[...] = normed_ffn
    st.inverse[:, 0:1] = inverse_attn
    st.inverse[:, 1:2] = inverse_ffn
    result.append(normed_ffn * row(w.gain_ffn) + row(w.shift_ffn))
    yield 400


def layer_backward(grad_out, layer, w, st, g, rest, grad_up_ref, grad_s_ref, step, result, fill=False):
    full, features = st.x.shape
    main = full - TILE
    width = features // HEADS
    place = pl.ds(pl.multiple_of(step * TILE, TILE), TILE)

    def row(ref):
        return ref[layer : layer + 1, :]

    def add(ref, value):
        ref[...] += value

    normed_ffn = st.normed_ffn[...]
    add(g.gain_ffn, column_sum(grad_out * normed_ffn))
    add(g.shift_ffn, column_sum(grad_out))
    grad_sum = norm_back(grad_out * row(w.gain_ffn), normed_ffn, st.inverse[:, 1:2])
    grad_branch = grad_sum.astype(BF16)
    rest.branch[place, :] = grad_branch[main:]
    add(g.b_down, column_sum(grad_branch))
    grad_middle = grad_sum
    yield 500
    for c in range(w.w_up.shape[2] // features):
        part = slice(c * features, (c + 1) * features)
        grad_up = dot_nt(grad_branch, w.w_down[at(w, layer), part, :]) * st.slope[:, part].astype(F32)
        grad_up = grad_up.astype(BF16)
        yield 150
        grad_up_ref[:, part] = grad_up
        g.b_up[:, part] += column_sum(grad_up)
        grad_middle = grad_middle + dot_nt(grad_up, w.w_up[at(w, layer), :, part])
        yield 150
    rest.middle[place, :] = st.middle[main:, :]
    rest.up[place, :] = grad_up_ref[main:, :]
    rest.active[place, :] = st.active[main:, :]
    rest.context[place, :] = st.context[main:, :]

    def grad_ffn(cuts):
        for cut in range(cuts):
            part = slice(cut * units // cuts, (cut + 1) * units // cuts)
            g.w_down[part, :] += dot_tn(st.active[:main, part], grad_branch[:main])
            yield 360 // cuts
            g.w_up[part, :] += dot_tn(grad_up_ref[:main, part], st.middle[:main, :])
            yield 360 // cuts

    units = w.w_up.shape[2]
    filler = grad_ffn(2 if fill else 1)
    if not fill:
        yield from filler
    normed_attn = st.normed_attn[...]
    yield next(filler, 0)
    add(g.gain_attn, column_sum(grad_middle * normed_attn))
    add(g.shift_attn, column_sum(grad_middle))
    if fill:
        yield 100
        yield next(filler, 0)
    grad_normed = grad_middle * row(w.gain_attn)
    mean_grad, mean_both = mean(grad_normed), mean(grad_normed * normed_attn)
    if fill:
        yield 150
        yield next(filler, 0)
    grad_resid = st.inverse[:, 0:1] * (grad_normed - mean_grad - normed_attn * mean_both)
    grad_attn = grad_resid.astype(BF16)
    if fill:
        yield 150
    yield from filler
    rest.attn[place, :] = grad_attn[main:]
    add(g.b_out, column_sum(grad_attn))
    yield 50
    add(g.w_out, dot_tn(st.context[:main, :], grad_attn[:main]))
    scale = jnp.concatenate([jnp.broadcast_to(st.scale[h : h + 1, :], (width, main)) for h in range(HEADS)], axis=0)
    grad_context_t = (dot_nt(w.w_out[at(w, layer)], grad_attn[:main]) * scale).astype(BF16)
    grad_context = grad_context_t.T
    product = grad_context_t.astype(F32) * st.context_t[...]
    q, k, v = st.query[...], st.key[...], st.value[...]
    k_t = k[:main].T
    yield 400
    def last_rows(out):
        grad_spread = spread_heads(dot_nt(grad_attn[main:], w.w_out[at(w, layer)]).astype(BF16), width)
        p_rest = st.prob_rest[...]
        p_rest_wide = p_rest.astype(F32)
        yield 60
        grad_p = dot_nt(v, grad_spread)
        out.append(dot(p_rest, grad_spread))
        yield 100
        centre = jnp.sum(p_rest_wide * grad_p, axis=0, keepdims=True) / jnp.sum(p_rest_wide, axis=0, keepdims=True)
        yield 100
        grad_s = (p_rest_wide * (grad_p - centre)).astype(BF16)
        yield 60
        out.append(dot(grad_s, spread_heads(q[main:], width)))
        yield 60
        out.append(fold_heads(dot_tn(grad_s, k), width).astype(BF16))
        yield 60

    left = lax.broadcasted_iota(jnp.int32, (full, 2 * width), 1) < width
    q_parts, k_parts, v_parts, bottoms = [], [], [], []

    def first_rows():
        for h in range(0, HEADS, 2):
            pair = slice(width * h, width * (h + 2))
            for i in (h, h + 1):
                own = slice(i * width, (i + 1) * width)
                grad_p = dot(own_half(v[:, pair], i, width), grad_context_t[pair, :])
                yield 130
                grad_s = st.prob[i].astype(F32) * (grad_p - jnp.sum(product[own, :], axis=0, keepdims=True))
                grad_s = grad_s.astype(BF16)
                grad_s_ref[i] = grad_s
                yield 140
                q_parts.append(dot(k_t[own, :], grad_s[:main]))
                bottoms.append(grad_s[main:])
                yield 130
            both = dot(st.prob[h : h + 2].reshape(2 * full, main), grad_context[:, pair])
            v_parts.append(jnp.where(left, both[:full], both[full:]))
            yield 350
            both = dot(grad_s_ref[h : h + 2].reshape(2 * full, main), q[:main, pair])
            k_parts.append(jnp.where(left, both[:full], both[full:]))
            yield 350

    at_last = []
    yield from woven((last_rows(at_last), 500), (first_rows(), 3000))
    grad_v, grad_k, grad_q_rest = at_last
    grad_v = (grad_v + jnp.concatenate(v_parts, axis=1)).astype(BF16)
    grad_k = (grad_k + jnp.concatenate(k_parts, axis=1)).astype(BF16)
    grad_q_t = jnp.concatenate(q_parts, axis=0)
    grad_q_t = grad_q_t + dot_tn(spread_heads(k[main:], width), jnp.concatenate(bottoms, axis=0))
    grad_q = jnp.concatenate([grad_q_t.astype(BF16).T, grad_q_rest], axis=0) * BF16(0.125)
    rest.x[place, :] = st.x[main:, :]
    rest.query[place, :] = grad_q[main:]
    rest.key[place, :] = grad_k[main:]
    rest.value[place, :] = grad_v[main:]
    add(g.b_query, column_sum(grad_q))
    add(g.b_value, column_sum(grad_v))
    yield 400
    x_main = st.x[:main, :]
    add(g.w_query, dot_tn(x_main, grad_q[:main]))
    add(g.w_key, dot_tn(x_main, grad_k[:main]))
    add(g.w_value, dot_tn(x_main, grad_v[:main]))
    yield 400
    result.append(
        grad_resid
        + dot_nt(grad_q, w.w_query[at(w, layer)])
        + dot_nt(grad_k, w.w_key[at(w, layer)])
        + dot_nt(grad_v, w.w_value[at(w, layer)])
    )
    yield 300


def add_rest(g, rest):
    def add(ref, left, right):
        ref[...] += dot_tn(left[...], right[...])

    add(g.w_query, rest.x, rest.query)
    add(g.w_key, rest.x, rest.key)
    add(g.w_value, rest.x, rest.value)
    add(g.w_out, rest.context, rest.attn)
    units, features = g.w_down.shape

    @pl.loop(0, units // features)
    def _(c):
        part = pl.ds(pl.multiple_of(c * features, features), features)
        g.w_up[part, :] += dot_tn(rest.up[:, part], rest.middle[...])
        g.w_down[part, :] += dot_tn(rest.active[:, part], rest.branch[...])


FORWARD, BACKWARD = 7600, 8650


def squares(g):
    return (g.w_query, g.w_key, g.w_value, g.w_out)


def lines(g):
    return (g.b_query, g.b_value, g.b_out, g.gain_attn, g.shift_attn, g.b_down, g.gain_ffn, g.shift_ffn)


def packed_rows(features, units):
    used = 4 * features + 2 * units + len(lines(Weights(*range(len(Weights._fields))))) + units // features
    return -(-used // (PIECES * TILE)) * PIECES * TILE


def spans(sizes, rows):
    piece = rows // PIECES
    out, at = [], 0
    for index, size in enumerate(sizes):
        done = 0
        while done < size:
            take = min(size - done, piece - at % piece)
            out.append((index, done, at // piece, at % piece, take))
            done, at = done + take, at + take
    return out


def emit(g, keep, send, ordered, me):
    units, features = g.w_down.shape
    rows = ordered.shape[0]
    piece = rows // PIECES
    chunks = units // features
    arrays = squares(g) + (g.w_up, g.w_down)
    last = [ref[...] for ref in lines(g)]
    last += [g.b_up[:, c * features : (c + 1) * features] for c in range(chunks)]
    sizes = [ref.shape[0] for ref in arrays]
    left = rows - sum(sizes)
    last.append(jnp.zeros((left - len(last), features), F32))
    tail = jnp.concatenate(last, axis=0).astype(BF16)
    for index, start, which, offset, take in spans(sizes + [left], rows):
        if index < len(arrays):
            value = arrays[index][start : start + take, :].astype(BF16)
        else:
            value = tail[start : start + take]
        at = pl.multiple_of((which ^ me) * piece, TILE) + offset
        ordered[pl.ds(pl.multiple_of(at, TILE), take), :] = value
    half = rows // 2
    keep[...] = ordered[:half, :]
    send[...] = ordered[half:, :]


def stash_shapes(full, features, units):
    main = full - TILE
    square = ((full, features), BF16)
    wide = ((full, units), BF16)
    exact = ((full, features), F32)
    return Stash(
        x=square,
        query=square,
        key=square,
        value=square,
        prob=((HEADS, full, main), BF16),
        prob_rest=((full, HEADS * TILE), BF16),
        scale=((HEADS, main), F32),
        context_t=((features, main), F32),
        context=square,
        inverse=((full, 2), F32),
        normed_attn=exact,
        middle=square,
        active=wide,
        slope=wide,
        normed_ffn=exact,
    )


def scratch(micro, full, features, units):
    square, line = (features, features), (1, features)
    sums = Weights(
        w_query=square, b_query=line, w_key=square, w_value=square, b_value=line, w_out=square, b_out=line,
        gain_attn=line, shift_attn=line, w_up=(units, features), b_up=(1, units), w_down=(units, features),
        b_down=line, gain_ffn=line, shift_ffn=line,
    )
    rest = Rest(*[(micro * TILE, features)] * 8, up=(micro * TILE, units), active=(micro * TILE, units))
    out = [pltpu.VMEM(size, F32) for size in sums] + [pltpu.VMEM(size, BF16) for size in rest]
    out.append(pltpu.VMEM((full, units), BF16))
    out.append(pltpu.VMEM((HEADS, full, full - TILE), BF16))
    out.append(pltpu.VMEM((packed_rows(features, units), features), BF16))
    return out


def take_scratch(refs):
    count = len(Weights._fields)
    g, refs = Weights(*refs[:count]), refs[count:]
    count = len(Rest._fields)
    return g, Rest(*refs[:count]), *refs[count:]


def weight_specs(weights, layer=None):
    specs = []
    for weight in weights:
        if layer is None:
            specs.append(whole())
        elif weight.ndim == 3:
            specs.append(pl.BlockSpec((1,) + weight.shape[1:], lambda m: (layer, 0, 0)))
        else:
            specs.append(pl.BlockSpec(weight.shape, lambda m: (0, 0)))
    return specs


def by_micro(shape):
    rank = len(shape)
    return pl.BlockSpec((1,) + tuple(shape[1:]), lambda m: (m,) + (0,) * (rank - 1))


def ahead(shape):
    rank, last = len(shape), shape[0] - 1
    return pl.BlockSpec((1,) + tuple(shape[1:]), lambda m: (jnp.minimum(m, last),) + (0,) * (rank - 1))


def behind(shape):
    rank = len(shape)
    return pl.BlockSpec((1,) + tuple(shape[1:]), lambda m: (jnp.maximum(m - 1, 0),) + (0,) * (rank - 1))


def fixed(shape):
    rank = len(shape)
    return pl.BlockSpec(tuple(shape), lambda m: (0,) * rank)


def whole():
    return pl.BlockSpec(memory_space=pltpu.VMEM)


def smem():
    return pl.BlockSpec(memory_space=pltpu.SMEM)


def lower_forward_kernel(x_ref, *refs):
    w, refs = Weights(*refs[: len(Weights._fields)]), refs[len(Weights._fields) :]
    out_ref, sent_ref, *refs = refs
    st = Stash(*[ref.at[0] for ref in refs[:-1]])
    padded = refs[-1]
    rows = x_ref.shape[1]
    main = padded.shape[0] - TILE
    padded[main:, :] = jnp.zeros((TILE, padded.shape[1]), BF16)
    padded[:rows, :] = x_ref[0]
    result = []
    weave((layer_forward(padded[...], 0, w, st, rows, result), 1))
    y = result[0].astype(BF16)
    out_ref[0] = y
    sent_ref[0] = y[main:]


def lower_forward(hidden, weights, full):
    micro, rows, features = hidden.shape
    outs = [jax.ShapeDtypeStruct((micro, full, features), BF16), jax.ShapeDtypeStruct((micro, TILE, features), BF16)]
    shapes = stash_shapes(full, features, weights.w_up.shape[2])
    outs += [jax.ShapeDtypeStruct((micro,) + shape, kind) for shape, kind in shapes]
    out, sent, *stash = pl.pallas_call(
        lower_forward_kernel,
        grid=(micro,),
        in_specs=[by_micro(hidden.shape)] + weight_specs(weights, 0),
        out_specs=[by_micro(o.shape) for o in outs],
        out_shape=outs,
        scratch_shapes=[pltpu.VMEM((full, features), BF16)],
        compiler_params=pltpu.CompilerParams(vmem_limit_bytes=56 * 2**20),
        name="lower_forward",
    )(hidden, *weights)
    return out, sent, Stash(*stash)


def zero_sums(g):
    for ref in g:
        rows, features = ref.shape
        if rows == 1:
            ref[...] = jnp.zeros_like(ref)
        else:

            @pl.loop(0, rows // STRIP)
            def _(i, ref=ref, features=features):
                ref[pl.ds(pl.multiple_of(i * STRIP, STRIP), STRIP), :] = jnp.zeros((STRIP, features), F32)


def upper_forward(rows, lead, arrived, cot_ref, target_ref, slot_ref, count, x_ref, out_ref, grad_out, w, st):
    full, features = x_ref.shape[1:]
    memory = cot_ref.shape[1]
    main = full - TILE
    x = x_ref[0]
    is_read = lax.broadcasted_iota(jnp.int32, (TILE, features), 0) < memory
    moved = jnp.logical_and(is_read, jnp.logical_not(lead))
    x = jnp.concatenate([jnp.where(moved, arrived, x[:TILE]), x[TILE:]], axis=0)
    result = []
    yield from layer_forward(x, 1, w, st, rows, result)
    y = result[0]
    out_ref[0] = y[:rows].astype(BF16)
    slots = slot_ref.shape[2]
    slot_row = lax.broadcasted_iota(jnp.int32, (main, slots), 0) - memory
    slot_at = lax.broadcasted_iota(jnp.int32, (main, slots), 1)
    hit = jnp.logical_and(slot_row == slot_ref[0], slot_at < count)
    hit = jnp.where(hit, 1.0, 0.0).astype(BF16)
    used = dot(hit, jnp.ones((slots, features), BF16))
    wanted = dot(hit, target_ref[0])
    grad_out[:main, :] = (y[:main] * used - wanted) / count.astype(F32)
    grad_out[main : main + memory, :] = cot_ref[0].astype(F32)
    yield 300


def upper_backward(lead, memory, grad_out, grad_ref, back_ref, w, st, *refs, fill):
    result = []
    yield from layer_backward(grad_out[...], 1, w, st, *refs, result, fill)
    grad_in = result[0]
    is_read = lax.broadcasted_iota(jnp.int32, (TILE, grad_in.shape[1]), 0) < memory
    moved = jnp.logical_and(is_read, jnp.logical_not(lead))
    back_ref[0] = grad_in[:TILE].astype(BF16)
    grad_ref[0, :TILE, :] = jnp.where(moved, 0.0, grad_in[:TILE])
    grad_ref[0, TILE:, :] = grad_in[TILE:]


def upper_kernel(rows, micro, bits, count_ref, x_ref, arrived_ref, cot_ref, target_ref, slot_ref, *refs):
    step = pl.program_id(0)
    w, refs = Weights(*refs[: len(Weights._fields)]), refs[len(Weights._fields) :]
    out_ref, grad_ref, back_ref, keep_ref, send_ref = refs[:5]
    refs = refs[5:]
    st, refs = Stash(*refs[: len(Stash._fields)]), refs[len(Stash._fields) :]
    grad_out, *refs = refs
    g, rest, grad_up_ref, grad_s_ref, ordered = take_scratch(refs)
    memory = cot_ref.shape[1]
    lead = lax.axis_index(LINE) == 0

    def turn(slot):
        twice = Stash(*[ref if ref.shape[0] != 2 else ref.at[slot] for ref in st])
        return twice

    def forward(slot):
        now = jnp.minimum(step, micro - 1)
        count, arrived = count_ref[now], arrived_ref[now]
        return upper_forward(
            rows, lead, arrived, cot_ref, target_ref, slot_ref, count, x_ref, out_ref, grad_out, w, turn(slot)
        )

    def backward(slot, fill):
        refs = (g, rest, grad_up_ref, grad_s_ref, step - 1)
        return upper_backward(lead, memory, grad_out, grad_ref, back_ref, w, turn(slot), *refs, fill=fill)

    @pl.when(step == 0)
    def _():
        zero_sums(g)
        grad_out[grad_out.shape[0] - TILE :, :] = jnp.zeros((TILE, grad_out.shape[1]), F32)
        weave((forward(0), FORWARD))

    @pl.when(jnp.logical_and(step > 0, step < micro))
    def _():
        slot = lax.rem(step, 2)
        weave((forward(slot), FORWARD), (backward(1 - slot, True), BACKWARD))

    @pl.when(step == micro)
    def _():
        weave((backward((micro - 1) % 2, False), BACKWARD))
        add_rest(g, rest)
        emit(g, keep_ref, send_ref, ordered, place_of(bits))


def half_packed(features, units):
    return jax.ShapeDtypeStruct((packed_rows(features, units) // 2, features), BF16)


def upper_both(bits, counts, x, arrived, cotangent, targets, slots, weights, rows):
    micro, full, features = x.shape
    units = weights.w_up.shape[2]
    outs = [
        jax.ShapeDtypeStruct((micro, rows, features), BF16),
        jax.ShapeDtypeStruct(x.shape, F32),
        jax.ShapeDtypeStruct((micro, TILE, features), BF16),
        half_packed(features, units),
        half_packed(features, units),
    ]
    ins = (x, arrived, cotangent, targets, slots)
    shapes = stash_shapes(full, features, units)
    once = (shapes.inverse, shapes.normed_attn, shapes.middle, shapes.active, shapes.slope, shapes.normed_ffn)
    stash = [pltpu.VMEM(s if (s, k) in once and (s, k) != shapes.x else (2,) + s, k) for s, k in shapes] + [pltpu.VMEM((full, features), F32)]
    return pl.pallas_call(
        functools.partial(upper_kernel, rows, micro, bits),
        grid=(micro + 1,),
        in_specs=[smem()] + [whole() if a is arrived else ahead(a.shape) for a in ins] + weight_specs(weights),
        out_specs=[ahead(outs[0].shape), behind(outs[1].shape), behind(outs[2].shape)]
        + [fixed(o.shape) for o in outs[3:]],
        out_shape=outs,
        scratch_shapes=stash + scratch(micro, full, features, units),
        compiler_params=pltpu.CompilerParams(vmem_limit_bytes=52 * 2**20),
        name="upper_both",
    )(counts, *ins, *weights)


def lower_backward_kernel(memory, bits, grad_ref, back_ref, *refs):
    step, steps = pl.program_id(0), pl.num_programs(0)
    w, refs = Weights(*refs[: len(Weights._fields)]), refs[len(Weights._fields) :]
    st, refs = Stash(*[ref.at[0] for ref in refs[: len(Stash._fields)]]), refs[len(Stash._fields) :]
    out_ref, keep_ref, send_ref, *refs = refs
    g, rest, grad_up_ref, grad_s_ref, ordered = take_scratch(refs)
    full, features = grad_ref.shape[1:]
    main = full - TILE

    @pl.when(step == 0)
    def _():
        zero_sums(g)

    is_write = lax.broadcasted_iota(jnp.int32, (TILE, features), 0) < memory
    returned = jnp.where(is_write, back_ref[step].astype(F32), 0.0)
    grad_out = jnp.concatenate([grad_ref[0, :main, :], grad_ref[0, main:, :] + returned], axis=0)
    result = []
    weave((layer_backward(grad_out, 0, w, st, g, rest, grad_up_ref, grad_s_ref, step, result), 1))
    out_ref[0] = result[0][: out_ref.shape[1]].astype(BF16)

    @pl.when(step == steps - 1)
    def _():
        add_rest(g, rest)
        emit(g, keep_ref, send_ref, ordered, place_of(bits))


def lower_backward(bits, grad, back, weights, stash, rows, memory):
    micro, full, features = grad.shape
    units = weights.w_up.shape[2]
    outs = [
        jax.ShapeDtypeStruct((micro, rows, features), BF16),
        half_packed(features, units),
        half_packed(features, units),
    ]
    return pl.pallas_call(
        functools.partial(lower_backward_kernel, memory, bits),
        grid=(micro,),
        in_specs=[by_micro(grad.shape), whole()]
        + weight_specs(weights)
        + [by_micro(a.shape) for a in stash],
        out_specs=[by_micro(outs[0].shape)] + [fixed(o.shape) for o in outs[1:]],
        out_shape=outs,
        scratch_shapes=scratch(micro, full, features, units),
        compiler_params=pltpu.CompilerParams(vmem_limit_bytes=52 * 2**20),
        name="lower_backward",
    )(grad, back, *weights, *stash)


def unpack_kernel(bits, *refs):
    sources, refs = refs[:4], refs[4:]
    out, refs = Weights(*refs[: len(Weights._fields)]), refs[len(Weights._fields) :]
    ordered, *staged, in_sems, out_sems, line_sems = refs
    features, units = out.w_up.shape[1:]
    chunks = units // features
    half = sources[0].shape[0]
    rows, piece = 2 * half, 2 * half // PIECES
    arrays = squares(out) + (out.w_up, out.w_down)
    names = lines(out) + (out.b_up,)
    short = staged[len(arrays) :]
    loads = [
        pltpu.make_async_copy(source, ordered.at[i // 2, (i % 2) * half : (i % 2 + 1) * half], in_sems.at[i])
        for i, source in enumerate(sources)
    ]
    for load in loads:
        load.start()
    sizes = [features] * 4 + [units, units]
    sizes.append(rows - sum(sizes))
    me = place_of(bits)

    def store(index, layer):
        return pltpu.make_async_copy(staged[index].at[layer], arrays[index].at[layer], out_sems.at[layer, index])

    @pl.loop(0, 2)
    def _(layer):
        for i in range(2):

            @pl.when(layer == i)
            def _(i=i):
                loads[2 * i].wait()
                loads[2 * i + 1].wait()

        for index, start, which, offset, take in spans(sizes, rows):
            at = pl.multiple_of((which ^ me) * piece, TILE) + offset
            value = ordered[layer, pl.ds(pl.multiple_of(at, TILE), take), :]
            if index == 4:
                staged[index][layer, :, start : start + take] = value.T.astype(F32)
            elif index < 6:
                staged[index][layer, start : start + take, :] = value.astype(F32)
            else:
                value = value.astype(F32)
                for i, ref in enumerate(short[:-1]):
                    ref[pl.ds(layer, 1), :] = value[i : i + 1]
                for c in range(chunks):
                    i = len(short) - 1 + c
                    short[-1][pl.ds(layer, 1), c * features : (c + 1) * features] = value[i : i + 1]
            if index < 6 and start + take == sizes[index]:
                store(index, layer).start()

    line_stores = [pltpu.make_async_copy(near, far, line_sems.at[i]) for i, (near, far) in enumerate(zip(short, names))]
    for copy in line_stores:
        copy.start()
    for layer in range(2):
        for index in range(6):
            store(index, layer).wait()
    for copy in line_stores:
        copy.wait()


def unpack(bits, parts, weights):
    outs = [jax.ShapeDtypeStruct(weight.shape, F32) for weight in weights]
    shapes = Weights(*outs)
    large = squares(shapes) + (shapes.w_up, shapes.w_down)
    short = lines(shapes) + (shapes.b_up,)
    return pl.pallas_call(
        functools.partial(unpack_kernel, bits),
        in_specs=[pl.BlockSpec(memory_space=pl.ANY)] * 4,
        out_specs=[pl.BlockSpec(memory_space=pl.ANY) for _ in outs],
        out_shape=outs,
        scratch_shapes=[pltpu.VMEM((2, 2 * parts[0].shape[0], parts[0].shape[1]), BF16)]
        + [pltpu.VMEM(o.shape, F32) for o in large + short]
        + [pltpu.SemaphoreType.DMA((4,)), pltpu.SemaphoreType.DMA((2, 6)), pltpu.SemaphoreType.DMA((len(short),))],
        compiler_params=pltpu.CompilerParams(vmem_limit_bytes=20 * 2**20),
        name="unpack",
    )(*parts)


def from_behind(value, axis, steps):
    count = lax.axis_size(axis)
    initial, last = (max(0, -steps), min(count, count - steps))
    return lax.ppermute(value, axis, [(source, source + steps) for source in range(initial, last)])


def swap(value, bit):
    axis, step = bit
    return lax.ppermute(value, axis, [(i, i ^ step) for i in range(lax.axis_size(axis))])


def plus(a, b):
    return (a.astype(F32) + b.astype(F32)).astype(BF16)


def place_of(bits):
    me = jnp.int32(0)
    for axis, step in bits:
        me = me * 2 + lax.rem(lax.div(lax.axis_index(axis), step), 2)
    return me


def sum_rest(value, bits):
    axis, step = bits[0]
    me = (lax.axis_index(axis) // step) % 4

    def across(part, k):
        return lax.ppermute(part, axis, [(i, i ^ (k * step)) for i in range(lax.axis_size(axis))])

    rows = value.shape[0] // 4
    quarter = [lax.dynamic_slice_in_dim(value, (me ^ k) * rows, rows) for k in range(4)]
    got = [across(quarter[k], k) for k in (1, 2, 3)]
    kept = quarter[0].astype(F32)
    for part in got:
        kept = kept + part.astype(F32)
    kept = kept.astype(BF16)
    for bit in bits[2:]:
        kept = plus(kept, swap(kept, bit))
    a, b, c, d = [kept] + [across(kept, k) for k in (1, 2, 3)]
    odd, high = me % 2 == 1, me >= 2
    first, second = jnp.where(odd, b, a), jnp.where(odd, a, b)
    third, fourth = jnp.where(odd, d, c), jnp.where(odd, c, d)
    lower, upper = jnp.concatenate([first, second], axis=0), jnp.concatenate([third, fourth], axis=0)
    return jnp.where(high, jnp.concatenate([upper, lower], axis=0), jnp.concatenate([lower, upper], axis=0))


def sum_all(halves, core, along, across, rest_bits, others):
    def to(part, j):
        swaps = [(axis, step) for (axis, step), used in ((across, j % 2), (along, j // 2)) if used]
        sizes = [lax.axis_size(axis) for axis in (LINE, PAIR)]
        line = sum(step for axis, step in swaps if axis == LINE)
        pair = sum(step for axis, step in swaps if axis == PAIR)
        perm = [(i * sizes[1] + k, (i ^ line) * sizes[1] + (k ^ pair)) for i in range(sizes[0]) for k in range(sizes[1])]
        return lax.ppermute(part, (LINE, PAIR), perm)

    chains = [plus(keep, swap(send, core)) for keep, send in halves]
    rows = chains[0].shape[0] // 4
    for i, kept in enumerate(chains):
        got = [to(kept[j * rows : (j + 1) * rows], j) for j in (3, 1, 2)]
        chains[i] = sum([part.astype(F32) for part in got], kept[:rows].astype(F32)).astype(BF16)
    chains = [sum_rest(kept, rest_bits) for kept in chains]
    others, chains[0] = lax.optimization_barrier((others, chains[0]))
    chains = [jnp.concatenate([kept] + [to(kept, j) for j in (1, 2, 3)], axis=0) for kept in chains]
    others = [with_layout_constraint(jnp.transpose(v, (1, 0, 2)), Layout((0, 1, 2))) for v in others]
    others, chains[0] = lax.optimization_barrier((others, chains[0]))
    return [part for kept in chains for part in (kept, swap(kept, core))], others


def local(hidden, write_cotangent, targets, positions, counts, *weights):
    weights = Weights(*weights)
    micro, _, _, rows, features = hidden.shape
    memory = write_cotangent.shape[3]
    full = -(-rows // TILE) * TILE
    bits = [(axis, 1 << i) for axis in (LINE, PAIR) for i in range(lax.axis_size(axis).bit_length() - 1)]
    core, along, across = (LINE, 1), (LINE, 2), (PAIR, 1)
    piece_bits = (core, along, across)
    rest_bits = [bit for bit in bits if bit not in piece_bits]

    hidden_rows = hidden.reshape(micro, rows, features)
    lower_out, sent, stash = lower_forward(hidden_rows, weights, full)
    arrived = from_behind(sent, LINE, 1)
    out, grad, back, *upper = upper_both(
        piece_bits,
        counts.reshape(micro),
        lower_out,
        arrived,
        write_cotangent.reshape(micro, memory, features),
        targets.reshape(micro, targets.shape[3], features),
        positions.reshape(micro, 1, positions.shape[3]),
        weights,
        rows,
    )
    returned = from_behind(back, LINE, -1)
    grad_in, *lower = lower_backward(piece_bits, grad, returned, weights, stash, rows, memory)
    parts, (out, grad_in) = sum_all((lower, upper), core, along, across, rest_bits, (out, grad_in))
    grads = unpack(piece_bits, parts, weights)
    out, grad_in = (jnp.transpose(v, (1, 0, 2)).reshape(hidden.shape) for v in (out, grad_in))
    return (out, grad_in) + tuple(grads)


def solution(mesh):
    split = P(None, PAIR, LINE, None, None)
    placed = (split, split, split, P(None, PAIR, LINE, None), P(None, PAIR, LINE))
    count = len(Weights._fields)
    return jax.shard_map(
        local,
        mesh=mesh,
        in_specs=placed + (P(),) * count,
        out_specs=(split, split) + (P(),) * count,
        check_vma=False,
    )
```

```python
import functools
from typing import Any, NamedTuple

import jax
import jax.numpy as jnp
from jax import lax
from jax.experimental import pallas as pl
from jax.experimental.layout import Layout, with_layout_constraint
from jax.experimental.pallas import tpu as pltpu
from jax.sharding import PartitionSpec as P

EPSILON = 1e-12
DENSITY = 0.3989422804014327
ROOT_HALF = 0.7071067811865476
BELL = -0.7213475204444817
LOG2_E = 1.4426950408889634
HEADS = 4
TILE = 16
STRIP = 64
PIECES = 8
LOW = -1e30
F32, BF16 = jnp.float32, jnp.bfloat16
LINE, PAIR = "seg", "item"


class Weights(NamedTuple):
    w_query: Any
    b_query: Any
    w_key: Any
    w_value: Any
    b_value: Any
    w_out: Any
    b_out: Any
    gain_attn: Any
    shift_attn: Any
    w_up: Any
    b_up: Any
    w_down: Any
    b_down: Any
    gain_ffn: Any
    shift_ffn: Any


class Stash(NamedTuple):
    x: Any
    query: Any
    key: Any
    value: Any
    prob: Any
    prob_rest: Any
    scale: Any
    context_t: Any
    context: Any
    inverse: Any
    normed_attn: Any
    middle: Any
    active: Any
    slope: Any
    normed_ffn: Any


class Rest(NamedTuple):
    x: Any
    query: Any
    key: Any
    value: Any
    context: Any
    attn: Any
    middle: Any
    branch: Any
    up: Any
    active: Any


def dot(a, b):
    return jnp.dot(a, b, preferred_element_type=F32)


def dot_nt(a, b):
    return lax.dot_general(a, b, (((1,), (1,)), ((), ())), preferred_element_type=F32)


def dot_tn(a, b):
    return lax.dot_general(a, b, (((0,), (0,)), ((), ())), preferred_element_type=F32)


def mean(v):
    return jnp.mean(v, axis=-1, keepdims=True)


def column_sum(v):
    return jnp.sum(v.astype(F32), axis=0, keepdims=True)


def normalize(v):
    centred = v - mean(v)
    inverse = lax.rsqrt(mean(centred * centred) + EPSILON)
    return centred * inverse, inverse


def norm_back(grad, normed, inverse):
    return inverse * (grad - mean(grad) - normed * mean(grad * normed))


def head_block(shape, width):
    rows = lax.div(lax.broadcasted_iota(jnp.int32, shape, 0), TILE)
    lanes = lax.div(lax.broadcasted_iota(jnp.int32, shape, 1), width)
    return rows == lanes


def spread_heads(rest, width):
    tiled = jnp.concatenate([rest] * HEADS, axis=0)
    return jnp.where(head_block(tiled.shape, width), tiled, jnp.zeros_like(tiled))


def fold_heads(spread, width):
    own = jnp.where(head_block(spread.shape, width), spread, 0.0)
    return own[:TILE] + own[TILE : 2 * TILE] + own[2 * TILE : 3 * TILE] + own[3 * TILE :]


def own_half(pair, h, width):
    lanes = lax.div(lax.broadcasted_iota(jnp.int32, pair.shape, 1), width)
    return jnp.where(lanes == h % 2, pair, jnp.zeros_like(pair))


def weigh_keys(s, live_rest):
    main = s.shape[0] - TILE
    top, bottom = s[:main], jnp.where(live_rest, s[main:], LOW)
    peak = jnp.maximum(jnp.max(top, axis=0, keepdims=True), jnp.max(bottom, axis=0, keepdims=True))
    yield 120
    top = jnp.exp2(top - peak).astype(BF16)
    yield 220
    return top, jnp.exp2(bottom - peak).astype(BF16)


def woven(*tasks):
    tasks = [[task, 0.0, total] for task, total in tasks]
    while tasks:
        task = min(tasks, key=lambda t: t[1] / t[2])
        length = next(task[0], None)
        if length is None:
            tasks.remove(task)
        else:
            task[1] += length
            yield length


def weave(*tasks):
    for _ in woven(*tasks):
        pass


def at(w, layer):
    return layer if w.w_query.shape[0] > 1 else 0


def layer_forward(x, layer, w, st, rows, result):
    full, features = x.shape
    main = full - TILE
    width = features // HEADS

    def row(ref):
        return ref[layer : layer + 1, :]

    st.x[...] = x
    q = ((dot(x, w.w_query[at(w, layer)]) + row(w.b_query)) * (0.125 * LOG2_E)).astype(BF16)
    yield 150
    k = dot(x, w.w_key[at(w, layer)]).astype(BF16)
    yield 150
    v = (dot(x, w.w_value[at(w, layer)]) + row(w.b_value)).astype(BF16)
    st.query[...] = q
    st.key[...] = k
    st.value[...] = v
    yield 150
    q_t = q[:main].T
    v_t = v[:main].T
    live_rest = lax.broadcasted_iota(jnp.int32, (TILE, 1), 0) < rows - main
    def last_rows(out):
        top, bottom = yield from weigh_keys(dot_nt(k, spread_heads(q[main:], width)), live_rest)
        p_rest = jnp.concatenate([top, bottom], axis=0)
        p_rest = (p_rest.astype(F32) * (1.0 / column_sum(p_rest))).astype(BF16)
        st.prob_rest[...] = p_rest
        yield 50
        out.append(fold_heads(dot_tn(p_rest, v), width).astype(BF16))
        yield 50

    ones = jnp.ones((TILE, main), BF16)
    scores, weights, parts, bottoms, scales = {}, {}, [], [], []

    def first_rows():
        for h in range(-1, HEADS + 1):
            if h + 1 < HEADS:
                pair = slice(2 * width * ((h + 1) // 2), 2 * width * ((h + 1) // 2 + 1))
                scores[h + 1] = dot(own_half(k[:, pair], h + 1, width), q_t[pair, :])
                yield 80
            if h > 0:
                top, bottom = weights.pop(h - 1)
                part = dot(jnp.concatenate([v_t[(h - 1) * width : h * width, :], ones], axis=0), top)
                parts.append(part[:width])
                bottoms.append(bottom)
                scale = 1.0 / (part[width : width + 1] + column_sum(bottom))
                st.scale[h - 1 : h, :] = scale
                scales.append(jnp.broadcast_to(scale, (width, main)))
                yield 80
            if 0 <= h < HEADS:
                top, bottom = yield from weigh_keys(scores.pop(h), live_rest)
                st.prob[h, :main, :] = top
                st.prob[h, main:, :] = bottom
                weights[h] = top, bottom
                yield 60

    at_last = []
    yield from woven((last_rows(at_last), 450), (first_rows(), 2600))
    (context_rest,) = at_last
    context_t = jnp.concatenate(parts, axis=0)
    context_t = context_t + dot_tn(spread_heads(v[main:], width), jnp.concatenate(bottoms, axis=0))
    context_t = context_t * jnp.concatenate(scales, axis=0)
    st.context_t[...] = context_t
    context = jnp.concatenate([context_t.astype(BF16).T, context_rest], axis=0)
    st.context[...] = context
    yield 200
    normed_attn, inverse_attn = normalize(x.astype(F32) + dot(context, w.w_out[at(w, layer)]) + row(w.b_out))
    st.normed_attn[...] = normed_attn
    middle = normed_attn * row(w.gain_attn) + row(w.shift_attn)
    middle_low = middle.astype(BF16)
    st.middle[...] = middle_low
    total = middle + row(w.b_down)
    yield 400
    chunks = w.w_up.shape[2] // features

    def upward(c):
        part = slice(c * features, (c + 1) * features)
        return dot(middle_low, w.w_up[at(w, layer), :, part]) + w.b_up[layer : layer + 1, part]

    ahead = upward(0)
    for c in range(chunks):
        part = slice(c * features, (c + 1) * features)
        u, ahead = ahead, (upward(c + 1) if c + 1 < chunks else None)
        yield 50
        phi = 0.5 + 0.5 * lax.erf(u * ROOT_HALF)
        active = (u * phi).astype(BF16)
        st.active[:, part] = active
        yield 200
        slope = phi + u * (jnp.exp2(u * u * BELL) * DENSITY)
        st.slope[:, part] = slope.astype(BF16)
        yield 220
        total = total + dot(active, w.w_down[at(w, layer), part, :])
        yield 80
    normed_ffn, inverse_ffn = normalize(total)
    st.normed_ffn[...] = normed_ffn
    st.inverse[:, 0:1] = inverse_attn
    st.inverse[:, 1:2] = inverse_ffn
    result.append(normed_ffn * row(w.gain_ffn) + row(w.shift_ffn))
    yield 400


def layer_backward(grad_out, layer, w, st, g, rest, grad_up_ref, grad_s_ref, step, result, fill=False):
    full, features = st.x.shape
    main = full - TILE
    width = features // HEADS
    place = pl.ds(pl.multiple_of(step * TILE, TILE), TILE)

    def row(ref):
        return ref[layer : layer + 1, :]

    def add(ref, value):
        ref[...] += value

    normed_ffn = st.normed_ffn[...]
    add(g.gain_ffn, column_sum(grad_out * normed_ffn))
    add(g.shift_ffn, column_sum(grad_out))
    grad_sum = norm_back(grad_out * row(w.gain_ffn), normed_ffn, st.inverse[:, 1:2])
    grad_branch = grad_sum.astype(BF16)
    rest.branch[place, :] = grad_branch[main:]
    add(g.b_down, column_sum(grad_branch))
    grad_middle = grad_sum
    yield 500
    for c in range(w.w_up.shape[2] // features):
        part = slice(c * features, (c + 1) * features)
        grad_up = dot_nt(grad_branch, w.w_down[at(w, layer), part, :]) * st.slope[:, part].astype(F32)
        grad_up = grad_up.astype(BF16)
        yield 150
        grad_up_ref[:, part] = grad_up
        g.b_up[:, part] += column_sum(grad_up)
        grad_middle = grad_middle + dot_nt(grad_up, w.w_up[at(w, layer), :, part])
        yield 150
    rest.middle[place, :] = st.middle[main:, :]
    rest.up[place, :] = grad_up_ref[main:, :]
    rest.active[place, :] = st.active[main:, :]
    rest.context[place, :] = st.context[main:, :]

    def grad_ffn(cuts):
        for cut in range(cuts):
            part = slice(cut * units // cuts, (cut + 1) * units // cuts)
            g.w_down[part, :] += dot_tn(st.active[:main, part], grad_branch[:main])
            yield 360 // cuts
            g.w_up[part, :] += dot_tn(grad_up_ref[:main, part], st.middle[:main, :])
            yield 360 // cuts

    units = w.w_up.shape[2]
    filler = grad_ffn(2 if fill else 1)
    if not fill:
        yield from filler
    normed_attn = st.normed_attn[...]
    yield next(filler, 0)
    add(g.gain_attn, column_sum(grad_middle * normed_attn))
    add(g.shift_attn, column_sum(grad_middle))
    if fill:
        yield 100
        yield next(filler, 0)
    grad_normed = grad_middle * row(w.gain_attn)
    mean_grad, mean_both = mean(grad_normed), mean(grad_normed * normed_attn)
    if fill:
        yield 150
        yield next(filler, 0)
    grad_resid = st.inverse[:, 0:1] * (grad_normed - mean_grad - normed_attn * mean_both)
    grad_attn = grad_resid.astype(BF16)
    if fill:
        yield 150
    yield from filler
    rest.attn[place, :] = grad_attn[main:]
    add(g.b_out, column_sum(grad_attn))
    yield 50
    add(g.w_out, dot_tn(st.context[:main, :], grad_attn[:main]))
    scale = jnp.concatenate([jnp.broadcast_to(st.scale[h : h + 1, :], (width, main)) for h in range(HEADS)], axis=0)
    grad_context_t = (dot_nt(w.w_out[at(w, layer)], grad_attn[:main]) * scale).astype(BF16)
    grad_context = grad_context_t.T
    product = grad_context_t.astype(F32) * st.context_t[...]
    q, k, v = st.query[...], st.key[...], st.value[...]
    k_t = k[:main].T
    yield 400
    def last_rows(out):
        grad_spread = spread_heads(dot_nt(grad_attn[main:], w.w_out[at(w, layer)]).astype(BF16), width)
        p_rest = st.prob_rest[...]
        p_rest_wide = p_rest.astype(F32)
        yield 60
        grad_p = dot_nt(v, grad_spread)
        out.append(dot(p_rest, grad_spread))
        yield 100
        centre = jnp.sum(p_rest_wide * grad_p, axis=0, keepdims=True) / jnp.sum(p_rest_wide, axis=0, keepdims=True)
        yield 100
        grad_s = (p_rest_wide * (grad_p - centre)).astype(BF16)
        yield 60
        out.append(dot(grad_s, spread_heads(q[main:], width)))
        yield 60
        out.append(fold_heads(dot_tn(grad_s, k), width).astype(BF16))
        yield 60

    left = lax.broadcasted_iota(jnp.int32, (full, 2 * width), 1) < width
    q_parts, k_parts, v_parts, bottoms = [], [], [], []

    def first_rows():
        for h in range(0, HEADS, 2):
            pair = slice(width * h, width * (h + 2))
            for i in (h, h + 1):
                own = slice(i * width, (i + 1) * width)
                grad_p = dot(own_half(v[:, pair], i, width), grad_context_t[pair, :])
                yield 130
                grad_s = st.prob[i].astype(F32) * (grad_p - jnp.sum(product[own, :], axis=0, keepdims=True))
                grad_s = grad_s.astype(BF16)
                grad_s_ref[i] = grad_s
                yield 140
                q_parts.append(dot(k_t[own, :], grad_s[:main]))
                bottoms.append(grad_s[main:])
                yield 130
            both = dot(st.prob[h : h + 2].reshape(2 * full, main), grad_context[:, pair])
            v_parts.append(jnp.where(left, both[:full], both[full:]))
            yield 350
            both = dot(grad_s_ref[h : h + 2].reshape(2 * full, main), q[:main, pair])
            k_parts.append(jnp.where(left, both[:full], both[full:]))
            yield 350

    at_last = []
    yield from woven((last_rows(at_last), 500), (first_rows(), 3000))
    grad_v, grad_k, grad_q_rest = at_last
    grad_v = (grad_v + jnp.concatenate(v_parts, axis=1)).astype(BF16)
    grad_k = ((grad_k + jnp.concatenate(k_parts, axis=1)) * (1.0 / LOG2_E)).astype(BF16)
    grad_q_t = jnp.concatenate(q_parts, axis=0)
    grad_q_t = grad_q_t + dot_tn(spread_heads(k[main:], width), jnp.concatenate(bottoms, axis=0))
    grad_q = jnp.concatenate([grad_q_t.astype(BF16).T, grad_q_rest], axis=0) * BF16(0.125)
    rest.x[place, :] = st.x[main:, :]
    rest.query[place, :] = grad_q[main:]
    rest.key[place, :] = grad_k[main:]
    rest.value[place, :] = grad_v[main:]
    add(g.b_query, column_sum(grad_q))
    add(g.b_value, column_sum(grad_v))
    yield 400
    x_main = st.x[:main, :]
    add(g.w_query, dot_tn(x_main, grad_q[:main]))
    add(g.w_key, dot_tn(x_main, grad_k[:main]))
    add(g.w_value, dot_tn(x_main, grad_v[:main]))
    yield 400
    result.append(
        grad_resid
        + dot_nt(grad_q, w.w_query[at(w, layer)])
        + dot_nt(grad_k, w.w_key[at(w, layer)])
        + dot_nt(grad_v, w.w_value[at(w, layer)])
    )
    yield 300


def add_rest(g, rest):
    def add(ref, left, right):
        ref[...] += dot_tn(left[...], right[...])

    add(g.w_query, rest.x, rest.query)
    add(g.w_key, rest.x, rest.key)
    add(g.w_value, rest.x, rest.value)
    add(g.w_out, rest.context, rest.attn)
    units, features = g.w_down.shape

    @pl.loop(0, units // features)
    def _(c):
        part = pl.ds(pl.multiple_of(c * features, features), features)
        g.w_up[part, :] += dot_tn(rest.up[:, part], rest.middle[...])
        g.w_down[part, :] += dot_tn(rest.active[:, part], rest.branch[...])


FORWARD, BACKWARD = 7600, 8650


def squares(g):
    return (g.w_query, g.w_key, g.w_value, g.w_out)


def lines(g):
    return (g.b_query, g.b_value, g.b_out, g.gain_attn, g.shift_attn, g.b_down, g.gain_ffn, g.shift_ffn)


def packed_rows(features, units):
    used = 4 * features + 2 * units + len(lines(Weights(*range(len(Weights._fields))))) + units // features
    return -(-used // (PIECES * TILE)) * PIECES * TILE


def spans(sizes, rows):
    piece = rows // PIECES
    out, at = [], 0
    for index, size in enumerate(sizes):
        done = 0
        while done < size:
            take = min(size - done, piece - at % piece)
            out.append((index, done, at // piece, at % piece, take))
            done, at = done + take, at + take
    return out


def emit(g, keep, send, ordered, me):
    units, features = g.w_down.shape
    rows = ordered.shape[0]
    piece = rows // PIECES
    chunks = units // features
    arrays = squares(g) + (g.w_up, g.w_down)
    last = [ref[...] for ref in lines(g)]
    last += [g.b_up[:, c * features : (c + 1) * features] for c in range(chunks)]
    sizes = [ref.shape[0] for ref in arrays]
    left = rows - sum(sizes)
    last.append(jnp.zeros((left - len(last), features), F32))
    tail = jnp.concatenate(last, axis=0).astype(BF16)
    for index, start, which, offset, take in spans(sizes + [left], rows):
        if index < len(arrays):
            value = arrays[index][start : start + take, :].astype(BF16)
        else:
            value = tail[start : start + take]
        at = pl.multiple_of((which ^ me) * piece, TILE) + offset
        ordered[pl.ds(pl.multiple_of(at, TILE), take), :] = value
    half = rows // 2
    keep[...] = ordered[:half, :]
    send[...] = ordered[half:, :]


def stash_shapes(full, features, units):
    main = full - TILE
    square = ((full, features), BF16)
    wide = ((full, units), BF16)
    exact = ((full, features), F32)
    return Stash(
        x=square,
        query=square,
        key=square,
        value=square,
        prob=((HEADS, full, main), BF16),
        prob_rest=((full, HEADS * TILE), BF16),
        scale=((HEADS, main), F32),
        context_t=((features, main), F32),
        context=square,
        inverse=((full, 2), F32),
        normed_attn=exact,
        middle=square,
        active=wide,
        slope=wide,
        normed_ffn=exact,
    )


def scratch(micro, full, features, units):
    square, line = (features, features), (1, features)
    sums = Weights(
        w_query=square, b_query=line, w_key=square, w_value=square, b_value=line, w_out=square, b_out=line,
        gain_attn=line, shift_attn=line, w_up=(units, features), b_up=(1, units), w_down=(units, features),
        b_down=line, gain_ffn=line, shift_ffn=line,
    )
    rest = Rest(*[(micro * TILE, features)] * 8, up=(micro * TILE, units), active=(micro * TILE, units))
    out = [pltpu.VMEM(size, F32) for size in sums] + [pltpu.VMEM(size, BF16) for size in rest]
    out.append(pltpu.VMEM((full, units), BF16))
    out.append(pltpu.VMEM((HEADS, full, full - TILE), BF16))
    out.append(pltpu.VMEM((packed_rows(features, units), features), BF16))
    return out


def take_scratch(refs):
    count = len(Weights._fields)
    g, refs = Weights(*refs[:count]), refs[count:]
    count = len(Rest._fields)
    return g, Rest(*refs[:count]), *refs[count:]


def weight_specs(weights, layer=None):
    specs = []
    for weight in weights:
        if layer is None:
            specs.append(whole())
        elif weight.ndim == 3:
            specs.append(pl.BlockSpec((1,) + weight.shape[1:], lambda m: (layer, 0, 0)))
        else:
            specs.append(pl.BlockSpec(weight.shape, lambda m: (0, 0)))
    return specs


def by_micro(shape):
    rank = len(shape)
    return pl.BlockSpec((1,) + tuple(shape[1:]), lambda m: (m,) + (0,) * (rank - 1))


def ahead(shape):
    rank, last = len(shape), shape[0] - 1
    return pl.BlockSpec((1,) + tuple(shape[1:]), lambda m: (jnp.minimum(m, last),) + (0,) * (rank - 1))


def behind(shape):
    rank = len(shape)
    return pl.BlockSpec((1,) + tuple(shape[1:]), lambda m: (jnp.maximum(m - 1, 0),) + (0,) * (rank - 1))


def fixed(shape):
    rank = len(shape)
    return pl.BlockSpec(tuple(shape), lambda m: (0,) * rank)


def whole():
    return pl.BlockSpec(memory_space=pltpu.VMEM)


def smem():
    return pl.BlockSpec(memory_space=pltpu.SMEM)


def lower_forward_kernel(x_ref, *refs):
    w, refs = Weights(*refs[: len(Weights._fields)]), refs[len(Weights._fields) :]
    out_ref, sent_ref, *refs = refs
    st = Stash(*[ref.at[0] for ref in refs[:-1]])
    padded = refs[-1]
    rows = x_ref.shape[1]
    main = padded.shape[0] - TILE
    padded[main:, :] = jnp.zeros((TILE, padded.shape[1]), BF16)
    padded[:rows, :] = x_ref[0]
    result = []
    weave((layer_forward(padded[...], 0, w, st, rows, result), 1))
    y = result[0].astype(BF16)
    out_ref[0] = y
    sent_ref[0] = y[main:]


def lower_forward(hidden, weights, full):
    micro, rows, features = hidden.shape
    outs = [jax.ShapeDtypeStruct((micro, full, features), BF16), jax.ShapeDtypeStruct((micro, TILE, features), BF16)]
    shapes = stash_shapes(full, features, weights.w_up.shape[2])
    outs += [jax.ShapeDtypeStruct((micro,) + shape, kind) for shape, kind in shapes]
    out, sent, *stash = pl.pallas_call(
        lower_forward_kernel,
        grid=(micro,),
        in_specs=[by_micro(hidden.shape)] + weight_specs(weights, 0),
        out_specs=[by_micro(o.shape) for o in outs],
        out_shape=outs,
        scratch_shapes=[pltpu.VMEM((full, features), BF16)],
        compiler_params=pltpu.CompilerParams(vmem_limit_bytes=56 * 2**20),
        name="lower_forward",
    )(hidden, *weights)
    return out, sent, Stash(*stash)


def zero_sums(g):
    for ref in g:
        rows, features = ref.shape
        if rows == 1:
            ref[...] = jnp.zeros_like(ref)
        else:

            @pl.loop(0, rows // STRIP)
            def _(i, ref=ref, features=features):
                ref[pl.ds(pl.multiple_of(i * STRIP, STRIP), STRIP), :] = jnp.zeros((STRIP, features), F32)


def upper_forward(rows, lead, arrived, cot_ref, target_ref, slot_ref, count, x_ref, out_ref, grad_out, w, st):
    full, features = x_ref.shape[1:]
    memory = cot_ref.shape[1]
    main = full - TILE
    x = x_ref[0]
    is_read = lax.broadcasted_iota(jnp.int32, (TILE, features), 0) < memory
    moved = jnp.logical_and(is_read, jnp.logical_not(lead))
    x = jnp.concatenate([jnp.where(moved, arrived, x[:TILE]), x[TILE:]], axis=0)
    result = []
    yield from layer_forward(x, 1, w, st, rows, result)
    y = result[0]
    out_ref[0] = y[:rows].astype(BF16)
    slots = slot_ref.shape[2]
    slot_row = lax.broadcasted_iota(jnp.int32, (main, slots), 0) - memory
    slot_at = lax.broadcasted_iota(jnp.int32, (main, slots), 1)
    hit = jnp.logical_and(slot_row == slot_ref[0], slot_at < count)
    hit = jnp.where(hit, 1.0, 0.0).astype(BF16)
    used = dot(hit, jnp.ones((slots, features), BF16))
    wanted = dot(hit, target_ref[0])
    grad_out[:main, :] = (y[:main] * used - wanted) / count.astype(F32)
    grad_out[main : main + memory, :] = cot_ref[0].astype(F32)
    yield 300


def upper_backward(lead, memory, grad_out, grad_ref, back_ref, w, st, *refs, fill):
    result = []
    yield from layer_backward(grad_out[...], 1, w, st, *refs, result, fill)
    grad_in = result[0]
    is_read = lax.broadcasted_iota(jnp.int32, (TILE, grad_in.shape[1]), 0) < memory
    moved = jnp.logical_and(is_read, jnp.logical_not(lead))
    back_ref[0] = grad_in[:TILE].astype(BF16)
    grad_ref[0, :TILE, :] = jnp.where(moved, 0.0, grad_in[:TILE])
    grad_ref[0, TILE:, :] = grad_in[TILE:]


def upper_kernel(rows, micro, bits, count_ref, x_ref, arrived_ref, cot_ref, target_ref, slot_ref, *refs):
    step = pl.program_id(0)
    w, refs = Weights(*refs[: len(Weights._fields)]), refs[len(Weights._fields) :]
    out_ref, grad_ref, back_ref, keep_ref, send_ref = refs[:5]
    refs = refs[5:]
    st, refs = Stash(*refs[: len(Stash._fields)]), refs[len(Stash._fields) :]
    grad_out, *refs = refs
    g, rest, grad_up_ref, grad_s_ref, ordered = take_scratch(refs)
    memory = cot_ref.shape[1]
    lead = lax.axis_index(LINE) == 0

    def turn(slot):
        twice = Stash(*[ref if ref.shape[0] != 2 else ref.at[slot] for ref in st])
        return twice

    def forward(slot):
        now = jnp.minimum(step, micro - 1)
        count, arrived = count_ref[now], arrived_ref[now]
        return upper_forward(
            rows, lead, arrived, cot_ref, target_ref, slot_ref, count, x_ref, out_ref, grad_out, w, turn(slot)
        )

    def backward(slot, fill):
        refs = (g, rest, grad_up_ref, grad_s_ref, step - 1)
        return upper_backward(lead, memory, grad_out, grad_ref, back_ref, w, turn(slot), *refs, fill=fill)

    @pl.when(step == 0)
    def _():
        zero_sums(g)
        grad_out[grad_out.shape[0] - TILE :, :] = jnp.zeros((TILE, grad_out.shape[1]), F32)
        weave((forward(0), FORWARD))

    @pl.when(jnp.logical_and(step > 0, step < micro))
    def _():
        slot = lax.rem(step, 2)
        weave((forward(slot), FORWARD), (backward(1 - slot, True), BACKWARD))

    @pl.when(step == micro)
    def _():
        weave((backward((micro - 1) % 2, False), BACKWARD))
        add_rest(g, rest)
        emit(g, keep_ref, send_ref, ordered, place_of(bits))


def half_packed(features, units):
    return jax.ShapeDtypeStruct((packed_rows(features, units) // 2, features), BF16)


def upper_both(bits, counts, x, arrived, cotangent, targets, slots, weights, rows):
    micro, full, features = x.shape
    units = weights.w_up.shape[2]
    outs = [
        jax.ShapeDtypeStruct((micro, rows, features), BF16),
        jax.ShapeDtypeStruct(x.shape, F32),
        jax.ShapeDtypeStruct((micro, TILE, features), BF16),
        half_packed(features, units),
        half_packed(features, units),
    ]
    ins = (x, arrived, cotangent, targets, slots)
    shapes = stash_shapes(full, features, units)
    once = (shapes.inverse, shapes.normed_attn, shapes.middle, shapes.active, shapes.slope, shapes.normed_ffn)
    stash = [pltpu.VMEM(s if (s, k) in once and (s, k) != shapes.x else (2,) + s, k) for s, k in shapes] + [pltpu.VMEM((full, features), F32)]
    return pl.pallas_call(
        functools.partial(upper_kernel, rows, micro, bits),
        grid=(micro + 1,),
        in_specs=[smem()] + [whole() if a is arrived else ahead(a.shape) for a in ins] + weight_specs(weights),
        out_specs=[ahead(outs[0].shape), behind(outs[1].shape), behind(outs[2].shape)]
        + [fixed(o.shape) for o in outs[3:]],
        out_shape=outs,
        scratch_shapes=stash + scratch(micro, full, features, units),
        compiler_params=pltpu.CompilerParams(vmem_limit_bytes=52 * 2**20),
        name="upper_both",
    )(counts, *ins, *weights)


def lower_backward_kernel(memory, bits, grad_ref, back_ref, *refs):
    step, steps = pl.program_id(0), pl.num_programs(0)
    w, refs = Weights(*refs[: len(Weights._fields)]), refs[len(Weights._fields) :]
    st, refs = Stash(*[ref.at[0] for ref in refs[: len(Stash._fields)]]), refs[len(Stash._fields) :]
    out_ref, keep_ref, send_ref, *refs = refs
    g, rest, grad_up_ref, grad_s_ref, ordered = take_scratch(refs)
    full, features = grad_ref.shape[1:]
    main = full - TILE

    @pl.when(step == 0)
    def _():
        zero_sums(g)

    is_write = lax.broadcasted_iota(jnp.int32, (TILE, features), 0) < memory
    returned = jnp.where(is_write, back_ref[step].astype(F32), 0.0)
    grad_out = jnp.concatenate([grad_ref[0, :main, :], grad_ref[0, main:, :] + returned], axis=0)
    result = []
    weave((layer_backward(grad_out, 0, w, st, g, rest, grad_up_ref, grad_s_ref, step, result), 1))
    out_ref[0] = result[0][: out_ref.shape[1]].astype(BF16)

    @pl.when(step == steps - 1)
    def _():
        add_rest(g, rest)
        emit(g, keep_ref, send_ref, ordered, place_of(bits))


def lower_backward(bits, grad, back, weights, stash, rows, memory):
    micro, full, features = grad.shape
    units = weights.w_up.shape[2]
    outs = [
        jax.ShapeDtypeStruct((micro, rows, features), BF16),
        half_packed(features, units),
        half_packed(features, units),
    ]
    return pl.pallas_call(
        functools.partial(lower_backward_kernel, memory, bits),
        grid=(micro,),
        in_specs=[by_micro(grad.shape), whole()]
        + weight_specs(weights)
        + [by_micro(a.shape) for a in stash],
        out_specs=[by_micro(outs[0].shape)] + [fixed(o.shape) for o in outs[1:]],
        out_shape=outs,
        scratch_shapes=scratch(micro, full, features, units),
        compiler_params=pltpu.CompilerParams(vmem_limit_bytes=52 * 2**20),
        name="lower_backward",
    )(grad, back, *weights, *stash)


def unpack_kernel(bits, *refs):
    sources, refs = refs[:4], refs[4:]
    out, refs = Weights(*refs[: len(Weights._fields)]), refs[len(Weights._fields) :]
    ordered, *staged, in_sems, out_sems, line_sems = refs
    features, units = out.w_up.shape[1:]
    chunks = units // features
    half = sources[0].shape[0]
    rows, piece = 2 * half, 2 * half // PIECES
    arrays = squares(out) + (out.w_up, out.w_down)
    names = lines(out) + (out.b_up,)
    short = staged[len(arrays) :]
    loads = [
        pltpu.make_async_copy(source, ordered.at[i // 2, (i % 2) * half : (i % 2 + 1) * half], in_sems.at[i])
        for i, source in enumerate(sources)
    ]
    for load in loads:
        load.start()
    sizes = [features] * 4 + [units, units]
    sizes.append(rows - sum(sizes))
    me = place_of(bits)

    def store(index, layer):
        return pltpu.make_async_copy(staged[index].at[layer], arrays[index].at[layer], out_sems.at[layer, index])

    @pl.loop(0, 2)
    def _(layer):
        for i in range(2):

            @pl.when(layer == i)
            def _(i=i):
                loads[2 * i].wait()
                loads[2 * i + 1].wait()

        for index, start, which, offset, take in spans(sizes, rows):
            at = pl.multiple_of((which ^ me) * piece, TILE) + offset
            value = ordered[layer, pl.ds(pl.multiple_of(at, TILE), take), :]
            if index == 4:
                staged[index][layer, :, start : start + take] = value.T.astype(F32)
            elif index < 6:
                staged[index][layer, start : start + take, :] = value.astype(F32)
            else:
                value = value.astype(F32)
                for i, ref in enumerate(short[:-1]):
                    ref[pl.ds(layer, 1), :] = value[i : i + 1]
                for c in range(chunks):
                    i = len(short) - 1 + c
                    short[-1][pl.ds(layer, 1), c * features : (c + 1) * features] = value[i : i + 1]
            if index < 6 and start + take == sizes[index]:
                store(index, layer).start()

    line_stores = [pltpu.make_async_copy(near, far, line_sems.at[i]) for i, (near, far) in enumerate(zip(short, names))]
    for copy in line_stores:
        copy.start()
    for layer in range(2):
        for index in range(6):
            store(index, layer).wait()
    for copy in line_stores:
        copy.wait()


def unpack(bits, parts, weights):
    outs = [jax.ShapeDtypeStruct(weight.shape, F32) for weight in weights]
    shapes = Weights(*outs)
    large = squares(shapes) + (shapes.w_up, shapes.w_down)
    short = lines(shapes) + (shapes.b_up,)
    return pl.pallas_call(
        functools.partial(unpack_kernel, bits),
        in_specs=[pl.BlockSpec(memory_space=pl.ANY)] * 4,
        out_specs=[pl.BlockSpec(memory_space=pl.ANY) for _ in outs],
        out_shape=outs,
        scratch_shapes=[pltpu.VMEM((2, 2 * parts[0].shape[0], parts[0].shape[1]), BF16)]
        + [pltpu.VMEM(o.shape, F32) for o in large + short]
        + [pltpu.SemaphoreType.DMA((4,)), pltpu.SemaphoreType.DMA((2, 6)), pltpu.SemaphoreType.DMA((len(short),))],
        compiler_params=pltpu.CompilerParams(vmem_limit_bytes=20 * 2**20),
        name="unpack",
    )(*parts)


def from_behind(value, axis, steps):
    count = lax.axis_size(axis)
    initial, last = (max(0, -steps), min(count, count - steps))
    return lax.ppermute(value, axis, [(source, source + steps) for source in range(initial, last)])


def swap(value, bit):
    axis, step = bit
    return lax.ppermute(value, axis, [(i, i ^ step) for i in range(lax.axis_size(axis))])


def plus(a, b):
    return (a.astype(F32) + b.astype(F32)).astype(BF16)


def place_of(bits):
    me = jnp.int32(0)
    for axis, step in bits:
        me = me * 2 + lax.rem(lax.div(lax.axis_index(axis), step), 2)
    return me


def sum_rest(value, bits):
    axis, step = bits[0]
    me = (lax.axis_index(axis) // step) % 4

    def across(part, k):
        return lax.ppermute(part, axis, [(i, i ^ (k * step)) for i in range(lax.axis_size(axis))])

    rows = value.shape[0] // 4
    quarter = [lax.dynamic_slice_in_dim(value, (me ^ k) * rows, rows) for k in range(4)]
    got = [across(quarter[k], k) for k in (1, 2, 3)]
    kept = quarter[0].astype(F32)
    for part in got:
        kept = kept + part.astype(F32)
    kept = kept.astype(BF16)
    for bit in bits[2:]:
        kept = plus(kept, swap(kept, bit))
    a, b, c, d = [kept] + [across(kept, k) for k in (1, 2, 3)]
    odd, high = me % 2 == 1, me >= 2
    first, second = jnp.where(odd, b, a), jnp.where(odd, a, b)
    third, fourth = jnp.where(odd, d, c), jnp.where(odd, c, d)
    lower, upper = jnp.concatenate([first, second], axis=0), jnp.concatenate([third, fourth], axis=0)
    return jnp.where(high, jnp.concatenate([upper, lower], axis=0), jnp.concatenate([lower, upper], axis=0))


def sum_all(halves, core, along, across, rest_bits, others):
    def to(part, j):
        swaps = [(axis, step) for (axis, step), used in ((across, j % 2), (along, j // 2)) if used]
        sizes = [lax.axis_size(axis) for axis in (LINE, PAIR)]
        line = sum(step for axis, step in swaps if axis == LINE)
        pair = sum(step for axis, step in swaps if axis == PAIR)
        perm = [(i * sizes[1] + k, (i ^ line) * sizes[1] + (k ^ pair)) for i in range(sizes[0]) for k in range(sizes[1])]
        return lax.ppermute(part, (LINE, PAIR), perm)

    chains = [plus(keep, swap(send, core)) for keep, send in halves]
    rows = chains[0].shape[0] // 4
    for i, kept in enumerate(chains):
        got = [to(kept[j * rows : (j + 1) * rows], j) for j in (3, 1, 2)]
        chains[i] = sum([part.astype(F32) for part in got], kept[:rows].astype(F32)).astype(BF16)
    chains = [sum_rest(kept, rest_bits) for kept in chains]
    others, chains[0] = lax.optimization_barrier((others, chains[0]))
    chains = [jnp.concatenate([kept] + [to(kept, j) for j in (1, 2, 3)], axis=0) for kept in chains]
    others = [with_layout_constraint(jnp.transpose(v, (1, 0, 2)), Layout((0, 1, 2))) for v in others]
    others, chains[0] = lax.optimization_barrier((others, chains[0]))
    return [part for kept in chains for part in (kept, swap(kept, core))], others


def local(hidden, write_cotangent, targets, positions, counts, *weights):
    weights = Weights(*weights)
    micro, _, _, rows, features = hidden.shape
    memory = write_cotangent.shape[3]
    full = -(-rows // TILE) * TILE
    bits = [(axis, 1 << i) for axis in (LINE, PAIR) for i in range(lax.axis_size(axis).bit_length() - 1)]
    core, along, across = (LINE, 1), (LINE, 2), (PAIR, 1)
    piece_bits = (core, along, across)
    rest_bits = [bit for bit in bits if bit not in piece_bits]

    hidden_rows = hidden.reshape(micro, rows, features)
    lower_out, sent, stash = lower_forward(hidden_rows, weights, full)
    arrived = from_behind(sent, LINE, 1)
    out, grad, back, *upper = upper_both(
        piece_bits,
        counts.reshape(micro),
        lower_out,
        arrived,
        write_cotangent.reshape(micro, memory, features),
        targets.reshape(micro, targets.shape[3], features),
        positions.reshape(micro, 1, positions.shape[3]),
        weights,
        rows,
    )
    returned = from_behind(back, LINE, -1)
    grad_in, *lower = lower_backward(piece_bits, grad, returned, weights, stash, rows, memory)
    parts, (out, grad_in) = sum_all((lower, upper), core, along, across, rest_bits, (out, grad_in))
    grads = unpack(piece_bits, parts, weights)
    out, grad_in = (jnp.transpose(v, (1, 0, 2)).reshape(hidden.shape) for v in (out, grad_in))
    return (out, grad_in) + tuple(grads)


def solution(mesh):
    split = P(None, PAIR, LINE, None, None)
    placed = (split, split, split, P(None, PAIR, LINE, None), P(None, PAIR, LINE))
    count = len(Weights._fields)
    return jax.shard_map(
        local,
        mesh=mesh,
        in_specs=placed + (P(),) * count,
        out_specs=(split, split) + (P(),) * count,
        check_vma=False,
    )
```
